32 devices in a mesh: grp: 2 (over y), gx: 4 (over x, core), gy: 4 (over z).
Axes of the slice: x: 2, y: 2, z: 4, core: 2. Of those that a mesh axis runs over, the one named last changes fastest.
Arguments:
- load_current: bfloat16 [16, 256, 512], P(None, ('grp', 'gx'), 'gy'), parts along dimension 1, may hold values from 0.29 to 9, as said below
- row_conductance: float32 [256, 512], P(('grp', 'gx'), 'gy'), parts along dimension 0, may hold values from 0.5 to 8
- col_conductance: float32 [256, 512], P(('grp', 'gx'), 'gy'), parts along dimension 0, may hold values from 0.5 to 8
- via_conductance: float32 [256, 512], P(('grp', 'gx'), 'gy'), parts along dimension 0, may hold values from 1 to 10
- pad_mask: int32 [256, 512], P(('grp', 'gx'), 'gy'), parts along dimension 0, may hold values 0 or 1
- via_mask: int32 [256, 512], P(('grp', 'gx'), 'gy'), parts along dimension 0, may hold values 0 or 1
- row_residual: float32 [256, 512], P(('grp', 'gx'), 'gy'), parts along dimension 0, may hold values from -6 to 6
- col_residual: float32 [256, 512], P(('grp', 'gx'), 'gy'), parts along dimension 0, may hold values from -6 to 6
Outputs:
- upper_drop: float32 [16, 256, 512], P(None, ('grp', 'gx'), 'gy'), parts along dimension 1
- row_stress: float32 [16, 256, 512], P(None, ('grp', 'gx'), 'gy'), parts along dimension 1
- col_stress: float32 [16, 256, 512], P(None, ('grp', 'gx'), 'gy'), parts along dimension 1
The draws below stay inside these ranges and needn't reach their ends.
There are 2 independent parts, one for each index of `grp`. The reference program is written for one: setup_inputs(seed, part) draws one part's arguments, and reference() takes and returns one part's arrays. A program takes and returns all parts, laid end to end along the dimension named above; each array names one. Nothing has to cross between parts.
Inputs may be any that keep to these rules, and one draw needn't show every extreme that they name: `load_current`: positive load currents of 16 scenarios.
All inputs are finite; a program needn't handle non-finite values. No bound on the sum of `pad_mask` or of `via_mask` on one device may be relied on, other than what follows from the above.
Results may differ from the reference program's by a relative error of at most 0.0003.
Values sent between devices are 32-bit elements; how exact they have to be, the bound alone decides.
No kernel may reach another device: no remote copies, remote signals or barrier semaphores. Data moves between devices by JAX's collectives and lax.ppermute only.
A program may use at most 64 MiB of HBM per device.

```python
import math
import jax
import jax.numpy as jnp
from jax import lax

K = 16
ITERS = 2
STEPS = 8
NX = 128
NY = 512


def draw_load_current(key, part):
    key = jax.random.fold_in(key, 7)
    first_key = jax.random.fold_in(key, 0)
    rise = 1.0 + 2.0 * jnp.arange(NX, dtype=jnp.float32)[None, :, None] / max(NX - 1, 1)
    base = jnp.exp(jax.random.uniform(first_key, (K, NX, NY), jnp.float32, math.log(0.3), math.log(3.0)))
    return (base * rise).astype(jnp.bfloat16)


def plant(array, rng, least, largest):
    index_at = [jax.random.randint(jax.random.fold_in(rng, axis), (), 0, length) for axis, length in enumerate(array.shape)]
    widest = array.shape.index(max(array.shape))
    neighbour = index_at[:widest] + [(index_at[widest] + 1) % array.shape[widest]] + index_at[widest + 1:]
    return array.at[tuple(index_at)].set(least).at[tuple(neighbour)].set(largest)


def level_of(stream_key, dims, pieces, least, high):
    gain, own = 1.0, jax.random.fold_in(stream_key, 6)
    for position, parts in pieces:
        heights = jnp.exp(jax.random.uniform(jax.random.fold_in(own, position), (parts,), jnp.float32, least / len(pieces), high / len(pieces)))
        gain = gain * jnp.repeat(heights, dims[position] // parts).reshape([-1 if axis == position else 1 for axis in range(len(dims))])
    return gain


def normal_values(stream_key, dims, deviation, limit, pieces=(), held_as=jnp.bfloat16):
    level = level_of(stream_key, dims, pieces, -0.22, 0.18) if pieces else 1.0
    entries = jax.random.normal(stream_key, dims, jnp.float32) * deviation * level
    return jnp.minimum(jnp.maximum(entries, -limit), limit).astype(held_as)


def setup_inputs(seed: int = 0, part: int = 0) -> dict:
    keys = jax.random.split(jax.random.key(seed), 9)
    part_splits = jax.random.split(jax.random.fold_in(keys[8], part), 9)
    return {
        "load_current": draw_load_current(jax.random.fold_in(jax.random.fold_in(keys[8], part), 71), part),
        "row_conductance": jnp.clip(jnp.exp(math.log(8.0) - 2.7725887 * jax.random.uniform(part_splits[1], (NX, NY), jnp.float32) ** level_of(part_splits[1], (NX, NY), ((0, 4), (1, 4)), -0.2, 0.2)), 0.5, 8.0),
        "col_conductance": jnp.clip(jnp.exp(math.log(8.0) - 2.7725887 * jax.random.uniform(part_splits[2], (NX, NY), jnp.float32) ** level_of(part_splits[2], (NX, NY), ((0, 4), (1, 4)), -0.2, 0.2)), 0.5, 8.0),
        "via_conductance": jnp.clip(jnp.exp(math.log(10.0) - 2.3025851 * jax.random.uniform(part_splits[3], (NX, NY), jnp.float32) ** level_of(part_splits[3], (NX, NY), ((0, 4), (1, 4)), -0.2, 0.2)), 1.0, 10.0),
        "pad_mask": plant((jax.random.randint(part_splits[4], (NX, NY), 0, 16) < 1).astype(jnp.int32), jax.random.fold_in(part_splits[4], 1), 0, 1),
        "via_mask": plant((jax.random.randint(part_splits[5], (NX, NY), 0, 2) < 1).astype(jnp.int32), jax.random.fold_in(part_splits[5], 1), 0, 1),
        "row_residual": normal_values(part_splits[6], (NX, NY), 1.0, 6.0, ((0, 4), (1, 4)), jnp.float32),
        "col_residual": normal_values(part_splits[7], (NX, NY), 1.0, 6.0, ((0, 4), (1, 4)), jnp.float32),
    }


relax_rate = 0.45
drive_gain = 4.0
pad_conductance = 20.0
leak_conductance = 0.05


def relax_step(stress_prev, stress_mid, stress_next, current_mid, current_next, open_mid, open_next):
    inflow = relax_rate * open_mid * ((stress_prev - stress_mid) + drive_gain * current_mid)
    outflow = relax_rate * open_next * ((stress_mid - stress_next) + drive_gain * current_next)
    return (stress_mid + inflow) - outflow


def reference(load_current, row_conductance, col_conductance, via_conductance, pad_mask, via_mask, row_residual, col_residual):
    row_index = jnp.arange(NX)[:, None]
    col_index = jnp.arange(NY)[None, :]
    row_seg = jnp.where(row_index >= 1, row_conductance, 0.0)
    row_seg_next = jnp.pad(row_seg[1:], ((0, 1), (0, 0)))
    col_seg = jnp.where(col_index >= 1, col_conductance, 0.0)
    col_seg_next = jnp.pad(col_seg[:, 1:], ((0, 0), (0, 1)))
    via_term = via_mask.astype(jnp.float32) * via_conductance
    tie_top = via_term + leak_conductance
    tie_low = via_term + pad_mask.astype(jnp.float32) * pad_conductance + leak_conductance
    diag_top = row_seg + row_seg_next + tie_top
    diag_low = col_seg + col_seg_next + tie_low
    open_rows = ((row_index >= 1) & (row_index <= NX - 1)).astype(jnp.float32)
    open_rows_next = ((row_index >= 0) & (row_index <= NX - 2)).astype(jnp.float32)
    open_cols = ((col_index >= 1) & (col_index <= NY - 1)).astype(jnp.float32)
    open_cols_next = ((col_index >= 0) & (col_index <= NY - 2)).astype(jnp.float32)

    def operate(field_top, field_low):
        wide_top = jnp.pad(field_top, ((1, 1), (0, 0)))
        wide_low = jnp.pad(field_low, ((0, 0), (1, 1)))
        img_top = row_seg * (field_top - wide_top[:-2]) - row_seg_next * (wide_top[2:] - field_top) + tie_top * field_top - via_term * field_low
        img_low = col_seg * (field_low - wide_low[:, :-2]) - col_seg_next * (wide_low[:, 2:] - field_low) + tie_low * field_low - via_term * field_top
        return img_top, img_low

    def inner_sum(first_top, first_low, second_top, second_low):
        return jnp.sum(first_top * second_top) + jnp.sum(first_low * second_low)

    def scenario(currents):
        res_top = currents.astype(jnp.float32)
        res_low = jnp.zeros_like(res_top)
        pre_top = res_top / diag_top
        pre_low = res_low / diag_low
        dir_top, dir_low = pre_top, pre_low
        norm_now = inner_sum(res_top, res_low, pre_top, pre_low)
        sol_top = jnp.zeros_like(res_top)
        sol_low = jnp.zeros_like(res_top)
        for repeat in range(ITERS):
            img_top, img_low = operate(dir_top, dir_low)
            step_size = norm_now / inner_sum(dir_top, dir_low, img_top, img_low)
            sol_top = sol_top + step_size * dir_top
            sol_low = sol_low + step_size * dir_low
            res_top = res_top - step_size * img_top
            res_low = res_low - step_size * img_low
            pre_top = res_top / diag_top
            pre_low = res_low / diag_low
            norm_next = inner_sum(res_top, res_low, pre_top, pre_low)
            momentum = norm_next / norm_now
            dir_top = pre_top + momentum * dir_top
            dir_low = pre_low + momentum * dir_low
            norm_now = norm_next
        wide_top = jnp.pad(sol_top, ((1, 1), (0, 0)))
        wide_low = jnp.pad(sol_low, ((0, 0), (1, 1)))
        current_row = row_seg * (wide_top[:-2] - sol_top)
        current_row_next = row_seg_next * (sol_top - wide_top[2:])
        current_col = col_seg * (wide_low[:, :-2] - sol_low)
        current_col_next = col_seg_next * (sol_low - wide_low[:, 2:])
        stress_row = row_residual
        stress_col = col_residual
        for repeat in range(STEPS):
            padded_row = jnp.pad(stress_row, ((1, 1), (0, 0)))
            stress_row = relax_step(padded_row[:-2], stress_row, padded_row[2:], current_row, current_row_next, open_rows, open_rows_next)
            padded_col = jnp.pad(stress_col, ((0, 0), (1, 1)))
            stress_col = relax_step(padded_col[:, :-2], stress_col, padded_col[:, 2:], current_col, current_col_next, open_cols, open_cols_next)
        return sol_top, stress_row, stress_col

    upper_drop, row_stress, col_stress = lax.map(scenario, load_current)
    return (upper_drop, row_stress, col_stress)
```

```python
import functools

import jax
import jax.numpy as jnp
import numpy as np
from jax import lax
from jax.experimental import pallas as pl
from jax.experimental.pallas import tpu as pltpu
from jax.sharding import PartitionSpec as P

STEPS = 8
RELAX = 0.45
DRIVE = 4.0
PAD = 20.0
LEAK = 0.05

F32 = jnp.float32
HALO = STEPS + 1
SLOT = 16
BLOCK = 24

FIRST_LANES = [0, 12, 11, 1, 2, 3, 4, 5, 6]
LAST_LANES = [-1, 13, 14, 9, 15, -2, 8, -7, -6, -5, -4, -3]
LAST_AT = 12


def dot_nt(a, b):
    return lax.dot_general(
        a, b, (((1,), (1,)), ((), ())), precision=lax.Precision.HIGHEST, preferred_element_type=F32
    )


def dot_nn(a, b):
    return lax.dot_general(
        a, b, (((1,), (0,)), ((), ())), precision=lax.Precision.HIGHEST, preferred_element_type=F32
    )


def dot_tn(a, b):
    return lax.dot_general(
        a, b, (((0,), (0,)), ((), ())), precision=lax.Precision.HIGHEST, preferred_element_type=F32
    )


def picker(cols):
    e = np.zeros((BLOCK + 16 + 8, cols), np.float32)
    for i, lane in enumerate(FIRST_LANES):
        e[i, lane % cols] = 1
    for i, lane in enumerate(LAST_LANES):
        e[LAST_AT + i, lane % cols] = 1
    for i in range(8):
        e[BLOCK + i, i] = 1
        e[BLOCK + 8 + i, cols - 8 + i] = 1
    e[BLOCK + 16 :] = 1
    return e


def spread(cols):
    size = cols + 16
    sources, starts = [], []
    for first, last in ((0, 0), (1, 0), (0, 1), (1, 1)):
        rate = np.full(size + 1, RELAX)
        rate[0] = rate[size] = 0
        if first:
            rate[8] = 0
        if last:
            rate[8 + cols] = 0
        step = np.eye(size)
        for i in range(size):
            step[i, i] -= rate[i] + rate[i + 1]
            if i:
                step[i, i - 1] += rate[i]
            if i + 1 < size:
                step[i, i + 1] += rate[i + 1]
        power, total = np.eye(size), np.zeros((size, size))
        for _ in range(STEPS):
            total += power
            power = step @ power
        source = (RELAX * DRIVE * total)[8 : 8 + cols].T
        start = power[8 : 8 + cols].T
        extra = np.zeros((24, cols))
        extra[0:7] = source[1:8]
        extra[8:15] = source[8 + cols : 15 + cols]
        extra[16] = source[8]
        extra[17] = source[8 + cols - 2]
        extra[18] = source[8 + cols - 1]
        sources.append(np.concatenate([source[8 : 8 + cols], extra]))
        starts.append(np.concatenate([start[8 : 8 + cols], start[:8], start[8 + cols :]]))
    return np.stack(sources).astype(np.float32), np.stack(starts).astype(np.float32)


def place(axis):
    at, count = lax.axis_index(axis), lax.axis_size(axis)
    return at, at == 0, at == count - 1


def pack_kernel(load_ref, rc_ref, vc_ref, vm_ref, rr_ref, lf_ref, a_ref, b_ref):
    scen, rows, cols = load_ref.shape
    at, first, _ = place("gx")
    even = lax.rem(at, 2) == 0
    for s in range(scen):
        lf_ref[pl.ds(s, rows, stride=scen), :] = load_ref[s].astype(F32)
    row = lax.broadcasted_iota(jnp.int32, (rows, cols), 0)
    h = jnp.where(jnp.logical_and(first, row == 0), 0.0, rc_ref[...])
    via = vm_ref[...].astype(F32) * vc_ref[...]
    n = HALO * scen

    def put(where, top, bottom):
        a_ref[where, :] = jnp.where(even, bottom, top)
        b_ref[where, :] = jnp.where(even, top, bottom)

    put(pl.ds(0, n), lf_ref[0:n, :], lf_ref[rows * scen - n :, :])
    put(pl.ds(n, SLOT), h[:SLOT], h[rows - SLOT :])
    put(pl.ds(n + SLOT, SLOT), via[:SLOT], via[rows - SLOT :])
    put(pl.ds(n + 2 * SLOT, 8), rr_ref[:8, :], rr_ref[rows - 8 :, :])


def fields_kernel(
    scen, lf_ref, rc_ref, cc_ref, vc_ref, pm_ref, vm_ref, cr_ref, a_ref, b_ref, pick_ref,
    v_ref, t_ref, fv_ref, ft_ref, fl_ref, msg_ref,
    inv_s, h_s, tie_s, low_s, w_s,
):
    rows, cols = rc_ref.shape
    at_x, first_x, _ = place("gx")
    odd = lax.rem(at_x, 2) == 1
    _, first_y, last_y = place("gy")
    n = HALO * scen

    def before(where):
        return jnp.where(odd, a_ref[where, :], b_ref[where, :])

    def after(where):
        return jnp.where(odd, b_ref[where, :], a_ref[where, :])

    row = lax.broadcasted_iota(jnp.int32, (rows, cols), 0)
    lane = lax.broadcasted_iota(jnp.int32, (rows, cols), 1)
    h = jnp.where(jnp.logical_and(first_x, row == 0), 0.0, rc_ref[...])
    via = vm_ref[...].astype(F32) * vc_ref[...]
    at = pl.ds(n, SLOT)
    h_ext = jnp.concatenate([before(at), h, after(at)], 0)
    at = pl.ds(n + SLOT, SLOT)
    tie_ext = jnp.concatenate([before(at), via, after(at)], 0) + LEAK
    h_s[...] = h_ext
    tie_s[...] = tie_ext
    h_next = pltpu.roll(h_ext, h_ext.shape[0] - 1, 0)
    inv_s[...] = 1.0 / (h_ext + h_next + tie_ext)

    tie_low = via + pm_ref[...].astype(F32) * PAD + LEAK
    vs = jnp.where(jnp.logical_and(first_y, lane == 0), 0.0, cc_ref[...])
    open_end = jnp.logical_and(jnp.logical_not(last_y), lane == cols - 1)
    vs_next = jnp.where(lane == cols - 1, 0.0, pltpu.roll(vs, cols - 1, 1))
    diag_low = vs + vs_next + tie_low
    low_s[0] = via
    low_s[1] = jnp.where(open_end, 0.0, -1.0 / diag_low)
    low_s[2] = tie_low
    low_s[3] = jnp.where(jnp.logical_or(open_end, lane == 0), 0.0, vs)
    low_s[4] = jnp.where(
        lane == 12,
        pltpu.roll(vs, 12, 1),
        jnp.where(
            lane == 13,
            pltpu.roll(diag_low, 14, 1),
            jnp.where(lane == 14, pltpu.roll(tie_low, 15, 1), pltpu.roll(vs, 16, 1)),
        ),
    )
    wide = lax.broadcasted_iota(jnp.int32, (scen, cols), 1)
    is_flux = jnp.logical_or(
        jnp.logical_and(wide >= 1, wide <= 6), jnp.logical_and(wide >= cols - 7, wide <= cols - 3)
    )
    is_t = jnp.logical_or(wide == 0, wide == cols - 2)
    is_end = wide == cols - 1
    is_rolled = jnp.logical_and(wide >= 8, wide <= 11)

    def load(r):
        if r < 0:
            return before(pl.ds((r + HALO) * scen, scen))
        if r >= rows:
            return after(pl.ds((r - rows) * scen, scen))
        return lf_ref[pl.ds(r * scen, scen), :]

    def bc(ref, r):
        return jnp.broadcast_to(ref[pl.ds(r, 1), :], (scen, cols))

    def low(k, r):
        return jnp.broadcast_to(low_s[k, pl.ds(r, 1), :], (scen, cols))

    g0 = g1 = g2 = g3 = jnp.zeros((scen, cols), F32)
    v0 = dv0 = hv0 = t0 = ht0 = l0 = None
    for r in range(-HALO, rows + HALO):
        l1 = load(r)
        v1 = l1 * bc(inv_s, r + SLOT)
        dv1 = hv1 = None
        if r > -HALO:
            dv1 = v0 - v1
            hv1 = bc(h_s, r + SLOT) * dv1
        if r > 1 - HALO:
            m = r - 1
            own = 0 <= m < rows
            fv = hv0 - hv1
            tie = bc(tie_s, m + SLOT)
            q_up = tie * v0 - fv
            t1 = q_up * bc(inv_s, m + SLOT)
            ht1 = None
            if m > 1 - HALO:
                dt = t0 - t1
                ht1 = bc(h_s, m + SLOT) * dt
                if m > 2 - HALO:
                    ft_ref[pl.ds((m - 1 + STEPS - 1) * scen, scen), :] = ht0 - ht1
                if m < rows + STEPS - 1:
                    fv_ref[pl.ds((m + STEPS - 1) * scen, scen), :] = fv
            if own:
                v_ref[pl.ds(m, scen, stride=rows), :] = v0
                t_ref[pl.ds(m, scen, stride=rows), :] = t1
                via_m = low(0, m)
                q = via_m * v0
                tl = q * low(1, m)
                dl = pltpu.roll(tl, 1, 1) - tl
                jl = low(3, m) * dl
                fl = jl - pltpu.roll(jl, cols - 1, 1)
                fl_ref[pl.ds(m * scen, scen), :] = fl
                p = via_m * t1
                g0 += l0 * v0
                g1 += hv0 * dv0 + tie * v0 * v0
                g2 += q_up * t1 - q * tl
                g3 += ht1 * dt + tie * t1 * t1 + tl * (low(2, m) * tl - 2.0 * p) + jl * dl
                rolled = pltpu.roll(jnp.where(is_end, p, jl), 10, 1)
                w_s[pl.ds(m * scen, scen), :] = jnp.where(
                    is_flux,
                    fl,
                    jnp.where(is_t, tl, jnp.where(is_end, q, jnp.where(is_rolled, rolled, low(4, m)))),
                )
            t0, ht0 = t1, ht1
        l0, v0, dv0, hv0 = l1, v1, dv1, hv1

    size = rows * scen
    for k, g in enumerate((g0, g1, g2, g3)):
        w_s[pl.ds(size + k * scen, scen), :] = g
    w_s[pl.ds(size + 4 * scen, rows), :] = cr_ref[...]
    w_s[size + 4 * scen + rows :, :] = jnp.zeros((w_s.shape[0] - size - 4 * scen - rows, cols), F32)
    picked = dot_nt(pick_ref[...], w_s[...])
    for k in range(size // cols):
        msg_ref[pl.ds(k * BLOCK, BLOCK), :] = picked[:BLOCK, k * cols : (k + 1) * cols]
    msg_ref[size // cols * BLOCK :, :] = picked[BLOCK:, size : size + cols]


def strips(ref, parts, cols):
    return jnp.concatenate([ref[pl.ds(k * BLOCK, BLOCK), :] for k in range(parts)], 1)


def meet(last, first):
    q, d, tie, p, vs, t_in = (last[LAST_AT + i : LAST_AT + i + 1] for i in range(6))
    t_next, vs_next = first[0:1], first[1:2]
    diag = d + vs_next
    t = -q / jnp.where(diag > 0, diag, 1.0)
    j_in = vs * (t_in - t)
    j_out = vs_next * (t - t_next)
    return q, tie, p, t, t_in, t_next, j_in, j_out


def merge_kernel(scen, axis, step, mine_ref, got_ref, *out_refs):
    cols = mine_ref.shape[1]
    parts = (mine_ref.shape[0] - 24) // BLOCK
    on_left = lax.rem(lax.div(lax.axis_index(axis), step), 2) == 0
    mine, got = strips(mine_ref, parts, cols), strips(got_ref, parts, cols)
    left, right = jnp.where(on_left, mine, got), jnp.where(on_left, got, mine)
    q, tie, p, t, t_in, t_next, j_in, j_out = meet(left, right)
    i2 = -q * t
    i3 = t * (tie * t - 2.0 * p) + j_in * (t_in - t) + j_out * (t - t_next)
    both = jnp.concatenate([i2, i3], 0)
    both = sum(both[:, k * cols : (k + 1) * cols] for k in range(parts))
    shift = scen
    while shift < cols:
        both = both + pltpu.roll(both, shift, 1)
        shift *= 2
    lane = lax.broadcasted_iota(jnp.int32, (8, cols), 1)
    group = lax.div(lane, scen)
    add = jnp.where(group == 2, both[0:1], jnp.where(group == 3, both[1:2], 0.0))
    base = parts * BLOCK
    sums = mine_ref[base + 16 :, :] + got_ref[base + 16 :, :] + add
    if len(out_refs) == 2:
        msg_ref, sums_ref = out_refs
        row = lax.broadcasted_iota(jnp.int32, (BLOCK, cols), 0)
        for k in range(parts):
            at = slice(k * cols, (k + 1) * cols)
            msg_ref[pl.ds(k * BLOCK, BLOCK), :] = jnp.where(row < LAST_AT, left[:, at], right[:, at])
        a, b = mine_ref[pl.ds(base, 16), :], got_ref[pl.ds(base, 16), :]
        msg_ref[pl.ds(base, 8), :] = jnp.where(on_left, a[:8], b[:8])
        msg_ref[pl.ds(base + 8, 8), :] = jnp.where(on_left, b[8:], a[8:])
        msg_ref[base + 16 :, :] = sums
    else:
        (sums_ref,) = out_refs
    sums_ref[...] = sums


def row_stress_kernel(scen, rows, fv_ref, ft_ref, rr_ref, a_ref, b_ref, gv_ref, gt_ref, br_ref, sv_s, st_s, s0_s):
    cols = fv_ref.shape[1]
    at_x, first, last = place("gx")
    odd = lax.rem(at_x, 2) == 1
    n = HALO * scen + 2 * SLOT
    count = rows + 2 * (STEPS - 1)
    rate_first = jnp.where(first, 0.0, RELAX)
    rate_last = jnp.where(last, 0.0, RELAX)

    def rate(r):
        return rate_first if r == 0 else rate_last if r == rows else RELAX

    s0 = jnp.concatenate(
        [
            jnp.where(odd, a_ref[n : n + 8, :], b_ref[n : n + 8, :]),
            rr_ref[...],
            jnp.where(odd, b_ref[n : n + 8, :], a_ref[n : n + 8, :]),
        ],
        0,
    )
    size = rows + 16
    row = lax.broadcasted_iota(jnp.int32, (size, cols), 0)
    rates = jnp.where(row == 8, rate_first, jnp.where(row == 8 + rows, rate_last, RELAX))

    sv_s[...] = fv_ref[...]
    st_s[...] = ft_ref[...]
    s0_s[...] = s0

    def one(_, carry):
        now = s0_s[...]
        flux = rates * (pltpu.roll(now, 1, 0) - now)
        s0_s[...] = now + flux - pltpu.roll(flux, size - 1, 0)
        for f_ref, s_ref in ((fv_ref, sv_s), (ft_ref, st_s)):
            here = s_ref[pl.ds(0, scen), :]
            flux = jnp.zeros_like(here)
            for i in range(count):
                r = i - (STEPS - 1)
                at = pl.ds(i * scen, scen)
                if i + 1 < count:
                    after = s_ref[pl.ds((i + 1) * scen, scen), :]
                    flux_next = rate(r + 1) * (here - after)
                else:
                    after, flux_next = here, jnp.zeros_like(here)
                s_ref[at, :] = here + (flux - flux_next) + f_ref[at, :]
                here, flux = after, flux_next
        return carry

    lax.fori_loop(0, STEPS - 1, one, 0)
    now = s0_s[...]
    flux = rates * (pltpu.roll(now, 1, 0) - now)
    now = now + flux - pltpu.roll(flux, size - 1, 0)
    br_ref[...] = now[8 : 8 + rows]
    gain = RELAX * DRIVE
    for m in range(rows):
        at = pl.ds((m + STEPS - 1) * scen, scen)
        gv_ref[pl.ds(m, scen, stride=rows), :] = gain * sv_s[at, :]
        gt_ref[pl.ds(m, scen, stride=rows), :] = gain * st_s[at, :]


def col_stress_kernel(scen, rows, fl_ref, cr_ref, mine_ref, *rest):
    *got_refs, source_ref, start_ref, gl_ref, bc_ref, out_s = rest
    cols = fl_ref.shape[1]
    parts = rows * scen // cols
    base = parts * BLOCK
    at, first, last = place("gy")
    kind = first.astype(jnp.int32) + 2 * last.astype(jnp.int32)
    own = strips(mine_ref, parts, cols)
    before, after = jnp.zeros_like(own), jnp.zeros_like(own)
    res_before = jnp.zeros((8, cols), F32)
    res_after = jnp.zeros((8, cols), F32)
    for k, ref in enumerate(got_refs):
        step = 1 << k
        rest_of = lax.rem(at, step)
        bit = lax.rem(lax.div(at, step), 2)
        block = strips(ref, parts, cols)
        from_right = jnp.logical_and(bit == 0, rest_of == step - 1)
        from_left = jnp.logical_and(bit == 1, rest_of == 0)
        after = jnp.where(from_right, block, after)
        before = jnp.where(from_left, block, before)
        res_after = jnp.where(from_right, ref[pl.ds(base, 8), :], res_after)
        res_before = jnp.where(from_left, ref[pl.ds(base + 8, 8), :], res_before)
    _, _, _, _, _, _, jl_last, jl_0 = meet(before, own)
    _, _, _, _, _, _, jr_last, jr_0 = meet(own, after)
    jr_last = jnp.where(last, 0.0, jr_last)
    jr_0 = jnp.where(last, 0.0, jr_0)
    lo = LAST_AT + 6
    zero = jnp.zeros_like(jl_0)
    strip = jnp.concatenate(
        [
            before[lo + 1 : lo + 6],
            before[lo : lo + 1] - jl_last,
            jl_last - jl_0,
            zero,
            jr_0 - after[2:3],
            after[3:9],
            zero,
            jl_0,
            -jr_last,
            jr_last - jr_0,
            zero,
            zero,
            zero,
            zero,
            zero,
        ],
        0,
    )
    source = source_ref[kind]
    out_s[...] = dot_nn(fl_ref[...], source[:cols]) + dot_tn(strip, source[cols:])
    for m in range(rows):
        gl_ref[pl.ds(m, scen, stride=rows), :] = out_s[pl.ds(m * scen, scen), :]
    start = start_ref[kind]
    edge = dot_tn(jnp.concatenate([res_before, res_after], 0), start[cols:])
    skip = 4 * scen
    bc_ref[...] = dot_nn(cr_ref[...], start[:cols]) + edge[skip : skip + rows]


def final_kernel(
    scen, rows, a_ref, b_ref, v_ref, t_ref, gv_ref, gt_ref, gl_ref, br_ref, bc_ref, up_ref, row_ref, col_ref
):
    cols = v_ref.shape[1]
    sums = a_ref[...] + b_ref[...]
    g0, g1, g2, g3 = (sums if k == 0 else pltpu.roll(sums, cols - k * scen, 1) for k in range(4))
    alpha = g0 / g1
    rz = alpha * alpha * g2 - g0
    grow = alpha * g2 / g1
    beta_alpha = rz / (alpha * alpha * (g3 - g2 * g2 / g1))
    c0 = alpha + beta_alpha * grow
    c1 = -alpha * beta_alpha
    lane = lax.broadcasted_iota(jnp.int32, (scen, cols), 1)
    sub = lax.broadcasted_iota(jnp.int32, (scen, cols), 0)

    def column(c):
        tall = jnp.concatenate([c] * (scen // 8), 0)
        return jnp.sum(jnp.where(lane == sub, tall, 0.0), 1, keepdims=True)

    c0, c1 = column(c0), column(c1)
    br, bc = br_ref[...], bc_ref[...]
    for s in range(scen):
        at = pl.ds(s * rows, rows)
        a = jnp.broadcast_to(c0[s : s + 1], (rows, cols))
        b = jnp.broadcast_to(c1[s : s + 1], (rows, cols))
        up_ref[s] = a * v_ref[at, :] + b * t_ref[at, :]
        row_ref[s] = br + a * gv_ref[at, :] + b * gt_ref[at, :]
        col_ref[s] = bc + b * gl_ref[at, :]


def swap(block, axis, step):
    count = lax.axis_size(axis)
    return lax.ppermute(block, axis, [(i, i ^ step) for i in range(count)])


def exchange(even_side, odd_side, axis):
    count = lax.axis_size(axis)

    def pairs(start):
        return [(i + a, i + 1 - a) for i in range(start, count - 1, 2) for a in (0, 1)]

    return lax.ppermute(even_side, axis, pairs(0)), lax.ppermute(odd_side, axis, pairs(1))


def call(kernel, out, scratch, cost, *args):
    return pl.pallas_call(
        kernel,
        out_shape=out,
        in_specs=[pl.BlockSpec(memory_space=pltpu.VMEM)] * len(args),
        out_specs=jax.tree.map(lambda _: pl.BlockSpec(memory_space=pltpu.VMEM), out),
        scratch_shapes=scratch,
        compiler_params=pltpu.CompilerParams(vmem_limit_bytes=24 * 2**20),
        cost_estimate=pl.CostEstimate(flops=cost, bytes_accessed=0, transcendentals=0),
    )(*args)


def on_device(
    load_current, row_conductance, col_conductance, via_conductance, pad_mask, via_mask, row_residual, col_residual
):
    scen, rows, cols = load_current.shape
    size = rows * scen

    def f32(*shape):
        return jax.ShapeDtypeStruct(shape, F32)

    def vmem(*shape):
        return pltpu.VMEM(shape, F32)

    pick = jnp.asarray(picker(cols))
    source, start = (jnp.asarray(m) for m in spread(cols))

    wide = HALO * scen + 2 * SLOT + 8
    lf, msg_a, msg_b = call(
        pack_kernel,
        (f32(size, cols), f32(wide, cols), f32(wide, cols)),
        [],
        10**5,
        load_current, row_conductance, via_conductance, via_mask, row_residual,
    )
    got_a, got_b = exchange(msg_a, msg_b, "gx")

    ext = rows + 2 * SLOT
    reach = (rows + 2 * (STEPS - 1)) * scen
    packed = size + cols * (-(-(4 * scen + rows) // cols))
    v, t, fv, ft, fl, msg = call(
        functools.partial(fields_kernel, scen),
        (
            f32(size, cols), f32(size, cols), f32(reach, cols), f32(reach, cols), f32(size, cols),
            f32(size // cols * BLOCK + 24, cols),
        ),
        [vmem(ext, cols), vmem(ext, cols), vmem(ext, cols), vmem(5, rows, cols), vmem(packed, cols)],
        10**7,
        lf, row_conductance, col_conductance, via_conductance, pad_mask, via_mask, col_residual, got_a, got_b, pick,
    )

    gv, gt, br = call(
        functools.partial(row_stress_kernel, scen, rows),
        (f32(size, cols), f32(size, cols), f32(rows, cols)),
        [vmem(reach, cols), vmem(reach, cols), vmem(rows + 16, cols)],
        10**7,
        fv, ft, row_residual, got_a, got_b,
    )

    first_msg, received = msg, []
    step, count = 1, lax.axis_size("gy")
    sums = msg[-8:]
    while step < count:
        got = swap(msg, "gy", step)
        received.append(got)
        merge = functools.partial(merge_kernel, scen, "gy", step)
        if 2 * step < count:
            msg, sums = call(merge, (f32(*msg.shape), f32(8, cols)), [], 10**5, msg, got)
        else:
            sums = call(merge, (f32(8, cols),), [], 10**5, msg, got)[0]
        step *= 2

    gl, bc = call(
        functools.partial(col_stress_kernel, scen, rows),
        (f32(size, cols), f32(rows, cols)),
        [vmem(size, cols)],
        10**7,
        fl, col_residual, first_msg, *received, source, start,
    )

    step = lax.axis_size("gx") // 2
    while step > 1:
        sums = sums + swap(sums, "gx", step)
        step //= 2
    other = swap(sums, "gx", 1)

    shape = f32(scen, rows, cols)
    return call(
        functools.partial(final_kernel, scen, rows),
        (shape, shape, shape),
        [],
        10**6,
        sums, other, v, t, gv, gt, gl, br, bc,
    )


def solution(mesh):
    field = P(None, ("grp", "gx"), "gy")
    grid = P(("grp", "gx"), "gy")
    return jax.shard_map(
        on_device,
        mesh=mesh,
        in_specs=(field,) + (grid,) * 7,
        out_specs=(field,) * 3,
        check_vma=False,
    )
```

```python
import functools

import jax
import jax.numpy as jnp
import numpy as np
from jax import lax
from jax.experimental import pallas as pl
from jax.experimental.pallas import tpu as pltpu
from jax.sharding import PartitionSpec as P

STEPS = 8
RELAX = 0.45
DRIVE = 4.0
PAD = 20.0
LEAK = 0.05

F32 = jnp.float32
HALO = STEPS + 1
SLOT = 16
BLOCK = 24

FIRST_LANES = [0, 12, 11, 1, 2, 3, 4, 5, 6]
LAST_LANES = [-1, 13, 14, 9, 15, -2, 8, -7, -6, -5, -4, -3]
LAST_AT = 12


def dot_nt(a, b):
    return lax.dot_general(
        a, b, (((1,), (1,)), ((), ())), precision=lax.Precision.HIGHEST, preferred_element_type=F32
    )


def dot_nn(a, b):
    return lax.dot_general(
        a, b, (((1,), (0,)), ((), ())), precision=lax.Precision.HIGHEST, preferred_element_type=F32
    )


def dot_tn(a, b):
    return lax.dot_general(
        a, b, (((0,), (0,)), ((), ())), precision=lax.Precision.HIGHEST, preferred_element_type=F32
    )


def picker(cols):
    e = np.zeros((BLOCK + 16 + 8, cols), np.float32)
    for i, lane in enumerate(FIRST_LANES):
        e[i, lane % cols] = 1
    for i, lane in enumerate(LAST_LANES):
        e[LAST_AT + i, lane % cols] = 1
    for i in range(8):
        e[BLOCK + i, i] = 1
        e[BLOCK + 8 + i, cols - 8 + i] = 1
    e[BLOCK + 16 :] = 1
    return e


def spread(cols):
    size = cols + 16
    sources, starts = [], []
    for first, last in ((0, 0), (1, 0), (0, 1), (1, 1)):
        rate = np.full(size + 1, RELAX)
        rate[0] = rate[size] = 0
        if first:
            rate[8] = 0
        if last:
            rate[8 + cols] = 0
        step = np.eye(size)
        for i in range(size):
            step[i, i] -= rate[i] + rate[i + 1]
            if i:
                step[i, i - 1] += rate[i]
            if i + 1 < size:
                step[i, i + 1] += rate[i + 1]
        power, total = np.eye(size), np.zeros((size, size))
        for _ in range(STEPS):
            total += power
            power = step @ power
        source = (RELAX * DRIVE * total)[8 : 8 + cols].T
        start = power[8 : 8 + cols].T
        extra = np.zeros((24, cols))
        extra[0:7] = source[1:8]
        extra[8:15] = source[8 + cols : 15 + cols]
        extra[16] = source[8]
        extra[17] = source[8 + cols - 2]
        extra[18] = source[8 + cols - 1]
        sources.append(np.concatenate([source[8 : 8 + cols], extra]))
        starts.append(np.concatenate([start[8 : 8 + cols], start[:8], start[8 + cols :]]))
    return np.stack(sources).astype(np.float32), np.stack(starts).astype(np.float32)


def place(axis):
    at, count = lax.axis_index(axis), lax.axis_size(axis)
    return at, at == 0, at == count - 1


def pack_kernel(*refs):
    args, (lf_ref, h_ref, via_ref, a_ref, b_ref), held, sem = refs[:5], refs[5:10], refs[10:15], refs[15]
    copies = [pltpu.make_async_copy(src, dst, sem.at[i]) for i, (src, dst) in enumerate(zip(args, held))]
    for copy in copies:
        copy.start()
    load_ref, rc_ref, vc_ref, vm_ref, rr_ref = held
    scen, rows, cols = load_ref.shape
    at, first, _ = place("gx")
    even = lax.rem(at, 2) == 0
    for copy in copies:
        copy.wait()
    for s in range(scen):
        lf_ref[pl.ds(s, rows, stride=scen), :] = load_ref[s].astype(F32)
    row = lax.broadcasted_iota(jnp.int32, (rows, cols), 0)
    h = jnp.where(jnp.logical_and(first, row == 0), 0.0, rc_ref[...])
    via = vm_ref[...].astype(F32) * vc_ref[...]
    h_ref[...] = h
    via_ref[...] = via
    n = HALO * scen

    def put(where, top, bottom):
        a_ref[where, :] = jnp.where(even, bottom, top)
        b_ref[where, :] = jnp.where(even, top, bottom)

    put(pl.ds(0, n), lf_ref[0:n, :], lf_ref[rows * scen - n :, :])
    put(pl.ds(n, SLOT), h[:SLOT], h[rows - SLOT :])
    put(pl.ds(n + SLOT, SLOT), via[:SLOT], via[rows - SLOT :])
    put(pl.ds(n + 2 * SLOT, 8), rr_ref[:8, :], rr_ref[rows - 8 :, :])


def fields_kernel(
    scen, lf_ref, h_ref, via_ref, cc_ref, pm_ref, cr_ref, a_ref, b_ref, pick_ref,
    v_ref, t_ref, fv_ref, ft_ref, fl_ref, msg_ref,
    inv_s, h_s, tie_s, low_s, w_s,
):
    rows, cols = h_ref.shape
    at_x = lax.axis_index("gx")
    odd = lax.rem(at_x, 2) == 1
    _, first_y, last_y = place("gy")
    n = HALO * scen

    def before(where):
        return jnp.where(odd, a_ref[where, :], b_ref[where, :])

    def after(where):
        return jnp.where(odd, b_ref[where, :], a_ref[where, :])

    lane = lax.broadcasted_iota(jnp.int32, (rows, cols), 1)
    h, via = h_ref[...], via_ref[...]
    at = pl.ds(n, SLOT)
    h_ext = jnp.concatenate([before(at), h, after(at)], 0)
    at = pl.ds(n + SLOT, SLOT)
    tie_ext = jnp.concatenate([before(at), via, after(at)], 0) + LEAK
    h_s[...] = h_ext
    tie_s[...] = tie_ext
    h_next = pltpu.roll(h_ext, h_ext.shape[0] - 1, 0)
    inv_s[...] = 1.0 / (h_ext + h_next + tie_ext)

    tie_low = via + pm_ref[...].astype(F32) * PAD + LEAK
    vs = jnp.where(jnp.logical_and(first_y, lane == 0), 0.0, cc_ref[...])
    open_end = jnp.logical_and(jnp.logical_not(last_y), lane == cols - 1)
    vs_next = jnp.where(lane == cols - 1, 0.0, pltpu.roll(vs, cols - 1, 1))
    diag_low = vs + vs_next + tie_low
    low_s[0] = via
    low_s[1] = jnp.where(open_end, 0.0, -1.0 / diag_low)
    low_s[2] = tie_low
    low_s[3] = jnp.where(jnp.logical_or(open_end, lane == 0), 0.0, vs)
    low_s[4] = jnp.where(
        lane == 12,
        pltpu.roll(vs, 12, 1),
        jnp.where(
            lane == 13,
            pltpu.roll(diag_low, 14, 1),
            jnp.where(lane == 14, pltpu.roll(tie_low, 15, 1), pltpu.roll(vs, 16, 1)),
        ),
    )
    wide = lax.broadcasted_iota(jnp.int32, (scen, cols), 1)
    is_flux = jnp.logical_or(
        jnp.logical_and(wide >= 1, wide <= 6), jnp.logical_and(wide >= cols - 7, wide <= cols - 3)
    )
    is_t = jnp.logical_or(wide == 0, wide == cols - 2)
    is_end = wide == cols - 1
    is_rolled = jnp.logical_and(wide >= 8, wide <= 11)

    def load(r):
        if r < 0:
            return before(pl.ds((r + HALO) * scen, scen))
        if r >= rows:
            return after(pl.ds((r - rows) * scen, scen))
        return lf_ref[pl.ds(r * scen, scen), :]

    def bc(ref, r):
        return jnp.broadcast_to(ref[pl.ds(r, 1), :], (scen, cols))

    def low(k, r):
        return jnp.broadcast_to(low_s[k, pl.ds(r, 1), :], (scen, cols))

    g0 = g1 = g2 = g3 = jnp.zeros((scen, cols), F32)
    v0 = dv0 = hv0 = t0 = ht0 = l0 = None
    for r in range(-HALO, rows + HALO):
        l1 = load(r)
        v1 = l1 * bc(inv_s, r + SLOT)
        dv1 = hv1 = None
        if r > -HALO:
            dv1 = v0 - v1
            hv1 = bc(h_s, r + SLOT) * dv1
        if r > 1 - HALO:
            m = r - 1
            own = 0 <= m < rows
            fv = hv0 - hv1
            tie = bc(tie_s, m + SLOT)
            q_up = tie * v0 - fv
            t1 = q_up * bc(inv_s, m + SLOT)
            ht1 = None
            if m > 1 - HALO:
                dt = t0 - t1
                ht1 = bc(h_s, m + SLOT) * dt
                if m > 2 - HALO:
                    ft_ref[pl.ds((m - 1 + STEPS - 1) * scen, scen), :] = ht0 - ht1
                if m < rows + STEPS - 1:
                    fv_ref[pl.ds((m + STEPS - 1) * scen, scen), :] = fv
            if own:
                v_ref[pl.ds(m, scen, stride=rows), :] = v0
                t_ref[pl.ds(m, scen, stride=rows), :] = t1
                via_m = low(0, m)
                q = via_m * v0
                tl = q * low(1, m)
                dl = pltpu.roll(tl, 1, 1) - tl
                jl = low(3, m) * dl
                fl = jl - pltpu.roll(jl, cols - 1, 1)
                fl_ref[pl.ds(m * scen, scen), :] = fl
                p = via_m * t1
                g0 += l0 * v0
                g1 += hv0 * dv0 + tie * v0 * v0
                g2 += q_up * t1 - q * tl
                g3 += ht1 * dt + tie * t1 * t1 + tl * (low(2, m) * tl - 2.0 * p) + jl * dl
                rolled = pltpu.roll(jnp.where(is_end, p, jl), 10, 1)
                w_s[pl.ds(m * scen, scen), :] = jnp.where(
                    is_flux,
                    fl,
                    jnp.where(is_t, tl, jnp.where(is_end, q, jnp.where(is_rolled, rolled, low(4, m)))),
                )
            t0, ht0 = t1, ht1
        l0, v0, dv0, hv0 = l1, v1, dv1, hv1

    size = rows * scen
    for k, g in enumerate((g0, g1, g2, g3)):
        w_s[pl.ds(size + k * scen, scen), :] = g
    w_s[pl.ds(size + 4 * scen, rows), :] = cr_ref[...]
    w_s[size + 4 * scen + rows :, :] = jnp.zeros((w_s.shape[0] - size - 4 * scen - rows, cols), F32)
    picked = dot_nt(pick_ref[...], w_s[...])
    for k in range(size // cols):
        msg_ref[pl.ds(k * BLOCK, BLOCK), :] = picked[:BLOCK, k * cols : (k + 1) * cols]
    msg_ref[size // cols * BLOCK :, :] = picked[BLOCK:, size : size + cols]


def strips(ref, parts, cols):
    return jnp.concatenate([ref[pl.ds(k * BLOCK, BLOCK), :] for k in range(parts)], 1)


def meet(last, first):
    q, d, tie, p, vs, t_in = (last[LAST_AT + i : LAST_AT + i + 1] for i in range(6))
    t_next, vs_next = first[0:1], first[1:2]
    diag = d + vs_next
    t = -q / jnp.where(diag > 0, diag, 1.0)
    j_in = vs * (t_in - t)
    j_out = vs_next * (t - t_next)
    return q, tie, p, t, t_in, t_next, j_in, j_out


def merge_kernel(scen, axis, step, mine_ref, got_ref, *out_refs):
    cols = mine_ref.shape[1]
    parts = (mine_ref.shape[0] - 24) // BLOCK
    on_left = lax.rem(lax.div(lax.axis_index(axis), step), 2) == 0
    mine, got = strips(mine_ref, parts, cols), strips(got_ref, parts, cols)
    left, right = jnp.where(on_left, mine, got), jnp.where(on_left, got, mine)
    q, tie, p, t, t_in, t_next, j_in, j_out = meet(left, right)
    i2 = -q * t
    i3 = t * (tie * t - 2.0 * p) + j_in * (t_in - t) + j_out * (t - t_next)
    both = jnp.concatenate([i2, i3], 0)
    both = sum(both[:, k * cols : (k + 1) * cols] for k in range(parts))
    shift = scen
    while shift < cols:
        both = both + pltpu.roll(both, shift, 1)
        shift *= 2
    lane = lax.broadcasted_iota(jnp.int32, (8, cols), 1)
    group = lax.div(lane, scen)
    add = jnp.where(group == 2, both[0:1], jnp.where(group == 3, both[1:2], 0.0))
    base = parts * BLOCK
    sums = mine_ref[base + 16 :, :] + got_ref[base + 16 :, :] + add
    if len(out_refs) == 2:
        msg_ref, sums_ref = out_refs
        row = lax.broadcasted_iota(jnp.int32, (BLOCK, cols), 0)
        for k in range(parts):
            at = slice(k * cols, (k + 1) * cols)
            msg_ref[pl.ds(k * BLOCK, BLOCK), :] = jnp.where(row < LAST_AT, left[:, at], right[:, at])
        a, b = mine_ref[pl.ds(base, 16), :], got_ref[pl.ds(base, 16), :]
        msg_ref[pl.ds(base, 8), :] = jnp.where(on_left, a[:8], b[:8])
        msg_ref[pl.ds(base + 8, 8), :] = jnp.where(on_left, b[8:], a[8:])
        msg_ref[base + 16 :, :] = sums
    else:
        (sums_ref,) = out_refs
    sums_ref[...] = sums


def row_stress_kernel(scen, rows, fv_ref, ft_ref, rr_ref, a_ref, b_ref, gv_ref, gt_ref, br_ref, sv_s, st_s, s0_s):
    cols = fv_ref.shape[1]
    at_x, first, last = place("gx")
    odd = lax.rem(at_x, 2) == 1
    n = HALO * scen + 2 * SLOT
    count = rows + 2 * (STEPS - 1)
    rate_first = jnp.where(first, 0.0, RELAX)
    rate_last = jnp.where(last, 0.0, RELAX)

    def rate(r):
        return rate_first if r == 0 else rate_last if r == rows else RELAX

    s0 = jnp.concatenate(
        [
            jnp.where(odd, a_ref[n : n + 8, :], b_ref[n : n + 8, :]),
            rr_ref[...],
            jnp.where(odd, b_ref[n : n + 8, :], a_ref[n : n + 8, :]),
        ],
        0,
    )
    size = rows + 16
    row = lax.broadcasted_iota(jnp.int32, (size, cols), 0)
    rates = jnp.where(row == 8, rate_first, jnp.where(row == 8 + rows, rate_last, RELAX))

    sv_s[...] = fv_ref[...]
    st_s[...] = ft_ref[...]
    s0_s[...] = s0

    def one(_, carry):
        now = s0_s[...]
        flux = rates * (pltpu.roll(now, 1, 0) - now)
        s0_s[...] = now + flux - pltpu.roll(flux, size - 1, 0)
        for f_ref, s_ref in ((fv_ref, sv_s), (ft_ref, st_s)):
            here = s_ref[pl.ds(0, scen), :]
            flux = jnp.zeros_like(here)
            for i in range(count):
                r = i - (STEPS - 1)
                at = pl.ds(i * scen, scen)
                if i + 1 < count:
                    after = s_ref[pl.ds((i + 1) * scen, scen), :]
                    flux_next = rate(r + 1) * (here - after)
                else:
                    after, flux_next = here, jnp.zeros_like(here)
                s_ref[at, :] = here + (flux - flux_next) + f_ref[at, :]
                here, flux = after, flux_next
        return carry

    lax.fori_loop(0, STEPS - 1, one, 0)
    now = s0_s[...]
    flux = rates * (pltpu.roll(now, 1, 0) - now)
    now = now + flux - pltpu.roll(flux, size - 1, 0)
    br_ref[...] = now[8 : 8 + rows]
    gain = RELAX * DRIVE
    for m in range(rows):
        at = pl.ds((m + STEPS - 1) * scen, scen)
        gv_ref[pl.ds(m, scen, stride=rows), :] = gain * sv_s[at, :]
        gt_ref[pl.ds(m, scen, stride=rows), :] = gain * st_s[at, :]


def col_stress_kernel(scen, rows, fl_ref, cr_ref, mine_ref, *rest):
    *got_refs, source_ref, start_ref, gl_ref, bc_ref, out_s = rest
    cols = fl_ref.shape[1]
    parts = rows * scen // cols
    base = parts * BLOCK
    at, first, last = place("gy")
    kind = first.astype(jnp.int32) + 2 * last.astype(jnp.int32)
    own = strips(mine_ref, parts, cols)
    before, after = jnp.zeros_like(own), jnp.zeros_like(own)
    res_before = jnp.zeros((8, cols), F32)
    res_after = jnp.zeros((8, cols), F32)
    for k, ref in enumerate(got_refs):
        step = 1 << k
        rest_of = lax.rem(at, step)
        bit = lax.rem(lax.div(at, step), 2)
        block = strips(ref, parts, cols)
        from_right = jnp.logical_and(bit == 0, rest_of == step - 1)
        from_left = jnp.logical_and(bit == 1, rest_of == 0)
        after = jnp.where(from_right, block, after)
        before = jnp.where(from_left, block, before)
        res_after = jnp.where(from_right, ref[pl.ds(base, 8), :], res_after)
        res_before = jnp.where(from_left, ref[pl.ds(base + 8, 8), :], res_before)
    _, _, _, _, _, _, jl_last, jl_0 = meet(before, own)
    _, _, _, _, _, _, jr_last, jr_0 = meet(own, after)
    jr_last = jnp.where(last, 0.0, jr_last)
    jr_0 = jnp.where(last, 0.0, jr_0)
    lo = LAST_AT + 6
    zero = jnp.zeros_like(jl_0)
    strip = jnp.concatenate(
        [
            before[lo + 1 : lo + 6],
            before[lo : lo + 1] - jl_last,
            jl_last - jl_0,
            zero,
            jr_0 - after[2:3],
            after[3:9],
            zero,
            jl_0,
            -jr_last,
            jr_last - jr_0,
            zero,
            zero,
            zero,
            zero,
            zero,
        ],
        0,
    )
    source = source_ref[kind]
    out_s[...] = dot_nn(fl_ref[...], source[:cols]) + dot_tn(strip, source[cols:])
    for m in range(rows):
        gl_ref[pl.ds(m, scen, stride=rows), :] = out_s[pl.ds(m * scen, scen), :]
    start = start_ref[kind]
    edge = dot_tn(jnp.concatenate([res_before, res_after], 0), start[cols:])
    skip = 4 * scen
    bc_ref[...] = dot_nn(cr_ref[...], start[:cols]) + edge[skip : skip + rows]


def final_kernel(
    scen, rows, a_ref, b_ref, v_ref, t_ref, gv_ref, gt_ref, gl_ref, br_ref, bc_ref, up_ref, row_ref, col_ref
):
    cols = v_ref.shape[1]
    sums = a_ref[...] + b_ref[...]
    g0, g1, g2, g3 = (sums if k == 0 else pltpu.roll(sums, cols - k * scen, 1) for k in range(4))
    alpha = g0 / g1
    rz = alpha * alpha * g2 - g0
    grow = alpha * g2 / g1
    beta_alpha = rz / (alpha * alpha * (g3 - g2 * g2 / g1))
    c0 = alpha + beta_alpha * grow
    c1 = -alpha * beta_alpha
    lane = lax.broadcasted_iota(jnp.int32, (scen, cols), 1)
    sub = lax.broadcasted_iota(jnp.int32, (scen, cols), 0)

    def column(c):
        tall = jnp.concatenate([c] * (scen // 8), 0)
        return jnp.sum(jnp.where(lane == sub, tall, 0.0), 1, keepdims=True)

    c0, c1 = column(c0), column(c1)
    br, bc = br_ref[...], bc_ref[...]
    for s in range(scen):
        at = pl.ds(s * rows, rows)
        a = jnp.broadcast_to(c0[s : s + 1], (rows, cols))
        b = jnp.broadcast_to(c1[s : s + 1], (rows, cols))
        up_ref[s] = a * v_ref[at, :] + b * t_ref[at, :]
        row_ref[s] = br + a * gv_ref[at, :] + b * gt_ref[at, :]
        col_ref[s] = bc + b * gl_ref[at, :]


def swap(block, axis, step):
    count = lax.axis_size(axis)
    return lax.ppermute(block, axis, [(i, i ^ step) for i in range(count)])


def exchange(even_side, odd_side, axis):
    count = lax.axis_size(axis)

    def pairs(start):
        return [(i + a, i + 1 - a) for i in range(start, count - 1, 2) for a in (0, 1)]

    return lax.ppermute(even_side, axis, pairs(0)), lax.ppermute(odd_side, axis, pairs(1))


def call(kernel, out, scratch, cost, *args, space=pltpu.VMEM):
    return pl.pallas_call(
        kernel,
        out_shape=out,
        in_specs=[pl.BlockSpec(memory_space=space)] * len(args),
        out_specs=jax.tree.map(lambda _: pl.BlockSpec(memory_space=pltpu.VMEM), out),
        scratch_shapes=scratch,
        compiler_params=pltpu.CompilerParams(vmem_limit_bytes=24 * 2**20),
        cost_estimate=pl.CostEstimate(flops=cost, bytes_accessed=0, transcendentals=0),
    )(*args)


def on_device(
    load_current, row_conductance, col_conductance, via_conductance, pad_mask, via_mask, row_residual, col_residual
):
    scen, rows, cols = load_current.shape
    size = rows * scen

    def f32(*shape):
        return jax.ShapeDtypeStruct(shape, F32)

    def vmem(*shape):
        return pltpu.VMEM(shape, F32)

    pick = jnp.asarray(picker(cols))
    source, start = (jnp.asarray(m) for m in spread(cols))

    wide = HALO * scen + 2 * SLOT + 8
    sources = (load_current, row_conductance, via_conductance, via_mask, row_residual)
    lf, h, via, msg_a, msg_b = call(
        pack_kernel,
        (f32(size, cols), f32(rows, cols), f32(rows, cols), f32(wide, cols), f32(wide, cols)),
        [pltpu.VMEM(x.shape, x.dtype) for x in sources] + [pltpu.SemaphoreType.DMA((len(sources),))],
        10**5,
        *(pltpu.with_memory_space_constraint(x, pltpu.HBM) for x in sources),
        space=pltpu.HBM,
    )
    got_a, got_b = exchange(msg_a, msg_b, "gx")

    ext = rows + 2 * SLOT
    reach = (rows + 2 * (STEPS - 1)) * scen
    packed = size + cols * (-(-(4 * scen + rows) // cols))
    v, t, fv, ft, fl, msg = call(
        functools.partial(fields_kernel, scen),
        (
            f32(size, cols), f32(size, cols), f32(reach, cols), f32(reach, cols), f32(size, cols),
            f32(size // cols * BLOCK + 24, cols),
        ),
        [vmem(ext, cols), vmem(ext, cols), vmem(ext, cols), vmem(5, rows, cols), vmem(packed, cols)],
        10**7,
        lf, h, via, col_conductance, pad_mask, col_residual, got_a, got_b, pick,
    )

    gv, gt, br = call(
        functools.partial(row_stress_kernel, scen, rows),
        (f32(size, cols), f32(size, cols), f32(rows, cols)),
        [vmem(reach, cols), vmem(reach, cols), vmem(rows + 16, cols)],
        10**7,
        fv, ft, row_residual, got_a, got_b,
    )

    first_msg, received = msg, []
    step, count = 1, lax.axis_size("gy")
    sums = msg[-8:]
    while step < count:
        got = swap(msg, "gy", step)
        received.append(got)
        if step == 1:
            got, br = lax.optimization_barrier((got, br))
        merge = functools.partial(merge_kernel, scen, "gy", step)
        if 2 * step < count:
            msg, sums = call(merge, (f32(*msg.shape), f32(8, cols)), [], 10**5, msg, got)
        else:
            sums = call(merge, (f32(8, cols),), [], 10**5, msg, got)[0]
        step *= 2

    gl, bc = call(
        functools.partial(col_stress_kernel, scen, rows),
        (f32(size, cols), f32(rows, cols)),
        [vmem(size, cols)],
        10**7,
        fl, col_residual, first_msg, *received, source, start,
    )

    step = lax.axis_size("gx") // 2
    while step > 1:
        got = swap(sums, "gx", step)
        if 2 * step == lax.axis_size("gx"):
            got, bc = lax.optimization_barrier((got, bc))
        sums = sums + got
        step //= 2
    other = swap(sums, "gx", 1)

    shape = f32(scen, rows, cols)
    return call(
        functools.partial(final_kernel, scen, rows),
        (shape, shape, shape),
        [],
        10**6,
        sums, other, v, t, gv, gt, gl, br, bc,
    )


def solution(mesh):
    field = P(None, ("grp", "gx"), "gy")
    grid = P(("grp", "gx"), "gy")
    return jax.shard_map(
        on_device,
        mesh=mesh,
        in_specs=(field,) + (grid,) * 7,
        out_specs=(field,) * 3,
        check_vma=False,
    )
```

```python
import functools

import jax
import jax.numpy as jnp
import numpy as np
from jax import lax
from jax.experimental import pallas as pl
from jax.experimental.pallas import tpu as pltpu
from jax.sharding import PartitionSpec as P

STEPS = 8
RELAX = 0.45
DRIVE = 4.0
PAD = 20.0
LEAK = 0.05

F32 = jnp.float32
HALO = STEPS + 1
SLOT = 16

SUM_LANES = [0, 12, -1, 13, 14, 9, 15, -2]
FIRST_LANES = [11, 1, 2, 3, 4, 5, 6]
LAST_LANES = [8, -7, -6, -5, -4, -3]
PICKED = 8 + 8 + 8


def dot_nt(a, b):
    return lax.dot_general(
        a, b, (((1,), (1,)), ((), ())), precision=lax.Precision.HIGHEST, preferred_element_type=F32
    )


def dot_nn(a, b):
    return lax.dot_general(
        a, b, (((1,), (0,)), ((), ())), precision=lax.Precision.HIGHEST, preferred_element_type=F32
    )


def dot_tn(a, b):
    return lax.dot_general(
        a, b, (((0,), (0,)), ((), ())), precision=lax.Precision.HIGHEST, preferred_element_type=F32
    )


def picker(cols):
    e = np.zeros((PICKED + 8 + 16, cols), np.float32)
    for base, lanes in ((0, SUM_LANES), (8, FIRST_LANES), (16, LAST_LANES)):
        for i, lane in enumerate(lanes):
            e[base + i, lane % cols] = 1
    e[PICKED : PICKED + 8] = 1
    for i in range(8):
        e[PICKED + 8 + i, i] = 1
        e[PICKED + 16 + i, cols - 8 + i] = 1
    return e


def spread(cols):
    size = cols + 16
    sources, starts = [], []
    for first, last in ((0, 0), (1, 0), (0, 1), (1, 1)):
        rate = np.full(size + 1, RELAX)
        rate[0] = rate[size] = 0
        if first:
            rate[8] = 0
        if last:
            rate[8 + cols] = 0
        step = np.eye(size)
        for i in range(size):
            step[i, i] -= rate[i] + rate[i + 1]
            if i:
                step[i, i - 1] += rate[i]
            if i + 1 < size:
                step[i, i + 1] += rate[i + 1]
        power, total = np.eye(size), np.zeros((size, size))
        for _ in range(STEPS):
            total += power
            power = step @ power
        source = (RELAX * DRIVE * total)[8 : 8 + cols].T
        start = power[8 : 8 + cols].T
        extra = np.zeros((24, cols))
        extra[0:7] = source[1:8]
        extra[8:15] = source[8 + cols : 15 + cols]
        extra[16] = source[8]
        extra[17] = source[8 + cols - 2]
        extra[18] = source[8 + cols - 1]
        sources.append(np.concatenate([source[8 : 8 + cols], extra]))
        starts.append(np.concatenate([start[8 : 8 + cols], start[:8], start[8 + cols :]]))
    return np.stack(sources).astype(np.float32), np.stack(starts).astype(np.float32)


def place(axis):
    at, count = lax.axis_index(axis), lax.axis_size(axis)
    return at, at == 0, at == count - 1


def pick_side(odd, even_ref, odd_ref):
    def before(*where):
        return jnp.where(odd, even_ref[where], odd_ref[where])

    def after(*where):
        return jnp.where(odd, odd_ref[where], even_ref[where])

    return before, after


def pack_kernel(*refs):
    args, outs, held, sem = refs[:5], refs[5:10], refs[10:15], refs[15]
    copies = [pltpu.make_async_copy(src, dst, sem.at[i]) for i, (src, dst) in enumerate(zip(args, held))]
    for copy in copies:
        copy.start()
    load_ref, rc_ref, vc_ref, vm_ref, rr_ref = held
    lf_ref, h_ref, via_ref, a_ref, b_ref = outs
    scen, rows, cols = load_ref.shape
    at, first, _ = place("gx")
    even = lax.rem(at, 2) == 0
    for copy in copies:
        copy.wait()
    for s in range(scen):
        lf_ref[pl.ds(s, rows, stride=scen), :] = load_ref[s].astype(F32)
    row = lax.broadcasted_iota(jnp.int32, (rows, cols), 0)
    h = jnp.where(jnp.logical_and(first, row == 0), 0.0, rc_ref[...])
    via = vm_ref[...].astype(F32) * vc_ref[...]
    h_ref[...] = h
    via_ref[...] = via

    def put(where, top, bottom):
        a_ref[where, :] = jnp.where(even, bottom, top)
        b_ref[where, :] = jnp.where(even, top, bottom)

    n = HALO * scen
    put(pl.ds(0, n), lf_ref[0:n, :], lf_ref[rows * scen - n :, :])
    put(pl.ds(n, SLOT), h[:SLOT], h[rows - SLOT :])
    put(pl.ds(n + SLOT, SLOT), via[:SLOT], via[rows - SLOT :])
    put(pl.ds(n + 2 * SLOT, 8), rr_ref[:8, :], rr_ref[rows - 8 :, :])


def packer(scen, cols):
    lane = lax.broadcasted_iota(jnp.int32, (scen, cols), 1)
    is_flux = jnp.logical_or(
        jnp.logical_and(lane >= 1, lane <= 6), jnp.logical_and(lane >= cols - 7, lane <= cols - 3)
    )
    is_t = jnp.logical_or(lane == 0, lane == cols - 2)
    is_end = lane == cols - 1
    is_rolled = jnp.logical_and(lane >= 8, lane <= 11)

    def pack(tl, q, jl, fl, p, grid_row):
        moved = jl if p is None else jnp.where(is_end, p, jl)
        rolled = pltpu.roll(moved, 10, 1)
        return jnp.where(
            is_flux, fl, jnp.where(is_t, tl, jnp.where(is_end, q, jnp.where(is_rolled, rolled, grid_row)))
        )

    def add_p(w, p):
        return jnp.where(lane == 9, pltpu.roll(p, 10, 1), w)

    return pack, add_p


def lower_row(v, via, minus_inv, vs, cols):
    q = via * v
    tl = q * minus_inv
    dl = pltpu.roll(tl, 1, 1) - tl
    jl = vs * dl
    return q, tl, dl, jl, jl - pltpu.roll(jl, cols - 1, 1)


def core_kernel(
    scen, lf_ref, h_ref, via_ref, cc_ref, pm_ref, cr_ref, pick_ref,
    fl_ref, acc_ref, edge_ref, low_ref, strip_ref, res_ref,
    inv_s, low_s, w_s,
):
    rows, cols = h_ref.shape
    _, first_y, last_y = place("gy")
    lane = lax.broadcasted_iota(jnp.int32, (rows, cols), 1)
    h, via = h_ref[...], via_ref[...]
    inv_s[...] = 1.0 / (h + pltpu.roll(h, rows - 1, 0) + via + LEAK)

    tie_low = via + pm_ref[...].astype(F32) * PAD + LEAK
    vs = jnp.where(jnp.logical_and(first_y, lane == 0), 0.0, cc_ref[...])
    open_end = jnp.logical_and(jnp.logical_not(last_y), lane == cols - 1)
    vs_next = jnp.where(lane == cols - 1, 0.0, pltpu.roll(vs, cols - 1, 1))
    diag_low = vs + vs_next + tie_low
    low_s[0] = jnp.where(open_end, 0.0, -1.0 / diag_low)
    low_s[1] = tie_low
    low_s[2] = jnp.where(jnp.logical_or(open_end, lane == 0), 0.0, vs)
    low_s[3] = jnp.where(
        lane == 12,
        pltpu.roll(vs, 12, 1),
        jnp.where(
            lane == 13,
            pltpu.roll(diag_low, 14, 1),
            jnp.where(lane == 14, pltpu.roll(tie_low, 15, 1), pltpu.roll(vs, 16, 1)),
        ),
    )
    low_ref[...] = jnp.concatenate([low_s[k, rows - 1 : rows, :] for k in range(4)] * 2, 0)
    pack, _ = packer(scen, cols)

    def bc(ref, r):
        return jnp.broadcast_to(ref[pl.ds(r, 1), :], (scen, cols))

    def low(k, r):
        return jnp.broadcast_to(low_s[k, pl.ds(r, 1), :], (scen, cols))

    def keep(i, x):
        edge_ref[pl.ds(i * scen, scen), :] = x

    zero = jnp.zeros((scen, cols), F32)
    g0 = g1 = g2 = g3 = zero
    v0 = hv0 = t0 = None
    last = rows - 1
    for r in range(rows):
        v1 = hv1 = dv1 = None
        if r < last:
            load = lf_ref[pl.ds(r * scen, scen), :]
            v1 = load * bc(inv_s, r)
            g0 += load * v1
            g1 += (bc(via_ref, r) + LEAK) * v1 * v1
            if r > 0:
                dv1 = v0 - v1
                hv1 = bc(h_ref, r) * dv1
                g1 += hv1 * dv1
        if r > 0:
            m = r - 1
            via_m = bc(via_ref, m)
            tie = via_m + LEAK
            q, tl, dl, jl, fl = lower_row(v0, via_m, low(0, m), low(2, m), cols)
            fl_ref[pl.ds(m * scen, scen), :] = fl
            g2 -= q * tl
            g3 += low(1, m) * tl * tl + jl * dl
            p = t1 = None
            if 0 < m < last - 1:
                q_up = tie * v0 - hv0 + hv1
                t1 = q_up * bc(inv_s, m)
                p = via_m * t1
                g2 += q_up * t1
                g3 += tie * t1 * t1 - 2.0 * p * tl
                if m > 1:
                    dt = t0 - t1
                    g3 += bc(h_ref, m) * dt * dt
            w = pack(tl, q, jl, fl, p, low(3, m))
            w_s[pl.ds(m * scen, scen), :] = w
            if m == 0:
                keep(0, v0)
                keep(1, hv1)
                keep(3, tl)
                keep(8, w)
            if m == 1:
                keep(2, t1)
            if m == last - 2:
                keep(6, t1)
            if m == last - 1:
                keep(4, v0)
                keep(5, hv0)
                keep(7, tl)
                keep(9, w)
            t0 = t1
        v0, hv0 = v1, hv1

    size = rows * scen
    fl_ref[pl.ds(last * scen, scen), :] = zero
    w_s[pl.ds(last * scen, scen), :] = zero
    w_s[pl.ds(size, rows), :] = cr_ref[...]
    w_s[size + rows :, :] = jnp.zeros((w_s.shape[0] - size - rows, cols), F32)
    for k, g in enumerate((g0, g1, g2, g3)):
        acc_ref[pl.ds(k * scen, scen), :] = g
    picked = dot_nt(pick_ref[...], w_s[...])
    for k in range(size // cols):
        strip_ref[pl.ds(k * PICKED, PICKED), :] = picked[:PICKED, k * cols : (k + 1) * cols]
    res_ref[...] = picked[PICKED + 8 :, size : size + cols]


def join_kernel(
    scen, lf_ref, h_ref, via_ref, acc_ref, edge_ref, low_ref, strip_ref, res_ref, a_ref, b_ref, pick_ref,
    msg_ref, other_ref, fl_ref,
    w_s,
):
    rows, cols = h_ref.shape
    odd_x = lax.rem(lax.axis_index("gx"), 2) == 1
    even_y = lax.rem(lax.axis_index("gy"), 2) == 0
    before, after = pick_side(odd_x, a_ref, b_ref)
    n = HALO * scen
    last = rows - 1

    def grid(h, via):
        tie = via + LEAK
        inv = 1.0 / (h + pltpu.roll(h, 15, 0) + tie)

        def row(x, i):
            return jnp.broadcast_to(x[i : i + 1], (scen, cols))

        return (lambda i: row(h, i)), (lambda i: row(tie, i)), (lambda i: row(inv, i)), (lambda i: row(via, i))

    def edge(i):
        return edge_ref[pl.ds(i * scen, scen), :]

    pack, add_p = packer(scen, cols)

    h, tie, inv, via = grid(
        jnp.concatenate([before(pl.ds(n + SLOT - 8, 8)), h_ref[:8, :]], 0),
        jnp.concatenate([before(pl.ds(n + 2 * SLOT - 8, 8)), via_ref[:8, :]], 0),
    )
    v0, hv1, t1, tl0 = (edge(i) for i in range(4))
    far, near = before(pl.ds(n - 2 * scen, scen)) * inv(6), before(pl.ds(n - scen, scen)) * inv(7)
    dv0 = near - v0
    hv0 = h(8) * dv0
    t_near = (tie(7) * near - h(7) * (far - near) + hv0) * inv(7)
    q_up = tie(8) * v0 - hv0 + hv1
    t0 = q_up * inv(8)
    d0, d1 = t_near - t0, t0 - t1
    p = via(8) * t0
    g1 = hv0 * dv0
    g2 = q_up * t0
    g3 = tie(8) * t0 * t0 + h(8) * d0 * d0 + h(9) * d1 * d1 - 2.0 * p * tl0
    w_first = add_p(edge(8), p)

    h, tie, inv, via = grid(
        jnp.concatenate([h_ref[rows - 8 :, :], after(pl.ds(n, 8))], 0),
        jnp.concatenate([via_ref[rows - 8 :, :], after(pl.ds(n + SLOT, 8))], 0),
    )
    v0, hv0, t0, tl0 = (edge(i) for i in range(4, 8))
    load = lf_ref[pl.ds(last * scen, scen), :]
    v1 = load * inv(7)
    v2 = after(pl.ds(0, scen)) * inv(8)
    dv1 = v0 - v1
    hv1, hv2 = h(7) * dv1, h(8) * (v1 - v2)
    q0 = tie(6) * v0 - hv0 + hv1
    q1 = tie(7) * v1 - hv1 + hv2
    t1 = q0 * inv(6)
    t2 = q1 * inv(7)
    d1, d2 = t0 - t1, t1 - t2
    p0, p1 = via(6) * t1, via(7) * t2
    g0 = load * v1
    g1 += hv1 * dv1 + tie(7) * v1 * v1
    g2 += q0 * t1 + q1 * t2
    g3 += tie(6) * t1 * t1 + tie(7) * t2 * t2 + h(6) * d1 * d1 + h(7) * d2 * d2 - 2.0 * p0 * tl0

    def low(k):
        return jnp.broadcast_to(low_ref[pl.ds(k, 1), :], (scen, cols))

    q, tl, dl, jl, fl = lower_row(v1, via(7), low(0), low(2), cols)
    fl_ref[...] = fl
    g2 -= q * tl
    g3 += tl * (low(1) * tl - 2.0 * p1) + jl * dl

    w_s[...] = jnp.zeros_like(w_s)
    w_s[0:scen, :] = w_first
    for k, g in enumerate((g0, g1, g2, g3)):
        w_s[pl.ds((k + 1) * scen, scen), :] = acc_ref[pl.ds(k * scen, scen), :] + g
    w_s[cols - 2 * scen : cols - scen, :] = add_p(edge(9), p0)
    w_s[cols - scen :, :] = pack(tl, q, jl, fl, p1, low(3))
    fresh = dot_nt(pick_ref[: PICKED + 8, :], w_s[...])

    lane = lax.broadcasted_iota(jnp.int32, (PICKED, cols), 1)
    parts = rows * scen // cols
    for k in range(parts):
        strip = strip_ref[pl.ds(k * PICKED, PICKED), :]
        if k == 0:
            strip = jnp.where(lane < scen, fresh[:PICKED], strip)
        if k == parts - 1:
            strip = jnp.where(lane >= cols - 2 * scen, fresh[:PICKED], strip)
        firsts, lasts = strip[8:16], strip[16:24]
        msg_ref[pl.ds(k * 16, 8), :] = strip[:8]
        msg_ref[pl.ds(k * 16 + 8, 8), :] = jnp.where(even_y, lasts, firsts)
        other_ref[pl.ds(k * 8, 8), :] = jnp.where(even_y, firsts, lasts)
    msg_ref[pl.ds(parts * 16, 8), :] = jnp.where(even_y, res_ref[8:, :], res_ref[:8, :])
    other_ref[pl.ds(parts * 8, 8), :] = jnp.where(even_y, res_ref[:8, :], res_ref[8:, :])
    msg_ref[pl.ds(parts * 16 + 8, 8), :] = fresh[PICKED:]


def across(ref, offset):
    parts = ref.shape[0] // 16 - 1
    return jnp.concatenate([ref[pl.ds(16 * k + offset, 8), :] for k in range(parts)], 1)


def merge_kernel(scen, axis, step, mine_ref, got_ref, other_ref, out_ref):
    cols = mine_ref.shape[1]
    parts = mine_ref.shape[0] // 16 - 1
    on_left = lax.rem(lax.div(lax.axis_index(axis), step), 2) == 0
    mine, got = across(mine_ref, 0), across(got_ref, 0)
    left, right = jnp.where(on_left, mine, got), jnp.where(on_left, got, mine)
    t_next, vs_next = right[0:1], right[1:2]
    q, d, tie, p, vs, t_in = (left[i : i + 1] for i in range(2, 8))
    t = -q / (d + vs_next)
    d_in, d_out = t_in - t, t - t_next
    i2 = -q * t
    i3 = t * (tie * t - 2.0 * p) + vs * d_in * d_in + vs_next * d_out * d_out
    both = jnp.concatenate([i2, i3], 0)
    both = sum(both[:, k * cols : (k + 1) * cols] for k in range(parts))
    shift = scen
    while shift < cols:
        both = both + pltpu.roll(both, shift, 1)
        shift *= 2
    group = lax.div(lax.broadcasted_iota(jnp.int32, (8, cols), 1), scen)
    add = jnp.where(group == 3, both[0:1], jnp.where(group == 4, both[1:2], 0.0))
    sums = mine_ref[parts * 16 + 8 :, :] + got_ref[parts * 16 + 8 :, :] + add
    if out_ref.shape[0] == 8:
        out_ref[...] = sums
    else:
        row = lax.broadcasted_iota(jnp.int32, (8, cols), 0)
        for k in range(parts):
            at = slice(k * cols, (k + 1) * cols)
            out_ref[pl.ds(k * 16, 8), :] = jnp.where(row < 2, left[:, at], right[:, at])
            out_ref[pl.ds(k * 16 + 8, 8), :] = other_ref[pl.ds(k * 8, 8), :]
        out_ref[pl.ds(parts * 16, 8), :] = other_ref[pl.ds(parts * 8, 8), :]
        out_ref[parts * 16 + 8 :, :] = sums


def row_kernel(
    scen, lf_ref, h_ref, via_ref, rr_ref, a_ref, b_ref,
    v_ref, t_ref, gv_ref, gt_ref, br_ref,
    inv_s, h_s, tie_s, fv_s, ft_s, sv_s, st_s, s0_s,
):
    rows, cols = h_ref.shape
    at_x, first, last = place("gx")
    before, after = pick_side(lax.rem(at_x, 2) == 1, a_ref, b_ref)
    n = HALO * scen
    at = pl.ds(n, SLOT)
    h = jnp.concatenate([before(at), h_ref[...], after(at)], 0)
    at = pl.ds(n + SLOT, SLOT)
    tie = jnp.concatenate([before(at), via_ref[...], after(at)], 0) + LEAK
    h_s[...] = h
    tie_s[...] = tie
    inv_s[...] = 1.0 / (h + pltpu.roll(h, h.shape[0] - 1, 0) + tie)

    def load(r):
        if r < 0:
            return before(pl.ds((r + HALO) * scen, scen))
        if r >= rows:
            return after(pl.ds((r - rows) * scen, scen))
        return lf_ref[pl.ds(r * scen, scen), :]

    def bc(ref, r):
        return jnp.broadcast_to(ref[pl.ds(r + SLOT, 1), :], (scen, cols))

    v0 = hv0 = t0 = ht0 = None
    for r in range(-HALO, rows + HALO):
        v1 = load(r) * bc(inv_s, r)
        hv1 = None
        if r > -HALO:
            hv1 = bc(h_s, r) * (v0 - v1)
        if r > 1 - HALO:
            m = r - 1
            fv = hv0 - hv1
            t1 = (bc(tie_s, m) * v0 - fv) * bc(inv_s, m)
            ht1 = None
            if m > 1 - HALO:
                ht1 = bc(h_s, m) * (t0 - t1)
                if m > 2 - HALO:
                    ft = ht0 - ht1
                    at = pl.ds((m - 1 + STEPS - 1) * scen, scen)
                    ft_s[at, :] = ft
                    st_s[at, :] = ft
                if m < rows + STEPS - 1:
                    at = pl.ds((m + STEPS - 1) * scen, scen)
                    fv_s[at, :] = fv
                    sv_s[at, :] = fv
            if 0 <= m < rows:
                v_ref[pl.ds(m, scen, stride=rows), :] = v0
                t_ref[pl.ds(m, scen, stride=rows), :] = t1
            t0, ht0 = t1, ht1
        v0, hv0 = v1, hv1

    n += 2 * SLOT
    count = rows + 2 * (STEPS - 1)
    rate_first = jnp.where(first, 0.0, RELAX)
    rate_last = jnp.where(last, 0.0, RELAX)

    def rate(r):
        return rate_first if r == 0 else rate_last if r == rows else RELAX

    size = rows + 16
    row = lax.broadcasted_iota(jnp.int32, (size, cols), 0)
    rates = jnp.where(row == 8, rate_first, jnp.where(row == 8 + rows, rate_last, RELAX))
    s0_s[...] = jnp.concatenate([before(pl.ds(n, 8)), rr_ref[...], after(pl.ds(n, 8))], 0)

    def start_step():
        now = s0_s[...]
        flux = rates * (pltpu.roll(now, 1, 0) - now)
        return now + flux - pltpu.roll(flux, size - 1, 0)

    def one(_, carry):
        s0_s[...] = start_step()
        for f_ref, s_ref in ((fv_s, sv_s), (ft_s, st_s)):
            here = s_ref[pl.ds(0, scen), :]
            flux = jnp.zeros_like(here)
            for i in range(count):
                r = i - (STEPS - 1)
                at = pl.ds(i * scen, scen)
                if i + 1 < count:
                    following = s_ref[pl.ds((i + 1) * scen, scen), :]
                    flux_next = rate(r + 1) * (here - following)
                else:
                    following, flux_next = here, jnp.zeros_like(here)
                s_ref[at, :] = here + (flux - flux_next) + f_ref[at, :]
                here, flux = following, flux_next
        return carry

    lax.fori_loop(0, STEPS - 1, one, 0)
    br_ref[...] = start_step()[8 : 8 + rows]
    gain = RELAX * DRIVE
    for m in range(rows):
        at = pl.ds((m + STEPS - 1) * scen, scen)
        gv_ref[pl.ds(m, scen, stride=rows), :] = gain * sv_s[at, :]
        gt_ref[pl.ds(m, scen, stride=rows), :] = gain * st_s[at, :]


def col_kernel(scen, fl_ref, fl_last_ref, cr_ref, own_ref, *rest):
    *got_refs, source_ref, start_ref, gl_ref, bc_ref, out_s = rest
    rows, cols = cr_ref.shape
    at, first, last = place("gy")
    kind = first.astype(jnp.int32) + 2 * last.astype(jnp.int32)
    odd = lax.rem(at, 2) == 1
    res_at = pl.ds(own_ref.shape[0] - 16, 8)

    def contents(ref):
        return across(ref, 0), across(ref, 8), ref[res_at, :]

    paired = contents(got_refs[0])
    met = tuple(jnp.zeros_like(x) for x in paired)
    for k, ref in enumerate(got_refs[1:], 1):
        span = lax.rem(at, 2 << k)
        here = jnp.logical_or(span == (1 << k) - 1, span == 1 << k)
        met = tuple(jnp.where(here, x, y) for x, y in zip(contents(ref), met))
    sums_before, before, res_before = (jnp.where(odd, x, y) for x, y in zip(paired, met))
    sums_after, after, res_after = (jnp.where(odd, y, x) for x, y in zip(paired, met))
    own = across(own_ref, 0)

    def seam(left, right):
        q, d, _, _, vs, t_in = (left[i : i + 1] for i in range(2, 8))
        t_next, vs_next = right[0:1], right[1:2]
        diag = d + vs_next
        t = -q / jnp.where(diag > 0, diag, 1.0)
        return vs * (t_in - t), vs_next * (t - t_next)

    jl_last, jl_0 = seam(sums_before, own)
    jr_last, jr_0 = seam(own, sums_after)
    jr_last = jnp.where(last, 0.0, jr_last)
    jr_0 = jnp.where(last, 0.0, jr_0)
    zero = jnp.zeros_like(jl_0)
    strip = jnp.concatenate(
        [
            before[1:6],
            before[0:1] - jl_last,
            jl_last - jl_0,
            zero,
            jr_0 - after[0:1],
            after[1:7],
            zero,
            jl_0,
            -jr_last,
            jr_last - jr_0,
            zero,
            zero,
            zero,
            zero,
            zero,
        ],
        0,
    )
    source = source_ref[kind]
    edge = dot_tn(strip, source[cols:])
    done = (rows - 1) * scen
    out_s[0:done, :] = dot_nn(fl_ref[0:done, :], source[:cols]) + edge[:done]
    out_s[done:, :] = dot_nn(fl_last_ref[...], source[:cols]) + edge[done:]
    for m in range(rows):
        gl_ref[pl.ds(m, scen, stride=rows), :] = out_s[pl.ds(m * scen, scen), :]
    start = start_ref[kind]
    edge = dot_tn(jnp.concatenate([res_before, res_after], 0), start[cols:])
    bc_ref[...] = dot_nn(cr_ref[...], start[:cols]) + edge[:rows]


def final_kernel(
    scen, rows, a_ref, b_ref, v_ref, t_ref, gv_ref, gt_ref, gl_ref, br_ref, bc_ref, up_ref, row_ref, col_ref
):
    cols = v_ref.shape[1]
    sums = a_ref[...] + b_ref[...]
    g0, g1, g2, g3 = (pltpu.roll(sums, cols - (k + 1) * scen, 1) for k in range(4))
    alpha = g0 / g1
    rz = alpha * alpha * g2 - g0
    grow = alpha * g2 / g1
    beta_alpha = rz / (alpha * alpha * (g3 - g2 * g2 / g1))
    c0 = alpha + beta_alpha * grow
    c1 = -alpha * beta_alpha
    lane = lax.broadcasted_iota(jnp.int32, (scen, cols), 1)
    sub = lax.broadcasted_iota(jnp.int32, (scen, cols), 0)

    def column(c):
        tall = jnp.concatenate([c] * (scen // 8), 0)
        return jnp.sum(jnp.where(lane == sub, tall, 0.0), 1, keepdims=True)

    c0, c1 = column(c0), column(c1)
    br, bc = br_ref[...], bc_ref[...]
    for s in range(scen):
        at = pl.ds(s * rows, rows)
        a = jnp.broadcast_to(c0[s : s + 1], (rows, cols))
        b = jnp.broadcast_to(c1[s : s + 1], (rows, cols))
        up_ref[s] = a * v_ref[at, :] + b * t_ref[at, :]
        row_ref[s] = br + a * gv_ref[at, :] + b * gt_ref[at, :]
        col_ref[s] = bc + b * gl_ref[at, :]


def swap(block, axis, mask):
    count = lax.axis_size(axis)
    return lax.ppermute(block, axis, [(i, i ^ mask) for i in range(count)])


def exchange(even_side, odd_side, axis):
    count = lax.axis_size(axis)

    def pairs(start):
        return [(i + a, i + 1 - a) for i in range(start, count - 1, 2) for a in (0, 1)]

    second = lax.ppermute(odd_side, axis, pairs(1))
    return lax.ppermute(even_side, axis, pairs(0)), second


def call(kernel, out, scratch, cost, *args, space=pltpu.VMEM):
    return pl.pallas_call(
        kernel,
        out_shape=out,
        in_specs=[pl.BlockSpec(memory_space=space)] * len(args),
        out_specs=jax.tree.map(lambda _: pl.BlockSpec(memory_space=pltpu.VMEM), out),
        scratch_shapes=scratch,
        compiler_params=pltpu.CompilerParams(vmem_limit_bytes=24 * 2**20),
        cost_estimate=pl.CostEstimate(flops=cost, bytes_accessed=0, transcendentals=0),
    )(*args)


def on_device(
    load_current, row_conductance, col_conductance, via_conductance, pad_mask, via_mask, row_residual, col_residual
):
    scen, rows, cols = load_current.shape
    size = rows * scen
    parts = size // cols

    def f32(*shape):
        return jax.ShapeDtypeStruct(shape, F32)

    def vmem(*shape):
        return pltpu.VMEM(shape, F32)

    pick = jnp.asarray(picker(cols))
    source, start = (jnp.asarray(m) for m in spread(cols))
    grid, field = f32(rows, cols), f32(size, cols)

    wide = f32(HALO * scen + 2 * SLOT + 8, cols)
    sources = (load_current, row_conductance, via_conductance, via_mask, row_residual)
    lf, h, via, x_a, x_b = call(
        pack_kernel,
        (field, grid, grid, wide, wide),
        [pltpu.VMEM(x.shape, x.dtype) for x in sources] + [pltpu.SemaphoreType.DMA((len(sources),))],
        10**5,
        *(pltpu.with_memory_space_constraint(x, pltpu.HBM) for x in sources),
        space=pltpu.HBM,
    )
    x_a, x_b = exchange(x_a, x_b, "gx")

    fl, acc, edge, low, strip, res = call(
        functools.partial(core_kernel, scen),
        (field, f32(4 * scen, cols), f32(10 * scen, cols), f32(8, cols), f32(parts * PICKED, cols), f32(16, cols)),
        [vmem(rows, cols), vmem(4, rows, cols), vmem(size + cols * (-(-rows // cols)), cols)],
        10**7,
        lf, h, via, col_conductance, pad_mask, col_residual, pick,
    )
    x_a, x_b, acc = lax.optimization_barrier((x_a, x_b, acc))

    msg, other, fl_last = call(
        functools.partial(join_kernel, scen),
        (f32(parts * 16 + 16, cols), f32(parts * 8 + 8, cols), f32(scen, cols)),
        [vmem(cols, cols)],
        10**6,
        lf, h, via, acc, edge, low, strip, res, x_a, x_b, pick,
    )

    ext = rows + 2 * SLOT
    reach = (rows + 2 * (STEPS - 1)) * scen
    v, t, gv, gt, br = call(
        functools.partial(row_kernel, scen),
        (field, field, field, field, grid),
        [vmem(ext, cols)] * 3 + [vmem(reach, cols)] * 4 + [vmem(rows + 16, cols)],
        10**7,
        lf, h, via, row_residual, x_a, x_b,
    )

    first_msg, received = msg, []
    step, count = 1, lax.axis_size("gy")
    while step < count:
        got = swap(msg, "gy", 2 * step - 1)
        received.append(got)
        if 2 * step >= count:
            got, br = lax.optimization_barrier((got, br))
        out = f32(*msg.shape) if 2 * step < count else f32(8, cols)
        msg = call(functools.partial(merge_kernel, scen, "gy", step), out, [], 10**5, msg, got, other)
        step *= 2
    sums = msg

    gl, bc = call(
        functools.partial(col_kernel, scen),
        (field, grid),
        [vmem(size, cols)],
        10**7,
        fl, fl_last, col_residual, first_msg, *received, source, start,
    )

    step = lax.axis_size("gx") // 2
    while step > 1:
        got = swap(sums, "gx", step)
        if 2 * step == lax.axis_size("gx"):
            got, bc = lax.optimization_barrier((got, bc))
        sums = sums + got
        step //= 2
    rest = swap(sums, "gx", 1)

    shape = f32(scen, rows, cols)
    return call(
        functools.partial(final_kernel, scen, rows),
        (shape, shape, shape),
        [],
        10**6,
        sums, rest, v, t, gv, gt, gl, br, bc,
    )


def solution(mesh):
    field = P(None, ("grp", "gx"), "gy")
    grid = P(("grp", "gx"), "gy")
    return jax.shard_map(
        on_device,
        mesh=mesh,
        in_specs=(field,) + (grid,) * 7,
        out_specs=(field,) * 3,
        check_vma=False,
    )
```

```python
import functools

import jax
import jax.numpy as jnp
import numpy as np
from jax import lax
from jax.experimental import pallas as pl
from jax.experimental.pallas import tpu as pltpu
from jax.sharding import PartitionSpec as P

STEPS = 8
RELAX = 0.45
DRIVE = 4.0
PAD = 20.0
LEAK = 0.05

F32 = jnp.float32
HALO = STEPS + 1
SLOT = 16

SUM_LANES = [0, 12, -1, 13, 14, 9, 15, -2]
FIRST_LANES = [11, 1, 2, 3, 4, 5, 6]
LAST_LANES = [8, -7, -6, -5, -4, -3]
PICKED = 8 + 8 + 8


def dot_nt(a, b):
    return lax.dot_general(
        a, b, (((1,), (1,)), ((), ())), precision=lax.Precision.HIGHEST, preferred_element_type=F32
    )


def dot_nn(a, b):
    return lax.dot_general(
        a, b, (((1,), (0,)), ((), ())), precision=lax.Precision.HIGHEST, preferred_element_type=F32
    )


def dot_tn(a, b):
    return lax.dot_general(
        a, b, (((0,), (0,)), ((), ())), precision=lax.Precision.HIGHEST, preferred_element_type=F32
    )


def picker(cols):
    e = np.zeros((PICKED + 8 + 16, cols), np.float32)
    for base, lanes in ((0, SUM_LANES), (8, FIRST_LANES), (16, LAST_LANES)):
        for i, lane in enumerate(lanes):
            e[base + i, lane % cols] = 1
    e[PICKED : PICKED + 8] = 1
    for i in range(8):
        e[PICKED + 8 + i, i] = 1
        e[PICKED + 16 + i, cols - 8 + i] = 1
    return e


def spread(cols):
    size = cols + 16
    sources, starts = [], []
    for first, last in ((0, 0), (1, 0), (0, 1), (1, 1)):
        rate = np.full(size + 1, RELAX)
        rate[0] = rate[size] = 0
        if first:
            rate[8] = 0
        if last:
            rate[8 + cols] = 0
        step = np.eye(size)
        for i in range(size):
            step[i, i] -= rate[i] + rate[i + 1]
            if i:
                step[i, i - 1] += rate[i]
            if i + 1 < size:
                step[i, i + 1] += rate[i + 1]
        power, total = np.eye(size), np.zeros((size, size))
        for _ in range(STEPS):
            total += power
            power = step @ power
        source = (RELAX * DRIVE * total)[8 : 8 + cols].T
        start = power[8 : 8 + cols].T
        extra = np.zeros((24, cols))
        extra[0:7] = source[1:8]
        extra[8:15] = source[8 + cols : 15 + cols]
        extra[16] = source[8]
        extra[17] = source[8 + cols - 2]
        extra[18] = source[8 + cols - 1]
        sources.append(np.concatenate([source[8 : 8 + cols], extra]))
        starts.append(np.concatenate([start[8 : 8 + cols], start[:8], start[8 + cols :]]))
    return np.stack(sources).astype(np.float32), np.stack(starts).astype(np.float32)


def place(axis):
    at, count = lax.axis_index(axis), lax.axis_size(axis)
    return at, at == 0, at == count - 1


def pick_side(odd, even_ref, odd_ref):
    def before(*where):
        return jnp.where(odd, even_ref[where], odd_ref[where])

    def after(*where):
        return jnp.where(odd, odd_ref[where], even_ref[where])

    return before, after


def pack_kernel(*refs):
    args, outs, held, sem = refs[:5], refs[5:10], refs[10:15], refs[15]
    copies = [pltpu.make_async_copy(src, dst, sem.at[i]) for i, (src, dst) in enumerate(zip(args, held))]
    for copy in copies:
        copy.start()
    load_ref, rc_ref, vc_ref, vm_ref, rr_ref = held
    lf_ref, h_ref, via_ref, a_ref, b_ref = outs
    scen, rows, cols = load_ref.shape
    at, first, _ = place("gx")
    even = lax.rem(at, 2) == 0
    for copy in copies:
        copy.wait()
    for s in range(scen):
        lf_ref[pl.ds(s, rows, stride=scen), :] = load_ref[s].astype(F32)
    row = lax.broadcasted_iota(jnp.int32, (rows, cols), 0)
    h = jnp.where(jnp.logical_and(first, row == 0), 0.0, rc_ref[...])
    via = vm_ref[...].astype(F32) * vc_ref[...]
    h_ref[...] = h
    via_ref[...] = via

    def put(where, top, bottom):
        a_ref[where, :] = jnp.where(even, bottom, top)
        b_ref[where, :] = jnp.where(even, top, bottom)

    n = HALO * scen
    put(pl.ds(0, n), lf_ref[0:n, :], lf_ref[rows * scen - n :, :])
    put(pl.ds(n, SLOT), h[:SLOT], h[rows - SLOT :])
    put(pl.ds(n + SLOT, SLOT), via[:SLOT], via[rows - SLOT :])
    put(pl.ds(n + 2 * SLOT, 8), rr_ref[:8, :], rr_ref[rows - 8 :, :])


def packer(scen, cols):
    lane = lax.broadcasted_iota(jnp.int32, (scen, cols), 1)
    is_flux = jnp.logical_or(
        jnp.logical_and(lane >= 1, lane <= 6), jnp.logical_and(lane >= cols - 7, lane <= cols - 3)
    )
    is_t = jnp.logical_or(lane == 0, lane == cols - 2)
    is_end = lane == cols - 1
    is_rolled = jnp.logical_and(lane >= 8, lane <= 11)

    def pack(tl, q, jl, fl, p, grid_row):
        moved = jl if p is None else jnp.where(is_end, p, jl)
        rolled = pltpu.roll(moved, 10, 1)
        return jnp.where(
            is_flux, fl, jnp.where(is_t, tl, jnp.where(is_end, q, jnp.where(is_rolled, rolled, grid_row)))
        )

    def add_p(w, p):
        return jnp.where(lane == 9, pltpu.roll(p, 10, 1), w)

    return pack, add_p


def lower_row(v, via, minus_inv, vs, cols):
    q = via * v
    tl = q * minus_inv
    dl = pltpu.roll(tl, 1, 1) - tl
    jl = vs * dl
    return q, tl, dl, jl, jl - pltpu.roll(jl, cols - 1, 1)


def core_kernel(
    scen, lf_ref, h_ref, via_ref, cc_ref, pm_ref, cr_ref, pick_ref,
    fl_ref, acc_ref, edge_ref, low_ref, strip_ref, res_ref,
    inv_s, low_s, w_s,
):
    rows, cols = h_ref.shape
    _, first_y, last_y = place("gy")
    lane = lax.broadcasted_iota(jnp.int32, (rows, cols), 1)
    h, via = h_ref[...], via_ref[...]
    inv_s[...] = 1.0 / (h + pltpu.roll(h, rows - 1, 0) + via + LEAK)

    tie_low = via + pm_ref[...].astype(F32) * PAD + LEAK
    vs = jnp.where(jnp.logical_and(first_y, lane == 0), 0.0, cc_ref[...])
    open_end = jnp.logical_and(jnp.logical_not(last_y), lane == cols - 1)
    vs_next = jnp.where(lane == cols - 1, 0.0, pltpu.roll(vs, cols - 1, 1))
    diag_low = vs + vs_next + tie_low
    low_s[0] = jnp.where(open_end, 0.0, -1.0 / diag_low)
    low_s[1] = tie_low
    low_s[2] = jnp.where(jnp.logical_or(open_end, lane == 0), 0.0, vs)
    low_s[3] = jnp.where(
        lane == 12,
        pltpu.roll(vs, 12, 1),
        jnp.where(
            lane == 13,
            pltpu.roll(diag_low, 14, 1),
            jnp.where(lane == 14, pltpu.roll(tie_low, 15, 1), pltpu.roll(vs, 16, 1)),
        ),
    )
    low_ref[...] = jnp.concatenate([low_s[k, rows - 1 : rows, :] for k in range(4)] * 2, 0)
    pack, _ = packer(scen, cols)

    def bc(ref, r):
        return jnp.broadcast_to(ref[pl.ds(r, 1), :], (scen, cols))

    def low(k, r):
        return jnp.broadcast_to(low_s[k, pl.ds(r, 1), :], (scen, cols))

    def keep(i, x):
        edge_ref[pl.ds(i * scen, scen), :] = x

    zero = jnp.zeros((scen, cols), F32)
    g0 = g1 = g2 = g3 = zero
    v0 = hv0 = t0 = None
    last = rows - 1
    for r in range(rows):
        v1 = hv1 = dv1 = None
        if r < last:
            load = lf_ref[pl.ds(r * scen, scen), :]
            v1 = load * bc(inv_s, r)
            g0 += load * v1
            g1 += (bc(via_ref, r) + LEAK) * v1 * v1
            if r > 0:
                dv1 = v0 - v1
                hv1 = bc(h_ref, r) * dv1
                g1 += hv1 * dv1
        if r > 0:
            m = r - 1
            via_m = bc(via_ref, m)
            tie = via_m + LEAK
            q, tl, dl, jl, fl = lower_row(v0, via_m, low(0, m), low(2, m), cols)
            fl_ref[pl.ds(m * scen, scen), :] = fl
            g2 -= q * tl
            g3 += low(1, m) * tl * tl + jl * dl
            p = t1 = None
            if 0 < m < last - 1:
                q_up = tie * v0 - hv0 + hv1
                t1 = q_up * bc(inv_s, m)
                p = via_m * t1
                g2 += q_up * t1
                g3 += tie * t1 * t1 - 2.0 * p * tl
                if m > 1:
                    dt = t0 - t1
                    g3 += bc(h_ref, m) * dt * dt
            w = pack(tl, q, jl, fl, p, low(3, m))
            w_s[pl.ds(m * scen, scen), :] = w
            if m == 0:
                keep(0, v0)
                keep(1, hv1)
                keep(3, tl)
                keep(8, w)
            if m == 1:
                keep(2, t1)
            if m == last - 2:
                keep(6, t1)
            if m == last - 1:
                keep(4, v0)
                keep(5, hv0)
                keep(7, tl)
                keep(9, w)
            t0 = t1
        v0, hv0 = v1, hv1

    size = rows * scen
    fl_ref[pl.ds(last * scen, scen), :] = zero
    w_s[pl.ds(last * scen, scen), :] = zero
    w_s[pl.ds(size, rows), :] = cr_ref[...]
    w_s[size + rows :, :] = jnp.zeros((w_s.shape[0] - size - rows, cols), F32)
    for k, g in enumerate((g0, g1, g2, g3)):
        acc_ref[pl.ds(k * scen, scen), :] = g
    picked = dot_nt(pick_ref[...], w_s[...])
    for k in range(size // cols):
        strip_ref[pl.ds(k * PICKED, PICKED), :] = picked[:PICKED, k * cols : (k + 1) * cols]
    res_ref[...] = picked[PICKED + 8 :, size : size + cols]


def join_kernel(
    scen, lf_ref, h_ref, via_ref, acc_ref, edge_ref, low_ref, strip_ref, res_ref, a_ref, b_ref, pick_ref,
    pair_ref, plain_ref, seam_ref, fl_ref,
    w_s,
):
    rows, cols = h_ref.shape
    odd_x = lax.rem(lax.axis_index("gx"), 2) == 1
    even_y = lax.rem(lax.axis_index("gy"), 2) == 0
    before, after = pick_side(odd_x, a_ref, b_ref)
    n = HALO * scen
    last = rows - 1

    def grid(h, via):
        tie = via + LEAK
        inv = 1.0 / (h + pltpu.roll(h, 15, 0) + tie)

        def row(x, i):
            return jnp.broadcast_to(x[i : i + 1], (scen, cols))

        return (lambda i: row(h, i)), (lambda i: row(tie, i)), (lambda i: row(inv, i)), (lambda i: row(via, i))

    def edge(i):
        return edge_ref[pl.ds(i * scen, scen), :]

    pack, add_p = packer(scen, cols)

    h, tie, inv, via = grid(
        jnp.concatenate([before(pl.ds(n + SLOT - 8, 8)), h_ref[:8, :]], 0),
        jnp.concatenate([before(pl.ds(n + 2 * SLOT - 8, 8)), via_ref[:8, :]], 0),
    )
    v0, hv1, t1, tl0 = (edge(i) for i in range(4))
    far, near = before(pl.ds(n - 2 * scen, scen)) * inv(6), before(pl.ds(n - scen, scen)) * inv(7)
    dv0 = near - v0
    hv0 = h(8) * dv0
    t_near = (tie(7) * near - h(7) * (far - near) + hv0) * inv(7)
    q_up = tie(8) * v0 - hv0 + hv1
    t0 = q_up * inv(8)
    d0, d1 = t_near - t0, t0 - t1
    p = via(8) * t0
    g1 = hv0 * dv0
    g2 = q_up * t0
    g3 = tie(8) * t0 * t0 + h(8) * d0 * d0 + h(9) * d1 * d1 - 2.0 * p * tl0
    w_first = add_p(edge(8), p)

    h, tie, inv, via = grid(
        jnp.concatenate([h_ref[rows - 8 :, :], after(pl.ds(n, 8))], 0),
        jnp.concatenate([via_ref[rows - 8 :, :], after(pl.ds(n + SLOT, 8))], 0),
    )
    v0, hv0, t0, tl0 = (edge(i) for i in range(4, 8))
    load = lf_ref[pl.ds(last * scen, scen), :]
    v1 = load * inv(7)
    v2 = after(pl.ds(0, scen)) * inv(8)
    dv1 = v0 - v1
    hv1, hv2 = h(7) * dv1, h(8) * (v1 - v2)
    q0 = tie(6) * v0 - hv0 + hv1
    q1 = tie(7) * v1 - hv1 + hv2
    t1 = q0 * inv(6)
    t2 = q1 * inv(7)
    d1, d2 = t0 - t1, t1 - t2
    p0, p1 = via(6) * t1, via(7) * t2
    g0 = load * v1
    g1 += hv1 * dv1 + tie(7) * v1 * v1
    g2 += q0 * t1 + q1 * t2
    g3 += tie(6) * t1 * t1 + tie(7) * t2 * t2 + h(6) * d1 * d1 + h(7) * d2 * d2 - 2.0 * p0 * tl0

    def low(k):
        return jnp.broadcast_to(low_ref[pl.ds(k, 1), :], (scen, cols))

    q, tl, dl, jl, fl = lower_row(v1, via(7), low(0), low(2), cols)
    fl_ref[...] = fl
    g2 -= q * tl
    g3 += tl * (low(1) * tl - 2.0 * p1) + jl * dl

    w_s[...] = jnp.zeros_like(w_s)
    w_s[0:scen, :] = w_first
    for k, g in enumerate((g0, g1, g2, g3)):
        w_s[pl.ds((k + 1) * scen, scen), :] = acc_ref[pl.ds(k * scen, scen), :] + g
    w_s[cols - 2 * scen : cols - scen, :] = add_p(edge(9), p0)
    w_s[cols - scen :, :] = pack(tl, q, jl, fl, p1, low(3))
    fresh = dot_nt(pick_ref[: PICKED + 8, :], w_s[...])

    lane = lax.broadcasted_iota(jnp.int32, (PICKED, cols), 1)
    parts = rows * scen // cols
    base = parts * 8 + 8
    for k in range(parts):
        strip = strip_ref[pl.ds(k * PICKED, PICKED), :]
        if k == 0:
            strip = jnp.where(lane < scen, fresh[:PICKED], strip)
        if k == parts - 1:
            strip = jnp.where(lane >= cols - 2 * scen, fresh[:PICKED], strip)
        firsts, lasts = strip[8:16], strip[16:24]
        for ref in (pair_ref, plain_ref, seam_ref):
            ref[pl.ds(k * 8, 8), :] = strip[:8]
        pair_ref[pl.ds(base + k * 8, 8), :] = jnp.where(even_y, lasts, firsts)
        seam_ref[pl.ds(base + k * 8, 8), :] = jnp.where(even_y, firsts, lasts)
    for ref in (pair_ref, plain_ref, seam_ref):
        ref[pl.ds(parts * 8, 8), :] = fresh[PICKED:]
    pair_ref[pl.ds(base + parts * 8, 8), :] = jnp.where(even_y, res_ref[8:, :], res_ref[:8, :])
    seam_ref[pl.ds(base + parts * 8, 8), :] = jnp.where(even_y, res_ref[:8, :], res_ref[8:, :])


def across(ref, start, parts):
    return jnp.concatenate([ref[pl.ds(start + 8 * k, 8), :] for k in range(parts)], 1)


def merge_kernel(scen, parts, axis, step, radix, *refs):
    in_refs, held_refs, out_refs = refs[:radix], refs[radix:-2], refs[-2:]
    if not held_refs:
        in_refs, out_refs = refs[:radix], refs[radix:]
    cols = in_refs[0].shape[1]
    at = lax.rem(lax.div(lax.axis_index(axis), step), radix)
    given = [across(ref, 0, parts) for ref in in_refs]
    blocks = []
    for j in range(radix):
        block = given[0]
        for k in range(1, radix):
            block = jnp.where(jnp.bitwise_xor(at, k) == j, given[k], block)
        blocks.append(block)
    i2 = i3 = 0.0
    for left, right in zip(blocks, blocks[1:]):
        t_next, vs_next = right[0:1], right[1:2]
        q, d, tie, p, vs, t_in = (left[i : i + 1] for i in range(2, 8))
        t = -q / (d + vs_next)
        d_in, d_out = t_in - t, t - t_next
        i2 = i2 - q * t
        i3 = i3 + t * (tie * t - 2.0 * p) + vs * d_in * d_in + vs_next * d_out * d_out
    both = jnp.concatenate([i2, i3], 0)
    both = sum(both[:, k * cols : (k + 1) * cols] for k in range(parts))
    shift = scen
    while shift < cols:
        both = both + pltpu.roll(both, shift, 1)
        shift *= 2
    group = lax.div(lax.broadcasted_iota(jnp.int32, (8, cols), 1), scen)
    sums = jnp.where(group == 3, both[0:1], jnp.where(group == 4, both[1:2], 0.0))
    sum_at = pl.ds(parts * 8, 8)
    for ref in in_refs:
        sums = sums + ref[sum_at, :]
    if not held_refs:
        out_refs[0][...] = sums
        return
    row = lax.broadcasted_iota(jnp.int32, (8, cols), 0)
    for ref in out_refs:
        for k in range(parts):
            where = slice(k * cols, (k + 1) * cols)
            ref[pl.ds(k * 8, 8), :] = jnp.where(row < 2, blocks[0][:, where], blocks[-1][:, where])
        ref[sum_at, :] = sums
    base = parts * 8 + 8
    out_refs[1][base:, :] = held_refs[0][base:, :]


def row_kernel(
    scen, lf_ref, h_ref, via_ref, rr_ref, a_ref, b_ref,
    v_ref, t_ref, gv_ref, gt_ref, br_ref,
    inv_s, h_s, tie_s, fv_s, ft_s, sv_s, st_s, s0_s,
):
    rows, cols = h_ref.shape
    at_x, first, last = place("gx")
    before, after = pick_side(lax.rem(at_x, 2) == 1, a_ref, b_ref)
    n = HALO * scen
    at = pl.ds(n, SLOT)
    h = jnp.concatenate([before(at), h_ref[...], after(at)], 0)
    at = pl.ds(n + SLOT, SLOT)
    tie = jnp.concatenate([before(at), via_ref[...], after(at)], 0) + LEAK
    h_s[...] = h
    tie_s[...] = tie
    inv_s[...] = 1.0 / (h + pltpu.roll(h, h.shape[0] - 1, 0) + tie)

    def load(r):
        if r < 0:
            return before(pl.ds((r + HALO) * scen, scen))
        if r >= rows:
            return after(pl.ds((r - rows) * scen, scen))
        return lf_ref[pl.ds(r * scen, scen), :]

    def bc(ref, r):
        return jnp.broadcast_to(ref[pl.ds(r + SLOT, 1), :], (scen, cols))

    v0 = hv0 = t0 = ht0 = None
    for r in range(-HALO, rows + HALO):
        v1 = load(r) * bc(inv_s, r)
        hv1 = None
        if r > -HALO:
            hv1 = bc(h_s, r) * (v0 - v1)
        if r > 1 - HALO:
            m = r - 1
            fv = hv0 - hv1
            t1 = (bc(tie_s, m) * v0 - fv) * bc(inv_s, m)
            ht1 = None
            if m > 1 - HALO:
                ht1 = bc(h_s, m) * (t0 - t1)
                if m > 2 - HALO:
                    ft = ht0 - ht1
                    at = pl.ds((m - 1 + STEPS - 1) * scen, scen)
                    ft_s[at, :] = ft
                    st_s[at, :] = ft
                if m < rows + STEPS - 1:
                    at = pl.ds((m + STEPS - 1) * scen, scen)
                    fv_s[at, :] = fv
                    sv_s[at, :] = fv
            if 0 <= m < rows:
                v_ref[pl.ds(m, scen, stride=rows), :] = v0
                t_ref[pl.ds(m, scen, stride=rows), :] = t1
            t0, ht0 = t1, ht1
        v0, hv0 = v1, hv1

    n += 2 * SLOT
    count = rows + 2 * (STEPS - 1)
    rate_first = jnp.where(first, 0.0, RELAX)
    rate_last = jnp.where(last, 0.0, RELAX)

    def rate(r):
        return rate_first if r == 0 else rate_last if r == rows else RELAX

    size = rows + 16
    row = lax.broadcasted_iota(jnp.int32, (size, cols), 0)
    rates = jnp.where(row == 8, rate_first, jnp.where(row == 8 + rows, rate_last, RELAX))
    s0_s[...] = jnp.concatenate([before(pl.ds(n, 8)), rr_ref[...], after(pl.ds(n, 8))], 0)

    def start_step():
        now = s0_s[...]
        flux = rates * (pltpu.roll(now, 1, 0) - now)
        return now + flux - pltpu.roll(flux, size - 1, 0)

    def one(_, carry):
        s0_s[...] = start_step()
        for f_ref, s_ref in ((fv_s, sv_s), (ft_s, st_s)):
            here = s_ref[pl.ds(0, scen), :]
            flux = jnp.zeros_like(here)
            for i in range(count):
                r = i - (STEPS - 1)
                at = pl.ds(i * scen, scen)
                if i + 1 < count:
                    following = s_ref[pl.ds((i + 1) * scen, scen), :]
                    flux_next = rate(r + 1) * (here - following)
                else:
                    following, flux_next = here, jnp.zeros_like(here)
                s_ref[at, :] = here + (flux - flux_next) + f_ref[at, :]
                here, flux = following, flux_next
        return carry

    lax.fori_loop(0, STEPS - 1, one, 0)
    br_ref[...] = start_step()[8 : 8 + rows]
    gain = RELAX * DRIVE
    for m in range(rows):
        at = pl.ds((m + STEPS - 1) * scen, scen)
        gv_ref[pl.ds(m, scen, stride=rows), :] = gain * sv_s[at, :]
        gt_ref[pl.ds(m, scen, stride=rows), :] = gain * st_s[at, :]


def col_kernel(scen, steps, fl_ref, fl_last_ref, cr_ref, own_ref, *rest):
    *got_refs, source_ref, start_ref, gl_ref, bc_ref, out_s = rest
    rows, cols = cr_ref.shape
    parts = rows * scen // cols
    base = parts * 8 + 8
    at, first, last = place("gy")
    kind = first.astype(jnp.int32) + 2 * last.astype(jnp.int32)
    odd = lax.rem(at, 2) == 1

    def contents(ref):
        return across(ref, 0, parts), across(ref, base, parts), ref[pl.ds(base + parts * 8, 8), :]

    paired = contents(got_refs[0])
    met = tuple(jnp.zeros_like(x) for x in paired)
    for mask, ref in zip(steps[1:], got_refs[1:]):
        here = jnp.abs(jnp.bitwise_xor(at, mask) - at) == 1
        met = tuple(jnp.where(here, x, y) for x, y in zip(contents(ref), met))
    sums_before, before, res_before = (jnp.where(odd, x, y) for x, y in zip(paired, met))
    sums_after, after, res_after = (jnp.where(odd, y, x) for x, y in zip(paired, met))
    own = across(own_ref, 0, parts)

    def seam(left, right):
        q, d, _, _, vs, t_in = (left[i : i + 1] for i in range(2, 8))
        t_next, vs_next = right[0:1], right[1:2]
        diag = d + vs_next
        t = -q / jnp.where(diag > 0, diag, 1.0)
        return vs * (t_in - t), vs_next * (t - t_next)

    jl_last, jl_0 = seam(sums_before, own)
    jr_last, jr_0 = seam(own, sums_after)
    jr_last = jnp.where(last, 0.0, jr_last)
    jr_0 = jnp.where(last, 0.0, jr_0)
    zero = jnp.zeros_like(jl_0)
    strip = jnp.concatenate(
        [
            before[1:6],
            before[0:1] - jl_last,
            jl_last - jl_0,
            zero,
            jr_0 - after[0:1],
            after[1:7],
            zero,
            jl_0,
            -jr_last,
            jr_last - jr_0,
            zero,
            zero,
            zero,
            zero,
            zero,
        ],
        0,
    )
    source = source_ref[kind]
    edge = dot_tn(strip, source[cols:])
    done = (rows - 1) * scen
    out_s[0:done, :] = dot_nn(fl_ref[0:done, :], source[:cols]) + edge[:done]
    out_s[done:, :] = dot_nn(fl_last_ref[...], source[:cols]) + edge[done:]
    for m in range(rows):
        gl_ref[pl.ds(m, scen, stride=rows), :] = out_s[pl.ds(m * scen, scen), :]
    start = start_ref[kind]
    edge = dot_tn(jnp.concatenate([res_before, res_after], 0), start[cols:])
    bc_ref[...] = dot_nn(cr_ref[...], start[:cols]) + edge[:rows]


def final_kernel(scen, rows, v_ref, t_ref, gv_ref, gt_ref, gl_ref, br_ref, bc_ref, *rest):
    *sum_refs, up_ref, row_ref, col_ref = rest
    cols = v_ref.shape[1]
    sums = sum(ref[...] for ref in sum_refs)
    g0, g1, g2, g3 = (pltpu.roll(sums, cols - (k + 1) * scen, 1) for k in range(4))
    alpha = g0 / g1
    rz = alpha * alpha * g2 - g0
    grow = alpha * g2 / g1
    beta_alpha = rz / (alpha * alpha * (g3 - g2 * g2 / g1))
    c0 = alpha + beta_alpha * grow
    c1 = -alpha * beta_alpha
    lane = lax.broadcasted_iota(jnp.int32, (scen, cols), 1)
    sub = lax.broadcasted_iota(jnp.int32, (scen, cols), 0)

    def column(c):
        tall = jnp.concatenate([c] * (scen // 8), 0)
        return jnp.sum(jnp.where(lane == sub, tall, 0.0), 1, keepdims=True)

    c0, c1 = column(c0), column(c1)
    br, bc = br_ref[...], bc_ref[...]
    for s in range(scen):
        at = pl.ds(s * rows, rows)
        a = jnp.broadcast_to(c0[s : s + 1], (rows, cols))
        b = jnp.broadcast_to(c1[s : s + 1], (rows, cols))
        up_ref[s] = a * v_ref[at, :] + b * t_ref[at, :]
        row_ref[s] = br + a * gv_ref[at, :] + b * gt_ref[at, :]
        col_ref[s] = bc + b * gl_ref[at, :]


def swap(block, axis, mask):
    count = lax.axis_size(axis)
    return lax.ppermute(block, axis, [(i, i ^ mask) for i in range(count)])


def exchange(even_side, odd_side, axis):
    count = lax.axis_size(axis)

    def pairs(start):
        return [(i + a, i + 1 - a) for i in range(start, count - 1, 2) for a in (0, 1)]

    second = lax.ppermute(odd_side, axis, pairs(1))
    return lax.ppermute(even_side, axis, pairs(0)), second


def call(kernel, out, scratch, cost, *args, space=pltpu.VMEM):
    return pl.pallas_call(
        kernel,
        out_shape=out,
        in_specs=[pl.BlockSpec(memory_space=space)] * len(args),
        out_specs=jax.tree.map(lambda _: pl.BlockSpec(memory_space=pltpu.VMEM), out),
        scratch_shapes=scratch,
        compiler_params=pltpu.CompilerParams(vmem_limit_bytes=24 * 2**20),
        cost_estimate=pl.CostEstimate(flops=cost, bytes_accessed=0, transcendentals=0),
    )(*args)


def on_device(
    load_current, row_conductance, col_conductance, via_conductance, pad_mask, via_mask, row_residual, col_residual
):
    scen, rows, cols = load_current.shape
    size = rows * scen
    parts = size // cols

    def f32(*shape):
        return jax.ShapeDtypeStruct(shape, F32)

    def vmem(*shape):
        return pltpu.VMEM(shape, F32)

    pick = jnp.asarray(picker(cols))
    source, start = (jnp.asarray(m) for m in spread(cols))
    grid, field = f32(rows, cols), f32(size, cols)

    wide = f32(HALO * scen + 2 * SLOT + 8, cols)
    sources = (load_current, row_conductance, via_conductance, via_mask, row_residual)
    lf, h, via, x_a, x_b = call(
        pack_kernel,
        (field, grid, grid, wide, wide),
        [pltpu.VMEM(x.shape, x.dtype) for x in sources] + [pltpu.SemaphoreType.DMA((len(sources),))],
        10**5,
        *(pltpu.with_memory_space_constraint(x, pltpu.HBM) for x in sources),
        space=pltpu.HBM,
    )
    x_a, x_b = exchange(x_a, x_b, "gx")

    fl, acc, edge, low, strip, res = call(
        functools.partial(core_kernel, scen),
        (field, f32(4 * scen, cols), f32(10 * scen, cols), f32(8, cols), f32(parts * PICKED, cols), f32(16, cols)),
        [vmem(rows, cols), vmem(4, rows, cols), vmem(size + cols * (-(-rows // cols)), cols)],
        10**7,
        lf, h, via, col_conductance, pad_mask, col_residual, pick,
    )
    x_a, x_b, acc = lax.optimization_barrier((x_a, x_b, acc))

    plain_shape, full_shape = f32(parts * 8 + 8, cols), f32(parts * 16 + 16, cols)
    pair, plain, seam, fl_last = call(
        functools.partial(join_kernel, scen),
        (full_shape, plain_shape, full_shape, f32(scen, cols)),
        [vmem(cols, cols)],
        10**6,
        lf, h, via, acc, edge, low, strip, res, x_a, x_b, pick,
    )

    ext = rows + 2 * SLOT
    reach = (rows + 2 * (STEPS - 1)) * scen
    v, t, gv, gt, br = call(
        functools.partial(row_kernel, scen),
        (field, field, field, field, grid),
        [vmem(ext, cols)] * 3 + [vmem(reach, cols)] * 4 + [vmem(rows + 16, cols)],
        10**7,
        lf, h, via, row_residual, x_a, x_b,
    )

    own, masks, received = pair, [], []
    step, count = 1, lax.axis_size("gy")
    while step < count:
        radix = 4 if 4 * step <= count else 2
        got = []
        for k in range(1, radix):
            mask = k * step + step - 1
            whole = k % 2 == 1
            got.append(swap((pair if mask == 1 else seam) if whole else plain, "gy", mask))
            if whole:
                masks.append(mask)
                received.append(got[-1])
        if step * radix == count:
            *got, br = lax.optimization_barrier((*got, br))
        merge = functools.partial(merge_kernel, scen, parts, "gy", step, radix)
        if step * radix < count:
            plain, seam = call(merge, (plain_shape, full_shape), [], 10**5, plain, *got, seam)
        else:
            sums = call(merge, f32(8, cols), [], 10**5, plain, *got)
        step *= radix

    gl, bc = call(
        functools.partial(col_kernel, scen, masks),
        (field, grid),
        [vmem(size, cols)],
        10**7,
        fl, fl_last, col_residual, own, *received, source, start,
    )

    step, others = 1, []
    while step < lax.axis_size("gx"):
        radix = 4 if 4 * step <= lax.axis_size("gx") else 2
        sums = sum(others, sums)
        others = [swap(sums, "gx", step * k) for k in range(1, radix)]
        if step == 1:
            *others, bc = lax.optimization_barrier((*others, bc))
        step *= radix

    shape = f32(scen, rows, cols)
    return call(
        functools.partial(final_kernel, scen, rows),
        (shape, shape, shape),
        [],
        10**6,
        v, t, gv, gt, gl, br, bc, sums, *others,
    )


def solution(mesh):
    field = P(None, ("grp", "gx"), "gy")
    grid = P(("grp", "gx"), "gy")
    return jax.shard_map(
        on_device,
        mesh=mesh,
        in_specs=(field,) + (grid,) * 7,
        out_specs=(field,) * 3,
        check_vma=False,
    )
```

```python
import functools

import jax
import jax.numpy as jnp
import numpy as np
from jax import lax
from jax.experimental import pallas as pl
from jax.experimental.pallas import tpu as pltpu
from jax.sharding import PartitionSpec as P

STEPS = 8
RELAX = 0.45
DRIVE = 4.0
PAD = 20.0
LEAK = 0.05

F32 = jnp.float32
HALO = STEPS + 1
SLOT = 16

SUM_LANES = [0, 12, -1, 13, 14, 9, 15, -2]
FIRST_LANES = [11, 1, 2, 3, 4, 5, 6]
LAST_LANES = [8, -7, -6, -5, -4, -3]
PICKED = 8 + 8 + 8


def dot_nt(a, b):
    return lax.dot_general(
        a, b, (((1,), (1,)), ((), ())), precision=lax.Precision.HIGHEST, preferred_element_type=F32
    )


def dot_nn(a, b):
    return lax.dot_general(
        a, b, (((1,), (0,)), ((), ())), precision=lax.Precision.HIGHEST, preferred_element_type=F32
    )


def dot_tn(a, b):
    return lax.dot_general(
        a, b, (((0,), (0,)), ((), ())), precision=lax.Precision.HIGHEST, preferred_element_type=F32
    )


def picker(cols):
    e = np.zeros((PICKED + 8 + 16, cols), np.float32)
    for base, lanes in ((0, SUM_LANES), (8, FIRST_LANES), (16, LAST_LANES)):
        for i, lane in enumerate(lanes):
            e[base + i, lane % cols] = 1
    e[PICKED : PICKED + 8] = 1
    for i in range(8):
        e[PICKED + 8 + i, i] = 1
        e[PICKED + 16 + i, cols - 8 + i] = 1
    return e


def spread(cols):
    size = cols + 16
    sources, starts = [], []
    for first, last in ((0, 0), (1, 0), (0, 1), (1, 1)):
        rate = np.full(size + 1, RELAX)
        rate[0] = rate[size] = 0
        if first:
            rate[8] = 0
        if last:
            rate[8 + cols] = 0
        step = np.eye(size)
        for i in range(size):
            step[i, i] -= rate[i] + rate[i + 1]
            if i:
                step[i, i - 1] += rate[i]
            if i + 1 < size:
                step[i, i + 1] += rate[i + 1]
        power, total = np.eye(size), np.zeros((size, size))
        for _ in range(STEPS):
            total += power
            power = step @ power
        source = (RELAX * DRIVE * total)[8 : 8 + cols].T
        start = power[8 : 8 + cols].T
        extra = np.zeros((24, cols))
        extra[0:7] = source[1:8]
        extra[8:15] = source[8 + cols : 15 + cols]
        extra[16] = source[8]
        extra[17] = source[8 + cols - 2]
        extra[18] = source[8 + cols - 1]
        sources.append(np.concatenate([source[8 : 8 + cols], extra]))
        starts.append(np.concatenate([start[8 : 8 + cols], start[:8], start[8 + cols :]]))
    return np.stack(sources).astype(np.float32), np.stack(starts).astype(np.float32)


def place(axis):
    at, count = lax.axis_index(axis), lax.axis_size(axis)
    return at, at == 0, at == count - 1


def sides(axis, even_ref, odd_ref):
    at, first, last = place(axis)
    odd = lax.rem(at, 2) == 1

    def before(*where):
        return jnp.where(odd, even_ref[where], jnp.where(first, 0.0, odd_ref[where]))

    def after(*where):
        return jnp.where(odd, jnp.where(last, 0.0, odd_ref[where]), even_ref[where])

    return before, after


def pack_kernel(*refs):
    args, outs, held, sem = refs[:5], refs[5:10], refs[10:15], refs[15]
    copies = [pltpu.make_async_copy(src, dst, sem.at[i]) for i, (src, dst) in enumerate(zip(args, held))]
    for copy in copies:
        copy.start()
    load_ref, rc_ref, vc_ref, vm_ref, rr_ref = held
    lf_ref, h_ref, via_ref, a_ref, b_ref = outs
    scen, rows, cols = load_ref.shape
    at, first, _ = place("gx")
    even = lax.rem(at, 2) == 0
    for copy in copies:
        copy.wait()
    for s in range(scen):
        lf_ref[pl.ds(s, rows, stride=scen), :] = load_ref[s].astype(F32)
    row = lax.broadcasted_iota(jnp.int32, (rows, cols), 0)
    h = jnp.where(jnp.logical_and(first, row == 0), 0.0, rc_ref[...])
    via = vm_ref[...].astype(F32) * vc_ref[...]
    h_ref[...] = h
    via_ref[...] = via

    def put(where, top, bottom):
        a_ref[where, :] = jnp.where(even, bottom, top)
        b_ref[where, :] = jnp.where(even, top, bottom)

    n = HALO * scen
    put(pl.ds(0, n), lf_ref[0:n, :], lf_ref[rows * scen - n :, :])
    put(pl.ds(n, SLOT), h[:SLOT], h[rows - SLOT :])
    put(pl.ds(n + SLOT, SLOT), via[:SLOT], via[rows - SLOT :])
    put(pl.ds(n + 2 * SLOT, 8), rr_ref[:8, :], rr_ref[rows - 8 :, :])


def packer(scen, cols):
    lane = lax.broadcasted_iota(jnp.int32, (scen, cols), 1)
    is_flux = jnp.logical_or(
        jnp.logical_and(lane >= 1, lane <= 6), jnp.logical_and(lane >= cols - 7, lane <= cols - 3)
    )
    is_t = jnp.logical_or(lane == 0, lane == cols - 2)
    is_end = lane == cols - 1
    is_rolled = jnp.logical_and(lane >= 8, lane <= 11)

    def pack(tl, q, jl, fl, p, grid_row):
        moved = jl if p is None else jnp.where(is_end, p, jl)
        rolled = pltpu.roll(moved, 10, 1)
        return jnp.where(
            is_flux, fl, jnp.where(is_t, tl, jnp.where(is_end, q, jnp.where(is_rolled, rolled, grid_row)))
        )

    def add_p(w, p):
        return jnp.where(lane == 9, pltpu.roll(p, 10, 1), w)

    return pack, add_p


def lower_row(v, via, minus_inv, vs, cols):
    q = via * v
    tl = q * minus_inv
    dl = pltpu.roll(tl, 1, 1) - tl
    jl = vs * dl
    return q, tl, dl, jl, jl - pltpu.roll(jl, cols - 1, 1)


def core_kernel(
    scen, lf_ref, h_ref, via_ref, cc_ref, pm_ref, cr_ref, pick_ref,
    fl_ref, acc_ref, edge_ref, low_ref, strip_ref, res_ref,
    inv_s, low_s, w_s,
):
    rows, cols = h_ref.shape
    _, first_y, last_y = place("gy")
    lane = lax.broadcasted_iota(jnp.int32, (rows, cols), 1)
    h, via = h_ref[...], via_ref[...]
    inv_s[...] = 1.0 / (h + pltpu.roll(h, rows - 1, 0) + via + LEAK)

    tie_low = via + pm_ref[...].astype(F32) * PAD + LEAK
    vs = jnp.where(jnp.logical_and(first_y, lane == 0), 0.0, cc_ref[...])
    open_end = jnp.logical_and(jnp.logical_not(last_y), lane == cols - 1)
    vs_next = jnp.where(lane == cols - 1, 0.0, pltpu.roll(vs, cols - 1, 1))
    diag_low = vs + vs_next + tie_low
    low_s[0] = jnp.where(open_end, 0.0, -1.0 / diag_low)
    low_s[1] = tie_low
    low_s[2] = jnp.where(jnp.logical_or(open_end, lane == 0), 0.0, vs)
    low_s[3] = jnp.where(
        lane == 12,
        pltpu.roll(vs, 12, 1),
        jnp.where(
            lane == 13,
            pltpu.roll(diag_low, 14, 1),
            jnp.where(lane == 14, pltpu.roll(tie_low, 15, 1), pltpu.roll(vs, 16, 1)),
        ),
    )
    low_ref[...] = jnp.concatenate([low_s[k, rows - 1 : rows, :] for k in range(4)] * 2, 0)
    pack, _ = packer(scen, cols)

    def bc(ref, r):
        return jnp.broadcast_to(ref[pl.ds(r, 1), :], (scen, cols))

    def low(k, r):
        return jnp.broadcast_to(low_s[k, pl.ds(r, 1), :], (scen, cols))

    def keep(i, x):
        edge_ref[pl.ds(i * scen, scen), :] = x

    zero = jnp.zeros((scen, cols), F32)
    g0 = g1 = g2 = g3 = zero
    v0 = hv0 = t0 = None
    last = rows - 1
    for r in range(rows):
        v1 = hv1 = dv1 = None
        if r < last:
            load = lf_ref[pl.ds(r * scen, scen), :]
            v1 = load * bc(inv_s, r)
            g0 += load * v1
            g1 += (bc(via_ref, r) + LEAK) * v1 * v1
            if r > 0:
                dv1 = v0 - v1
                hv1 = bc(h_ref, r) * dv1
                g1 += hv1 * dv1
        if r > 0:
            m = r - 1
            via_m = bc(via_ref, m)
            tie = via_m + LEAK
            q, tl, dl, jl, fl = lower_row(v0, via_m, low(0, m), low(2, m), cols)
            fl_ref[pl.ds(m * scen, scen), :] = fl
            g2 -= q * tl
            g3 += low(1, m) * tl * tl + jl * dl
            p = t1 = None
            if 0 < m < last - 1:
                q_up = tie * v0 - hv0 + hv1
                t1 = q_up * bc(inv_s, m)
                p = via_m * t1
                g2 += q_up * t1
                g3 += tie * t1 * t1 - 2.0 * p * tl
                if m > 1:
                    dt = t0 - t1
                    g3 += bc(h_ref, m) * dt * dt
            w = pack(tl, q, jl, fl, p, low(3, m))
            w_s[pl.ds(m * scen, scen), :] = w
            if m == 0:
                keep(0, v0)
                keep(1, hv1)
                keep(3, tl)
                keep(8, w)
            if m == 1:
                keep(2, t1)
            if m == last - 2:
                keep(6, t1)
            if m == last - 1:
                keep(4, v0)
                keep(5, hv0)
                keep(7, tl)
                keep(9, w)
            t0 = t1
        v0, hv0 = v1, hv1

    size = rows * scen
    fl_ref[pl.ds(last * scen, scen), :] = zero
    w_s[pl.ds(last * scen, scen), :] = zero
    w_s[pl.ds(size, rows), :] = cr_ref[...]
    w_s[size + rows :, :] = jnp.zeros((w_s.shape[0] - size - rows, cols), F32)
    for k, g in enumerate((g0, g1, g2, g3)):
        acc_ref[pl.ds(k * scen, scen), :] = g
    picked = dot_nt(pick_ref[...], w_s[...])
    for k in range(size // cols):
        strip_ref[pl.ds(k * PICKED, PICKED), :] = picked[:PICKED, k * cols : (k + 1) * cols]
    res_ref[...] = picked[PICKED + 8 :, size : size + cols]


def join_kernel(
    scen, lf_ref, h_ref, via_ref, acc_ref, edge_ref, low_ref, strip_ref, res_ref, a_ref, b_ref, pick_ref,
    pair_ref, plain_ref, seam_ref, fl_ref,
    w_s,
):
    rows, cols = h_ref.shape
    even_y = lax.rem(lax.axis_index("gy"), 2) == 0
    before, after = sides("gx", a_ref, b_ref)
    n = HALO * scen
    last = rows - 1

    def grid(h, via):
        tie = via + LEAK
        inv = 1.0 / (h + pltpu.roll(h, 15, 0) + tie)

        def row(x, i):
            return jnp.broadcast_to(x[i : i + 1], (scen, cols))

        return (lambda i: row(h, i)), (lambda i: row(tie, i)), (lambda i: row(inv, i)), (lambda i: row(via, i))

    def edge(i):
        return edge_ref[pl.ds(i * scen, scen), :]

    pack, add_p = packer(scen, cols)

    h, tie, inv, via = grid(
        jnp.concatenate([before(pl.ds(n + SLOT - 8, 8)), h_ref[:8, :]], 0),
        jnp.concatenate([before(pl.ds(n + 2 * SLOT - 8, 8)), via_ref[:8, :]], 0),
    )
    v0, hv1, t1, tl0 = (edge(i) for i in range(4))
    far, near = before(pl.ds(n - 2 * scen, scen)) * inv(6), before(pl.ds(n - scen, scen)) * inv(7)
    dv0 = near - v0
    hv0 = h(8) * dv0
    t_near = (tie(7) * near - h(7) * (far - near) + hv0) * inv(7)
    q_up = tie(8) * v0 - hv0 + hv1
    t0 = q_up * inv(8)
    d0, d1 = t_near - t0, t0 - t1
    p = via(8) * t0
    g1 = hv0 * dv0
    g2 = q_up * t0
    g3 = tie(8) * t0 * t0 + h(8) * d0 * d0 + h(9) * d1 * d1 - 2.0 * p * tl0
    w_first = add_p(edge(8), p)

    h, tie, inv, via = grid(
        jnp.concatenate([h_ref[rows - 8 :, :], after(pl.ds(n, 8))], 0),
        jnp.concatenate([via_ref[rows - 8 :, :], after(pl.ds(n + SLOT, 8))], 0),
    )
    v0, hv0, t0, tl0 = (edge(i) for i in range(4, 8))
    load = lf_ref[pl.ds(last * scen, scen), :]
    v1 = load * inv(7)
    v2 = after(pl.ds(0, scen)) * inv(8)
    dv1 = v0 - v1
    hv1, hv2 = h(7) * dv1, h(8) * (v1 - v2)
    q0 = tie(6) * v0 - hv0 + hv1
    q1 = tie(7) * v1 - hv1 + hv2
    t1 = q0 * inv(6)
    t2 = q1 * inv(7)
    d1, d2 = t0 - t1, t1 - t2
    p0, p1 = via(6) * t1, via(7) * t2
    g0 = load * v1
    g1 += hv1 * dv1 + tie(7) * v1 * v1
    g2 += q0 * t1 + q1 * t2
    g3 += tie(6) * t1 * t1 + tie(7) * t2 * t2 + h(6) * d1 * d1 + h(7) * d2 * d2 - 2.0 * p0 * tl0

    def low(k):
        return jnp.broadcast_to(low_ref[pl.ds(k, 1), :], (scen, cols))

    q, tl, dl, jl, fl = lower_row(v1, via(7), low(0), low(2), cols)
    fl_ref[...] = fl
    g2 -= q * tl
    g3 += tl * (low(1) * tl - 2.0 * p1) + jl * dl

    w_s[...] = jnp.zeros_like(w_s)
    w_s[0:scen, :] = w_first
    for k, g in enumerate((g0, g1, g2, g3)):
        w_s[pl.ds((k + 1) * scen, scen), :] = acc_ref[pl.ds(k * scen, scen), :] + g
    w_s[cols - 2 * scen : cols - scen, :] = add_p(edge(9), p0)
    w_s[cols - scen :, :] = pack(tl, q, jl, fl, p1, low(3))
    fresh = dot_nt(pick_ref[: PICKED + 8, :], w_s[...])

    lane = lax.broadcasted_iota(jnp.int32, (PICKED, cols), 1)
    parts = rows * scen // cols
    base = parts * 8 + 8
    for k in range(parts):
        strip = strip_ref[pl.ds(k * PICKED, PICKED), :]
        if k == 0:
            strip = jnp.where(lane < scen, fresh[:PICKED], strip)
        if k == parts - 1:
            strip = jnp.where(lane >= cols - 2 * scen, fresh[:PICKED], strip)
        firsts, lasts = strip[8:16], strip[16:24]
        for ref in (pair_ref, plain_ref, seam_ref):
            ref[pl.ds(k * 8, 8), :] = strip[:8]
        pair_ref[pl.ds(base + k * 8, 8), :] = jnp.where(even_y, lasts, firsts)
        seam_ref[pl.ds(base + k * 8, 8), :] = jnp.where(even_y, firsts, lasts)
    for ref in (pair_ref, plain_ref, seam_ref):
        ref[pl.ds(parts * 8, 8), :] = fresh[PICKED:]
    pair_ref[pl.ds(base + parts * 8, 8), :] = jnp.where(even_y, res_ref[8:, :], res_ref[:8, :])
    seam_ref[pl.ds(base + parts * 8, 8), :] = jnp.where(even_y, res_ref[:8, :], res_ref[8:, :])


def across(ref, start, parts):
    return jnp.concatenate([ref[pl.ds(start + 8 * k, 8), :] for k in range(parts)], 1)


def merge_kernel(scen, parts, axis, step, radix, *refs):
    in_refs, held_refs, out_refs = refs[:radix], refs[radix:-2], refs[-2:]
    if not held_refs:
        in_refs, out_refs = refs[:radix], refs[radix:]
    cols = in_refs[0].shape[1]
    at = lax.rem(lax.div(lax.axis_index(axis), step), radix)
    given = [across(ref, 0, parts) for ref in in_refs]
    blocks = []
    for j in range(radix):
        block = given[0]
        for k in range(1, radix):
            block = jnp.where(jnp.bitwise_xor(at, k) == j, given[k], block)
        blocks.append(block)
    i2 = i3 = 0.0
    for left, right in zip(blocks, blocks[1:]):
        t_next, vs_next = right[0:1], right[1:2]
        q, d, tie, p, vs, t_in = (left[i : i + 1] for i in range(2, 8))
        t = -q / (d + vs_next)
        d_in, d_out = t_in - t, t - t_next
        i2 = i2 - q * t
        i3 = i3 + t * (tie * t - 2.0 * p) + vs * d_in * d_in + vs_next * d_out * d_out
    both = jnp.concatenate([i2, i3], 0)
    both = sum(both[:, k * cols : (k + 1) * cols] for k in range(parts))
    shift = scen
    while shift < cols:
        both = both + pltpu.roll(both, shift, 1)
        shift *= 2
    group = lax.div(lax.broadcasted_iota(jnp.int32, (8, cols), 1), scen)
    sums = jnp.where(group == 3, both[0:1], jnp.where(group == 4, both[1:2], 0.0))
    sum_at = pl.ds(parts * 8, 8)
    for ref in in_refs:
        sums = sums + ref[sum_at, :]
    if not held_refs:
        out_refs[0][...] = sums
        return
    row = lax.broadcasted_iota(jnp.int32, (8, cols), 0)
    for ref in out_refs:
        for k in range(parts):
            where = slice(k * cols, (k + 1) * cols)
            ref[pl.ds(k * 8, 8), :] = jnp.where(row < 2, blocks[0][:, where], blocks[-1][:, where])
        ref[sum_at, :] = sums
    base = parts * 8 + 8
    out_refs[1][base:, :] = held_refs[0][base:, :]


def row_kernel(
    scen, lf_ref, h_ref, via_ref, rr_ref, a_ref, b_ref,
    v_ref, t_ref, gv_ref, gt_ref, br_ref,
    inv_s, h_s, tie_s, fv_s, ft_s, sv_s, st_s, s0_s,
):
    rows, cols = h_ref.shape
    _, first, last = place("gx")
    before, after = sides("gx", a_ref, b_ref)
    n = HALO * scen
    at = pl.ds(n, SLOT)
    h = jnp.concatenate([before(at), h_ref[...], after(at)], 0)
    at = pl.ds(n + SLOT, SLOT)
    tie = jnp.concatenate([before(at), via_ref[...], after(at)], 0) + LEAK
    h_s[...] = h
    tie_s[...] = tie
    inv_s[...] = 1.0 / (h + pltpu.roll(h, h.shape[0] - 1, 0) + tie)

    def load(r):
        if r < 0:
            return before(pl.ds((r + HALO) * scen, scen))
        if r >= rows:
            return after(pl.ds((r - rows) * scen, scen))
        return lf_ref[pl.ds(r * scen, scen), :]

    def bc(ref, r):
        return jnp.broadcast_to(ref[pl.ds(r + SLOT, 1), :], (scen, cols))

    v0 = hv0 = t0 = ht0 = None
    for r in range(-HALO, rows + HALO):
        v1 = load(r) * bc(inv_s, r)
        hv1 = None
        if r > -HALO:
            hv1 = bc(h_s, r) * (v0 - v1)
        if r > 1 - HALO:
            m = r - 1
            fv = hv0 - hv1
            t1 = (bc(tie_s, m) * v0 - fv) * bc(inv_s, m)
            ht1 = None
            if m > 1 - HALO:
                ht1 = bc(h_s, m) * (t0 - t1)
                if m > 2 - HALO:
                    ft = ht0 - ht1
                    at = pl.ds((m - 1 + STEPS - 1) * scen, scen)
                    ft_s[at, :] = ft
                    st_s[at, :] = ft
                if m < rows + STEPS - 1:
                    at = pl.ds((m + STEPS - 1) * scen, scen)
                    fv_s[at, :] = fv
                    sv_s[at, :] = fv
            if 0 <= m < rows:
                v_ref[pl.ds(m, scen, stride=rows), :] = v0
                t_ref[pl.ds(m, scen, stride=rows), :] = t1
            t0, ht0 = t1, ht1
        v0, hv0 = v1, hv1

    n += 2 * SLOT
    count = rows + 2 * (STEPS - 1)
    rate_first = jnp.where(first, 0.0, RELAX)
    rate_last = jnp.where(last, 0.0, RELAX)

    def rate(r):
        return rate_first if r == 0 else rate_last if r == rows else RELAX

    size = rows + 16
    row = lax.broadcasted_iota(jnp.int32, (size, cols), 0)
    rates = jnp.where(row == 8, rate_first, jnp.where(row == 8 + rows, rate_last, RELAX))
    s0_s[...] = jnp.concatenate([before(pl.ds(n, 8)), rr_ref[...], after(pl.ds(n, 8))], 0)

    def start_step():
        now = s0_s[...]
        flux = rates * (pltpu.roll(now, 1, 0) - now)
        return now + flux - pltpu.roll(flux, size - 1, 0)

    def one(_, carry):
        s0_s[...] = start_step()
        for f_ref, s_ref in ((fv_s, sv_s), (ft_s, st_s)):
            here = s_ref[pl.ds(0, scen), :]
            flux = jnp.zeros_like(here)
            for i in range(count):
                r = i - (STEPS - 1)
                at = pl.ds(i * scen, scen)
                if i + 1 < count:
                    following = s_ref[pl.ds((i + 1) * scen, scen), :]
                    flux_next = rate(r + 1) * (here - following)
                else:
                    following, flux_next = here, jnp.zeros_like(here)
                s_ref[at, :] = here + (flux - flux_next) + f_ref[at, :]
                here, flux = following, flux_next
        return carry

    lax.fori_loop(0, STEPS - 1, one, 0)
    br_ref[...] = start_step()[8 : 8 + rows]
    gain = RELAX * DRIVE
    for m in range(rows):
        at = pl.ds((m + STEPS - 1) * scen, scen)
        gv_ref[pl.ds(m, scen, stride=rows), :] = gain * sv_s[at, :]
        gt_ref[pl.ds(m, scen, stride=rows), :] = gain * st_s[at, :]


def col_kernel(scen, steps, fl_ref, fl_last_ref, cr_ref, own_ref, *rest):
    *got_refs, source_ref, start_ref, gl_ref, bc_ref, out_s = rest
    rows, cols = cr_ref.shape
    parts = rows * scen // cols
    base = parts * 8 + 8
    at, first, last = place("gy")
    kind = first.astype(jnp.int32) + 2 * last.astype(jnp.int32)
    odd = lax.rem(at, 2) == 1

    def contents(ref):
        return across(ref, 0, parts), across(ref, base, parts), ref[pl.ds(base + parts * 8, 8), :]

    paired = contents(got_refs[0])
    met = tuple(jnp.zeros_like(x) for x in paired)
    for mask, ref in zip(steps[1:], got_refs[1:]):
        here = jnp.abs(jnp.bitwise_xor(at, mask) - at) == 1
        met = tuple(jnp.where(here, x, y) for x, y in zip(contents(ref), met))
    sums_before, before, res_before = (jnp.where(odd, x, y) for x, y in zip(paired, met))
    sums_after, after, res_after = (jnp.where(odd, y, x) for x, y in zip(paired, met))
    own = across(own_ref, 0, parts)

    def seam(left, right):
        q, d, _, _, vs, t_in = (left[i : i + 1] for i in range(2, 8))
        t_next, vs_next = right[0:1], right[1:2]
        diag = d + vs_next
        t = -q / jnp.where(diag > 0, diag, 1.0)
        return vs * (t_in - t), vs_next * (t - t_next)

    jl_last, jl_0 = seam(sums_before, own)
    jr_last, jr_0 = seam(own, sums_after)
    jr_last = jnp.where(last, 0.0, jr_last)
    jr_0 = jnp.where(last, 0.0, jr_0)
    zero = jnp.zeros_like(jl_0)
    strip = jnp.concatenate(
        [
            before[1:6],
            before[0:1] - jl_last,
            jl_last - jl_0,
            zero,
            jr_0 - after[0:1],
            after[1:7],
            zero,
            jl_0,
            -jr_last,
            jr_last - jr_0,
            zero,
            zero,
            zero,
            zero,
            zero,
        ],
        0,
    )
    source = source_ref[kind]
    edge = dot_tn(strip, source[cols:])
    done = (rows - 1) * scen
    out_s[0:done, :] = dot_nn(fl_ref[0:done, :], source[:cols]) + edge[:done]
    out_s[done:, :] = dot_nn(fl_last_ref[...], source[:cols]) + edge[done:]
    for m in range(rows):
        gl_ref[pl.ds(m, scen, stride=rows), :] = out_s[pl.ds(m * scen, scen), :]
    start = start_ref[kind]
    edge = dot_tn(jnp.concatenate([res_before, res_after], 0), start[cols:])
    bc_ref[...] = dot_nn(cr_ref[...], start[:cols]) + edge[:rows]


def final_kernel(scen, rows, v_ref, t_ref, gv_ref, gt_ref, gl_ref, br_ref, bc_ref, *rest):
    *sum_refs, up_ref, row_ref, col_ref = rest
    cols = v_ref.shape[1]
    sums = sum(ref[...] for ref in sum_refs)
    g0, g1, g2, g3 = (pltpu.roll(sums, cols - (k + 1) * scen, 1) for k in range(4))
    alpha = g0 / g1
    rz = alpha * alpha * g2 - g0
    grow = alpha * g2 / g1
    beta_alpha = rz / (alpha * alpha * (g3 - g2 * g2 / g1))
    c0 = alpha + beta_alpha * grow
    c1 = -alpha * beta_alpha
    lane = lax.broadcasted_iota(jnp.int32, (scen, cols), 1)
    sub = lax.broadcasted_iota(jnp.int32, (scen, cols), 0)

    def column(c):
        tall = jnp.concatenate([c] * (scen // 8), 0)
        return jnp.sum(jnp.where(lane == sub, tall, 0.0), 1, keepdims=True)

    c0, c1 = column(c0), column(c1)
    br, bc = br_ref[...], bc_ref[...]
    for s in range(scen):
        at = pl.ds(s * rows, rows)
        a = jnp.broadcast_to(c0[s : s + 1], (rows, cols))
        b = jnp.broadcast_to(c1[s : s + 1], (rows, cols))
        up_ref[s] = a * v_ref[at, :] + b * t_ref[at, :]
        row_ref[s] = br + a * gv_ref[at, :] + b * gt_ref[at, :]
        col_ref[s] = bc + b * gl_ref[at, :]


def swap(block, axis, mask):
    count = lax.axis_size(axis)
    return lax.ppermute(block, axis, [(i, i ^ mask) for i in range(count)])


def exchange(even_side, odd_side, axis):
    count = lax.axis_size(axis)

    def pairs(start):
        return [((i + a) % count, (i + 1 - a) % count) for i in range(start, count, 2) for a in (0, 1)]

    second = lax.ppermute(odd_side, axis, pairs(1))
    return lax.ppermute(even_side, axis, pairs(0)), second


def call(kernel, out, scratch, cost, *args, space=pltpu.VMEM):
    return pl.pallas_call(
        kernel,
        out_shape=out,
        in_specs=[pl.BlockSpec(memory_space=space)] * len(args),
        out_specs=jax.tree.map(lambda _: pl.BlockSpec(memory_space=pltpu.VMEM), out),
        scratch_shapes=scratch,
        compiler_params=pltpu.CompilerParams(vmem_limit_bytes=24 * 2**20),
        cost_estimate=pl.CostEstimate(flops=cost, bytes_accessed=0, transcendentals=0),
    )(*args)


def on_device(
    load_current, row_conductance, col_conductance, via_conductance, pad_mask, via_mask, row_residual, col_residual
):
    scen, rows, cols = load_current.shape
    size = rows * scen
    parts = size // cols

    def f32(*shape):
        return jax.ShapeDtypeStruct(shape, F32)

    def vmem(*shape):
        return pltpu.VMEM(shape, F32)

    pick = jnp.asarray(picker(cols))
    source, start = (jnp.asarray(m) for m in spread(cols))
    grid, field = f32(rows, cols), f32(size, cols)

    wide = f32(HALO * scen + 2 * SLOT + 8, cols)
    sources = (load_current, row_conductance, via_conductance, via_mask, row_residual)
    lf, h, via, x_a, x_b = call(
        pack_kernel,
        (field, grid, grid, wide, wide),
        [pltpu.VMEM(x.shape, x.dtype) for x in sources] + [pltpu.SemaphoreType.DMA((len(sources),))],
        10**5,
        *(pltpu.with_memory_space_constraint(x, pltpu.HBM) for x in sources),
        space=pltpu.HBM,
    )
    x_a, x_b = exchange(x_a, x_b, "gx")

    fl, acc, edge, low, strip, res = call(
        functools.partial(core_kernel, scen),
        (field, f32(4 * scen, cols), f32(10 * scen, cols), f32(8, cols), f32(parts * PICKED, cols), f32(16, cols)),
        [vmem(rows, cols), vmem(4, rows, cols), vmem(size + cols * (-(-rows // cols)), cols)],
        10**7,
        lf, h, via, col_conductance, pad_mask, col_residual, pick,
    )
    x_a, x_b, acc = lax.optimization_barrier((x_a, x_b, acc))

    plain_shape, full_shape = f32(parts * 8 + 8, cols), f32(parts * 16 + 16, cols)
    pair, plain, seam, fl_last = call(
        functools.partial(join_kernel, scen),
        (full_shape, plain_shape, full_shape, f32(scen, cols)),
        [vmem(cols, cols)],
        10**6,
        lf, h, via, acc, edge, low, strip, res, x_a, x_b, pick,
    )

    ext = rows + 2 * SLOT
    reach = (rows + 2 * (STEPS - 1)) * scen
    v, t, gv, gt, br = call(
        functools.partial(row_kernel, scen),
        (field, field, field, field, grid),
        [vmem(ext, cols)] * 3 + [vmem(reach, cols)] * 4 + [vmem(rows + 16, cols)],
        10**7,
        lf, h, via, row_residual, x_a, x_b,
    )

    own, masks, received = pair, [], []
    step, count = 1, lax.axis_size("gy")
    while step < count:
        radix = 4 if 4 * step <= count else 2
        got = []
        for k in range(1, radix):
            mask = k * step + step - 1
            whole = k % 2 == 1
            got.append(swap((pair if mask == 1 else seam) if whole else plain, "gy", mask))
            if whole:
                masks.append(mask)
                received.append(got[-1])
        if step * radix == count:
            *got, br = lax.optimization_barrier((*got, br))
        merge = functools.partial(merge_kernel, scen, parts, "gy", step, radix)
        if step * radix < count:
            plain, seam = call(merge, (plain_shape, full_shape), [], 10**5, plain, *got, seam)
        else:
            sums = call(merge, f32(8, cols), [], 10**5, plain, *got)
        step *= radix

    gl, bc = call(
        functools.partial(col_kernel, scen, masks),
        (field, grid),
        [vmem(size, cols)],
        10**7,
        fl, fl_last, col_residual, own, *received, source, start,
    )

    step, others = 1, []
    while step < lax.axis_size("gx"):
        radix = 4 if 4 * step <= lax.axis_size("gx") else 2
        sums = sum(others, sums)
        others = [swap(sums, "gx", step * k) for k in range(1, radix)]
        if step == 1:
            *others, bc = lax.optimization_barrier((*others, bc))
        step *= radix

    shape = f32(scen, rows, cols)
    return call(
        functools.partial(final_kernel, scen, rows),
        (shape, shape, shape),
        [],
        10**6,
        v, t, gv, gt, gl, br, bc, sums, *others,
    )


def solution(mesh):
    field = P(None, ("grp", "gx"), "gy")
    grid = P(("grp", "gx"), "gy")
    return jax.shard_map(
        on_device,
        mesh=mesh,
        in_specs=(field,) + (grid,) * 7,
        out_specs=(field,) * 3,
        check_vma=False,
    )
```

```python
import functools

import jax
import jax.numpy as jnp
import numpy as np
from jax import lax
from jax.experimental import pallas as pl
from jax.experimental.pallas import tpu as pltpu
from jax.sharding import PartitionSpec as P

STEPS = 8
RELAX = 0.45
DRIVE = 4.0
PAD = 20.0
LEAK = 0.05

F32 = jnp.float32
HALO = STEPS + 1
SLOT = 16

SUM_LANES = [-1, 0, 13, 10, 12]
FIRST_LANES = [11, 1, 2, 3, 4, 5, 6]
LAST_LANES = [8, -7, -6, -5, -4, -3, 9, 15]
PICKED = 8 + 8 + 8
USED = 6


def dot_nt(a, b):
    return lax.dot_general(
        a, b, (((1,), (1,)), ((), ())), precision=lax.Precision.HIGHEST, preferred_element_type=F32
    )


def dot_nn(a, b):
    return lax.dot_general(
        a, b, (((1,), (0,)), ((), ())), precision=lax.Precision.HIGHEST, preferred_element_type=F32
    )


def dot_tn(a, b):
    return lax.dot_general(
        a, b, (((0,), (0,)), ((), ())), precision=lax.Precision.HIGHEST, preferred_element_type=F32
    )


def picker(cols):
    e = np.zeros((PICKED + 8 + 16, cols), np.float32)
    for base, lanes in ((0, SUM_LANES), (8, FIRST_LANES), (16, LAST_LANES)):
        for i, lane in enumerate(lanes):
            e[base + i, lane % cols] = 1
    e[PICKED : PICKED + 8] = 1
    for i in range(8):
        e[PICKED + 8 + i, i] = 1
        e[PICKED + 16 + i, cols - 8 + i] = 1
    return e


def spread(cols):
    size = cols + 16
    sources, starts = [], []
    for first, last in ((0, 0), (1, 0), (0, 1), (1, 1)):
        rate = np.full(size + 1, RELAX)
        rate[0] = rate[size] = 0
        if first:
            rate[8] = 0
        if last:
            rate[8 + cols] = 0
        step = np.eye(size)
        for i in range(size):
            step[i, i] -= rate[i] + rate[i + 1]
            if i:
                step[i, i - 1] += rate[i]
            if i + 1 < size:
                step[i, i + 1] += rate[i + 1]
        power, total = np.eye(size), np.zeros((size, size))
        for _ in range(STEPS):
            total += power
            power = step @ power
        source = (RELAX * DRIVE * total)[8 : 8 + cols].T
        start = power[8 : 8 + cols].T
        extra = np.zeros((24, cols))
        extra[0:7] = source[1:8]
        extra[8:15] = source[8 + cols : 15 + cols]
        extra[16] = source[8]
        extra[17] = source[8 + cols - 2]
        extra[18] = source[8 + cols - 1]
        sources.append(np.concatenate([source[8 : 8 + cols], extra]))
        starts.append(np.concatenate([start[8 : 8 + cols], start[:8], start[8 + cols :]]))
    return np.stack(sources).astype(np.float32), np.stack(starts).astype(np.float32)


def taps():
    size = 4 * STEPS + 1
    step = np.eye(size) * (1 - 2 * RELAX) + RELAX * (np.eye(size, k=1) + np.eye(size, k=-1))
    total = sum(np.linalg.matrix_power(step, k) for k in range(STEPS))
    return [float(x) for x in RELAX * DRIVE * total[size // 2, size // 2 : size // 2 + STEPS]]


def place(axis):
    at, count = lax.axis_index(axis), lax.axis_size(axis)
    return at, at == 0, at == count - 1


def sides(axis, even_ref, odd_ref):
    at, first, last = place(axis)
    odd = lax.rem(at, 2) == 1

    def before(*where):
        return jnp.where(odd, even_ref[where], jnp.where(first, 0.0, odd_ref[where]))

    def after(*where):
        return jnp.where(odd, jnp.where(last, 0.0, odd_ref[where]), even_ref[where])

    return before, after


def fetch(args, held, sem):
    copies = [pltpu.make_async_copy(src, dst, sem.at[i]) for i, (src, dst) in enumerate(zip(args, held))]
    for copy in copies:
        copy.start()
    for copy in copies:
        copy.wait()


def edge_kernel(load_ref, rc_ref, vc_ref, vm_ref, rr_ref, out_ref, *scratch):
    *held, lf_s, sem = scratch
    scen, rows, cols = load_ref.shape
    odd = lax.rem(lax.axis_index("gx"), 2) == 1
    part = pl.ds(pl.multiple_of(jnp.where(odd, rows - SLOT, 0), SLOT), SLOT)
    fetch([load_ref.at[:, part], *(ref.at[part] for ref in (rc_ref, vc_ref, vm_ref, rr_ref))], held, sem)
    load_v, rc_v, vc_v, vm_v, rr_v = held
    for s in range(scen):
        lf_s[pl.ds(s, SLOT, stride=scen), :] = load_v[s].astype(F32)
    n = HALO * scen
    out_ref[0:n, :] = jnp.where(odd, lf_s[(SLOT - HALO) * scen :, :], lf_s[0:n, :])
    out_ref[n : n + SLOT, :] = rc_v[...]
    out_ref[n + SLOT : n + 2 * SLOT, :] = vm_v[...].astype(F32) * vc_v[...]
    out_ref[n + 2 * SLOT :, :] = jnp.where(odd, rr_v[SLOT - 8 :, :], rr_v[:8, :])


def pack_kernel(load_ref, rc_ref, vc_ref, vm_ref, rr_ref, lf_ref, h_ref, via_ref, out_ref, *scratch):
    *held, sem = scratch
    fetch([load_ref, rc_ref, vc_ref, vm_ref, rr_ref], held, sem)
    load_v, rc_v, vc_v, vm_v, rr_v = held
    scen, rows, cols = load_ref.shape
    at, first, _ = place("gx")
    even = lax.rem(at, 2) == 0
    for s in range(scen):
        lf_ref[pl.ds(s, rows, stride=scen), :] = load_v[s].astype(F32)
    row = lax.broadcasted_iota(jnp.int32, (rows, cols), 0)
    h = jnp.where(jnp.logical_and(first, row == 0), 0.0, rc_v[...])
    via = vm_v[...].astype(F32) * vc_v[...]
    h_ref[...] = h
    via_ref[...] = via
    n = HALO * scen
    out_ref[0:n, :] = jnp.where(even, lf_ref[rows * scen - n :, :], lf_ref[0:n, :])
    out_ref[n : n + SLOT, :] = jnp.where(even, h[rows - SLOT :], h[:SLOT])
    out_ref[n + SLOT : n + 2 * SLOT, :] = jnp.where(even, via[rows - SLOT :], via[:SLOT])
    out_ref[n + 2 * SLOT :, :] = jnp.where(even, rr_v[rows - 8 :, :], rr_v[:8, :])


def packer(scen, cols):
    lane = lax.broadcasted_iota(jnp.int32, (scen, cols), 1)
    is_flux = jnp.logical_or(
        jnp.logical_and(lane >= 1, lane <= 6), jnp.logical_and(lane >= cols - 7, lane <= cols - 3)
    )
    is_end = lane == cols - 1
    is_rolled = jnp.logical_and(lane >= 8, lane <= 11)

    def pack(q, jl, fl, p, grid_row):
        ends = jl if p is None else jl + p
        return jnp.where(
            is_flux,
            fl,
            jnp.where(
                is_end,
                q,
                jnp.where(lane == 0, pltpu.roll(ends, 1, 1), jnp.where(is_rolled, pltpu.roll(jl, 10, 1), grid_row)),
            ),
        )

    def add_p(w, p):
        return w + jnp.where(lane == 0, pltpu.roll(p, 1, 1), 0.0)

    return pack, add_p


def lower_row(v, via, minus_inv, vs, open_end):
    scen, cols = v.shape
    lane = lax.broadcasted_iota(jnp.int32, (scen, cols), 1)
    q = via * v
    tl = q * minus_inv
    dl = jnp.where(lane == 0, 0.0, pltpu.roll(tl, 1, 1)) - tl
    jl = vs * dl
    inner = jnp.where(jnp.logical_or(lane == 0, jnp.logical_and(open_end, lane == cols - 1)), 0.0, jl)
    return q, tl, dl, jl, inner - pltpu.roll(inner, cols - 1, 1)


def core_kernel(
    scen, lf_ref, h_ref, via_ref, cc_ref, pm_ref, cr_ref, pick_ref,
    fl_ref, acc_ref, edge_ref, low_ref, strip_ref, res_ref,
    inv_s, low_s, w_s,
):
    rows, cols = h_ref.shape
    _, first_y, last_y = place("gy")
    lane = lax.broadcasted_iota(jnp.int32, (rows, cols), 1)
    h, via = h_ref[...], via_ref[...]
    inv_s[...] = 1.0 / (h + pltpu.roll(h, rows - 1, 0) + via + LEAK)

    tie_low = via + pm_ref[...].astype(F32) * PAD + LEAK
    vs = jnp.where(jnp.logical_and(first_y, lane == 0), 0.0, cc_ref[...])
    open_end = jnp.logical_and(jnp.logical_not(last_y), lane == cols - 1)
    vs_next = jnp.where(lane == cols - 1, 0.0, pltpu.roll(vs, cols - 1, 1))
    diag_low = vs + vs_next + tie_low
    low_s[0] = jnp.where(open_end, 0.0, -1.0 / diag_low)
    low_s[1] = tie_low
    low_s[2] = vs
    low_s[3] = jnp.where(
        lane == 12,
        pltpu.roll(vs, 12, 1),
        jnp.where(
            lane == 13,
            pltpu.roll(diag_low, 14, 1),
            pltpu.roll(vs, 16, 1),
        ),
    )
    low_ref[...] = jnp.concatenate([low_s[k, rows - 1 : rows, :] for k in range(4)] * 2, 0)
    pack, _ = packer(scen, cols)

    def bc(ref, r):
        return jnp.broadcast_to(ref[pl.ds(r, 1), :], (scen, cols))

    def low(k, r):
        return jnp.broadcast_to(low_s[k, pl.ds(r, 1), :], (scen, cols))

    def keep(i, x):
        edge_ref[pl.ds(i * scen, scen), :] = x

    zero = jnp.zeros((scen, cols), F32)
    g0 = g1 = g2 = g3 = zero
    v0 = hv0 = t0 = None
    last = rows - 1
    for r in range(rows):
        v1 = hv1 = dv1 = None
        if r < last:
            load = lf_ref[pl.ds(r * scen, scen), :]
            v1 = load * bc(inv_s, r)
            g0 += load * v1
            g1 += (bc(via_ref, r) + LEAK) * v1 * v1
            if r > 0:
                dv1 = v0 - v1
                hv1 = bc(h_ref, r) * dv1
                g1 += hv1 * dv1
        if r > 0:
            m = r - 1
            via_m = bc(via_ref, m)
            tie = via_m + LEAK
            q, tl, dl, jl, fl = lower_row(v0, via_m, low(0, m), low(2, m), jnp.logical_not(last_y))
            fl_ref[pl.ds(m * scen, scen), :] = fl
            g2 -= q * tl
            g3 += low(1, m) * tl * tl + jl * dl
            p = t1 = None
            if 0 < m < last - 1:
                q_up = tie * v0 - hv0 + hv1
                t1 = q_up * bc(inv_s, m)
                p = via_m * t1
                g2 += q_up * t1
                g3 += tie * t1 * t1 - 2.0 * p * tl
                if m > 1:
                    dt = t0 - t1
                    g3 += bc(h_ref, m) * dt * dt
            w = pack(q, jl, fl, p, low(3, m))
            w_s[pl.ds(m * scen, scen), :] = w
            if m == 0:
                keep(0, v0)
                keep(1, hv1)
                keep(3, tl)
                keep(8, w)
            if m == 1:
                keep(2, t1)
            if m == last - 2:
                keep(6, t1)
            if m == last - 1:
                keep(4, v0)
                keep(5, hv0)
                keep(7, tl)
                keep(9, w)
            t0 = t1
        v0, hv0 = v1, hv1

    size = rows * scen
    fl_ref[pl.ds(last * scen, scen), :] = zero
    w_s[pl.ds(last * scen, scen), :] = zero
    w_s[pl.ds(size, rows), :] = cr_ref[...]
    w_s[size + rows :, :] = jnp.zeros((w_s.shape[0] - size - rows, cols), F32)
    for k, g in enumerate((g0, g1, g2, g3)):
        acc_ref[pl.ds(k * scen, scen), :] = g
    picked = dot_nt(pick_ref[...], w_s[...])
    for k in range(size // cols):
        strip_ref[pl.ds(k * PICKED, PICKED), :] = picked[:PICKED, k * cols : (k + 1) * cols]
    res = picked[PICKED + 8 :, size : size + cols]
    per = cols // rows
    group = lax.div(lax.broadcasted_iota(jnp.int32, (1, cols), 1), rows)
    packed = []
    for start in range(0, 16, per):
        line = res[start : start + 1]
        for k in range(1, per):
            line = jnp.where(group == k, pltpu.roll(res[start + k : start + k + 1], k * rows, 1), line)
        packed.append(line)
    res_ref[...] = jnp.concatenate(packed + [jnp.zeros((16 - len(packed), cols), F32)], 0)


def join_kernel(
    scen, lf_ref, h_ref, via_ref, acc_ref, edge_ref, low_ref, strip_ref, res_ref, a_ref, b_ref, pick_ref,
    pair_ref, plain_ref, seam_ref, fl_ref,
    w_s,
):
    rows, cols = h_ref.shape
    at_y, _, last_y = place("gy")
    even_y = lax.rem(at_y, 2) == 0
    before, after = sides("gx", a_ref, b_ref)
    n = HALO * scen
    last = rows - 1

    def grid(h, via):
        tie = via + LEAK
        inv = 1.0 / (h + pltpu.roll(h, 15, 0) + tie)

        def row(x, i):
            return jnp.broadcast_to(x[i : i + 1], (scen, cols))

        return (lambda i: row(h, i)), (lambda i: row(tie, i)), (lambda i: row(inv, i)), (lambda i: row(via, i))

    def edge(i):
        return edge_ref[pl.ds(i * scen, scen), :]

    pack, add_p = packer(scen, cols)

    h, tie, inv, via = grid(
        jnp.concatenate([before(pl.ds(n + SLOT - 8, 8)), h_ref[:8, :]], 0),
        jnp.concatenate([before(pl.ds(n + 2 * SLOT - 8, 8)), via_ref[:8, :]], 0),
    )
    v0, hv1, t1, tl0 = (edge(i) for i in range(4))
    far, near = before(pl.ds(n - 2 * scen, scen)) * inv(6), before(pl.ds(n - scen, scen)) * inv(7)
    dv0 = near - v0
    hv0 = h(8) * dv0
    t_near = (tie(7) * near - h(7) * (far - near) + hv0) * inv(7)
    q_up = tie(8) * v0 - hv0 + hv1
    t0 = q_up * inv(8)
    d0, d1 = t_near - t0, t0 - t1
    p = via(8) * t0
    g1 = hv0 * dv0
    g2 = q_up * t0
    g3 = tie(8) * t0 * t0 + h(8) * d0 * d0 + h(9) * d1 * d1 - 2.0 * p * tl0
    w_first = add_p(edge(8), p)

    h, tie, inv, via = grid(
        jnp.concatenate([h_ref[rows - 8 :, :], after(pl.ds(n, 8))], 0),
        jnp.concatenate([via_ref[rows - 8 :, :], after(pl.ds(n + SLOT, 8))], 0),
    )
    v0, hv0, t0, tl0 = (edge(i) for i in range(4, 8))
    load = lf_ref[pl.ds(last * scen, scen), :]
    v1 = load * inv(7)
    v2 = after(pl.ds(0, scen)) * inv(8)
    dv1 = v0 - v1
    hv1, hv2 = h(7) * dv1, h(8) * (v1 - v2)
    q0 = tie(6) * v0 - hv0 + hv1
    q1 = tie(7) * v1 - hv1 + hv2
    t1 = q0 * inv(6)
    t2 = q1 * inv(7)
    d1, d2 = t0 - t1, t1 - t2
    p0, p1 = via(6) * t1, via(7) * t2
    g0 = load * v1
    g1 += hv1 * dv1 + tie(7) * v1 * v1
    g2 += q0 * t1 + q1 * t2
    g3 += tie(6) * t1 * t1 + tie(7) * t2 * t2 + h(6) * d1 * d1 + h(7) * d2 * d2 - 2.0 * p0 * tl0

    def low(k):
        return jnp.broadcast_to(low_ref[pl.ds(k, 1), :], (scen, cols))

    q, tl, dl, jl, fl = lower_row(v1, via(7), low(0), low(2), jnp.logical_not(last_y))
    fl_ref[...] = fl
    g2 -= q * tl
    g3 += tl * (low(1) * tl - 2.0 * p1) + jl * dl

    w_s[...] = jnp.zeros_like(w_s)
    w_s[0:scen, :] = w_first
    for k, g in enumerate((g0, g1, g2, g3)):
        w_s[pl.ds((k + 1) * scen, scen), :] = acc_ref[pl.ds(k * scen, scen), :] + g
    w_s[cols - 2 * scen : cols - scen, :] = add_p(edge(9), p0)
    w_s[cols - scen :, :] = pack(q, jl, fl, p1, low(3))
    fresh = dot_nt(pick_ref[: PICKED + 8, :], w_s[...])

    lane = lax.broadcasted_iota(jnp.int32, (PICKED, cols), 1)
    parts = rows * scen // cols
    base = parts * USED
    half = 8 * rows // cols
    row = lax.broadcasted_iota(jnp.int32, (8, cols), 0)
    groups, pair_groups, seam_groups = [], [], []
    for k in range(parts):
        strip = strip_ref[pl.ds(k * PICKED, PICKED), :]
        if k == 0:
            strip = jnp.where(lane < scen, fresh[:PICKED], strip)
        if k == parts - 1:
            strip = jnp.where(lane >= cols - 2 * scen, fresh[:PICKED], strip)
        group = strip[:8]
        if k == 0:
            group = jnp.where(row == USED - 1, fresh[PICKED:], group)
        of_pair = of_seam = group
        if 1 <= k <= half:
            firsts, lasts = res_ref[k - 1 : k, :], res_ref[half + k - 1 : half + k, :]
            of_pair = jnp.where(row == USED - 1, jnp.where(even_y, lasts, firsts), group)
            of_seam = jnp.where(row == USED - 1, jnp.where(even_y, firsts, lasts), group)
        groups.append(group)
        pair_groups.append(of_pair)
        seam_groups.append(of_seam)
        firsts, lasts = strip[8:16], strip[16:24]
        pair_ref[pl.ds(base + k * 8, 8), :] = jnp.where(even_y, lasts, firsts)
        seam_ref[pl.ds(base + k * 8, 8), :] = jnp.where(even_y, firsts, lasts)
    pack_rows(pair_ref, pair_groups)
    pack_rows(plain_ref, groups)
    pack_rows(seam_ref, seam_groups)


def pack_rows(ref, groups):
    ref[0 : len(groups) * USED, :] = jnp.concatenate([g[:USED] for g in groups], 0)


def unpack_rows(ref, parts):
    return jnp.concatenate([ref[k * USED : (k + 1) * USED, :] for k in range(parts)], 1)


def across(ref, start, parts):
    return jnp.concatenate([ref[pl.ds(start + 8 * k, 8), :] for k in range(parts)], 1)


def merge_kernel(scen, parts, axis, step, radix, *refs):
    in_refs, held_refs, out_refs = refs[:radix], refs[radix:-2], refs[-2:]
    if not held_refs:
        in_refs, out_refs = refs[:radix], refs[radix:]
    cols = in_refs[0].shape[1]
    at = lax.rem(lax.div(lax.axis_index(axis), step), radix)
    given = [unpack_rows(ref, parts) for ref in in_refs]
    blocks = []
    for j in range(radix):
        block = given[0]
        for k in range(1, radix):
            block = jnp.where(jnp.bitwise_xor(at, k) == j, given[k], block)
        blocks.append(block)
    i2 = i3 = 0.0
    for left, right in zip(blocks, blocks[1:]):
        q, e, d = (left[i : i + 1] for i in range(3))
        jl_next, vs_next = right[3:4], right[4:5]
        r = q / (d + vs_next)
        i2 = i2 + q * r
        i3 = i3 + r * (e - jl_next)
    i3 = i2 + 2.0 * i3
    both = jnp.concatenate([i2, i3], 0)
    both = sum(both[:, k * cols : (k + 1) * cols] for k in range(parts))
    shift = scen
    while shift < cols:
        both = both + pltpu.roll(both, shift, 1)
        shift *= 2
    group = lax.div(lax.broadcasted_iota(jnp.int32, (1, cols), 1), scen)
    sums = jnp.where(group == 3, both[0:1], jnp.where(group == 4, both[1:2], 0.0))
    sums = sum((block[USED - 1 : USED, :cols] for block in given), sums)
    if not held_refs:
        out_refs[0][...] = jnp.broadcast_to(sums, (8, cols))
        return
    row = lax.broadcasted_iota(jnp.int32, (USED, cols), 0)
    held = unpack_rows(held_refs[0], parts)
    groups = []
    for k in range(parts):
        where = slice(k * cols, (k + 1) * cols)
        group = jnp.where(row < 3, blocks[-1][:, where], blocks[0][:, where])
        groups.append(jnp.where(row == USED - 1, sums if k == 0 else held[:, where], group))
    pack_rows(out_refs[0], groups)
    pack_rows(out_refs[1], groups)
    out_refs[1][parts * USED :, :] = held_refs[0][parts * USED :, :]


def row_kernel(
    scen, lf_ref, h_ref, via_ref, rr_ref, a_ref, b_ref,
    v_ref, t_ref, gv_ref, gt_ref, br_ref,
    inv_s, h_s, tie_s, fv_s, ft_s, s0_s,
):
    rows, cols = h_ref.shape
    _, first, last = place("gx")
    before, after = sides("gx", a_ref, b_ref)
    n = HALO * scen
    at = pl.ds(n, SLOT)
    h = jnp.concatenate([before(at), h_ref[...], after(at)], 0)
    at = pl.ds(n + SLOT, SLOT)
    tie = jnp.concatenate([before(at), via_ref[...], after(at)], 0) + LEAK
    h_s[...] = h
    tie_s[...] = tie
    inv_s[...] = 1.0 / (h + pltpu.roll(h, h.shape[0] - 1, 0) + tie)

    def load(r):
        if r < 0:
            return before(pl.ds((r + HALO) * scen, scen))
        if r >= rows:
            return after(pl.ds((r - rows) * scen, scen))
        return lf_ref[pl.ds(r * scen, scen), :]

    def bc(ref, r):
        return jnp.broadcast_to(ref[pl.ds(r + SLOT, 1), :], (scen, cols))

    v0 = hv0 = t0 = ht0 = None
    for r in range(-HALO, rows + HALO):
        v1 = load(r) * bc(inv_s, r)
        hv1 = None
        if r > -HALO:
            hv1 = bc(h_s, r) * (v0 - v1)
        if r > 1 - HALO:
            m = r - 1
            fv = hv0 - hv1
            t1 = (bc(tie_s, m) * v0 - fv) * bc(inv_s, m)
            ht1 = None
            if m > 1 - HALO:
                ht1 = bc(h_s, m) * (t0 - t1)
                if m > 2 - HALO:
                    ft_s[pl.ds((m - 1 + STEPS - 1) * scen, scen), :] = ht0 - ht1
                if m < rows + STEPS - 1:
                    fv_s[pl.ds((m + STEPS - 1) * scen, scen), :] = fv
            if 0 <= m < rows:
                v_ref[pl.ds(m, scen, stride=rows), :] = v0
                t_ref[pl.ds(m, scen, stride=rows), :] = t1
            t0, ht0 = t1, ht1
        v0, hv0 = v1, hv1

    n += 2 * SLOT
    size = rows + 16
    row = lax.broadcasted_iota(jnp.int32, (size, cols), 0)
    closed = jnp.logical_or(jnp.logical_and(first, row == 8), jnp.logical_and(last, row == 8 + rows))
    rates = jnp.where(closed, 0.0, RELAX)
    s0_s[...] = jnp.concatenate([before(pl.ds(n, 8)), rr_ref[...], after(pl.ds(n, 8))], 0)

    def one(_, carry):
        now = s0_s[...]
        flux = rates * (pltpu.roll(now, 1, 0) - now)
        s0_s[...] = now + flux - pltpu.roll(flux, size - 1, 0)
        return carry

    lax.fori_loop(0, STEPS, one, 0)
    br_ref[...] = s0_s[8 : 8 + rows, :]

    weights = taps()
    reach = STEPS - 1
    for f_ref, out_ref in ((fv_s, gv_ref), (ft_s, gt_ref)):

        def at(r):
            return f_ref[pl.ds((r + reach) * scen, scen), :]

        window = {}
        for r in range(-reach, rows + reach):
            if r < 0:
                x = jnp.where(first, at(-1 - r), at(r))
            elif r >= rows:
                x = jnp.where(last, at(2 * rows - 1 - r), at(r))
            else:
                x = at(r)
            window[r] = x
            m = r - reach
            if m >= 0:
                total = weights[0] * window[m]
                for d in range(1, STEPS):
                    total = total + weights[d] * (window[m - d] + window[m + d])
                out_ref[pl.ds(m, scen, stride=rows), :] = total
                del window[m - reach]


def col_kernel(scen, steps, fl_ref, fl_last_ref, cr_ref, pair_ref, seam_ref, *rest):
    *got_refs, source_ref, start_ref, gl_ref, bc_ref, out_s = rest
    rows, cols = cr_ref.shape
    parts = rows * scen // cols
    base = parts * USED
    at, first, last = place("gy")
    kind = first.astype(jnp.int32) + 2 * last.astype(jnp.int32)
    odd = lax.rem(at, 2) == 1

    def contents(ref):
        return unpack_rows(ref, parts), across(ref, base, parts)

    paired = contents(got_refs[0])
    met = tuple(jnp.zeros_like(x) for x in paired)
    for mask, ref in zip(steps[1:], got_refs[1:]):
        here = jnp.abs(jnp.bitwise_xor(at, mask) - at) == 1
        met = tuple(jnp.where(here, x, y) for x, y in zip(contents(ref), met))
    sums_before, before = (jnp.where(odd, x, y) for x, y in zip(paired, met))
    sums_after, after = (jnp.where(odd, y, x) for x, y in zip(paired, met))
    own, own_pair = contents(pair_ref)
    own_last = jnp.where(odd, across(seam_ref, base, parts), own_pair)

    def seam(left, lasts, right):
        q, d = left[0:1], left[2:3]
        u, vs = lasts[6:7], lasts[7:8]
        jl_next, vs_next = right[3:4], right[4:5]
        diag = d + vs_next
        t = -q / jnp.where(diag > 0, diag, 1.0)
        return u - vs * t, vs_next * t + jl_next

    jl_last, jl_0 = seam(sums_before, before, own)
    jr_last, jr_0 = seam(own, own_last, sums_after)
    jr_last = jnp.where(last, 0.0, jr_last)
    jr_0 = jnp.where(last, 0.0, jr_0)
    zero = jnp.zeros_like(jl_0)
    strip = jnp.concatenate(
        [
            before[1:6],
            before[0:1] - jl_last,
            jl_last - jl_0,
            zero,
            jr_0 - after[0:1],
            after[1:7],
            zero,
            jl_0,
            -jr_last,
            jr_last - jr_0,
            zero,
            zero,
            zero,
            zero,
            zero,
        ],
        0,
    )
    source = source_ref[kind]
    edge = dot_tn(strip, source[cols:])
    done = (rows - 1) * scen
    out_s[0:done, :] = dot_nn(fl_ref[0:done, :], source[:cols]) + edge[:done]
    out_s[done:, :] = dot_nn(fl_last_ref[...], source[:cols]) + edge[done:]
    for m in range(rows):
        gl_ref[pl.ds(m, scen, stride=rows), :] = out_s[pl.ds(m * scen, scen), :]
    start = start_ref[kind]
    per = cols // rows
    res = []
    for block in (sums_before, sums_after):
        for k in range(8):
            lanes = block[USED - 1 : USED, (1 + k // per) * cols : (2 + k // per) * cols]
            res.append(lanes if k % per == 0 else pltpu.roll(lanes, cols - k % per * rows, 1))
    edge = dot_tn(jnp.concatenate(res, 0), start[cols:])
    bc_ref[...] = dot_nn(cr_ref[...], start[:cols]) + edge[:rows]


def final_kernel(scen, rows, v_ref, t_ref, gv_ref, gt_ref, gl_ref, br_ref, bc_ref, *rest):
    *sum_refs, up_ref, row_ref, col_ref = rest
    cols = v_ref.shape[1]
    sums = sum(ref[...] for ref in sum_refs)
    g0, g1, g2, g3 = (pltpu.roll(sums, cols - (k + 1) * scen, 1) for k in range(4))
    alpha = g0 / g1
    rz = alpha * alpha * g2 - g0
    grow = alpha * g2 / g1
    beta_alpha = rz / (alpha * alpha * (g3 - g2 * g2 / g1))
    c0 = alpha + beta_alpha * grow
    c1 = -alpha * beta_alpha
    lane = lax.broadcasted_iota(jnp.int32, (scen, cols), 1)
    sub = lax.broadcasted_iota(jnp.int32, (scen, cols), 0)

    def column(c):
        tall = jnp.concatenate([c] * (scen // 8), 0)
        return jnp.sum(jnp.where(lane == sub, tall, 0.0), 1, keepdims=True)

    c0, c1 = column(c0), column(c1)
    br, bc = br_ref[...], bc_ref[...]
    for s in range(scen):
        at = pl.ds(s * rows, rows)
        a = jnp.broadcast_to(c0[s : s + 1], (rows, cols))
        b = jnp.broadcast_to(c1[s : s + 1], (rows, cols))
        up_ref[s] = a * v_ref[at, :] + b * t_ref[at, :]
        row_ref[s] = br + a * gv_ref[at, :] + b * gt_ref[at, :]
        col_ref[s] = bc + b * gl_ref[at, :]


def swap(block, axis, mask):
    count = lax.axis_size(axis)
    return lax.ppermute(block, axis, [(i, i ^ mask) for i in range(count)])


def swap_odd(block, axis, idle):
    count, lines = lax.axis_size(axis), lax.axis_size(idle)
    pairs = []
    for line in range(lines):
        for i in range(count):
            if 0 < i < count - 1:
                partner = line * count + (i + 1 if i % 2 else i - 1)
            elif lines % 2 == 0:
                partner = (line ^ 1) * count + i
            else:
                partner = line * count + count - 1 - i
            pairs.append((line * count + i, partner))
    return lax.ppermute(block, (idle, axis), pairs)


def call(kernel, out, scratch, cost, *args, space=pltpu.VMEM):
    return pl.pallas_call(
        kernel,
        out_shape=out,
        in_specs=[pl.BlockSpec(memory_space=space)] * len(args),
        out_specs=jax.tree.map(lambda _: pl.BlockSpec(memory_space=pltpu.VMEM), out),
        scratch_shapes=scratch,
        compiler_params=pltpu.CompilerParams(vmem_limit_bytes=24 * 2**20),
        cost_estimate=pl.CostEstimate(flops=cost, bytes_accessed=0, transcendentals=0),
    )(*args)


def on_device(
    load_current, row_conductance, col_conductance, via_conductance, pad_mask, via_mask, row_residual, col_residual
):
    scen, rows, cols = load_current.shape
    size = rows * scen
    parts = size // cols

    def f32(*shape):
        return jax.ShapeDtypeStruct(shape, F32)

    def vmem(*shape):
        return pltpu.VMEM(shape, F32)

    pick = jnp.asarray(picker(cols))
    source, start = (jnp.asarray(m) for m in spread(cols))
    grid, field = f32(rows, cols), f32(size, cols)

    wide = f32(HALO * scen + 2 * SLOT + 8, cols)
    sources = (load_current, row_conductance, via_conductance, via_mask, row_residual)
    pinned = [pltpu.with_memory_space_constraint(x, pltpu.HBM) for x in sources]
    sems = pltpu.SemaphoreType.DMA((len(sources),))
    shapes = [(scen, SLOT, cols)] + [(SLOT, cols)] * 4
    odd_strip = call(
        edge_kernel,
        wide,
        [pltpu.VMEM(shape, x.dtype) for shape, x in zip(shapes, sources)] + [vmem(SLOT * scen, cols), sems],
        10**5,
        *pinned,
        space=pltpu.HBM,
    )
    x_b = swap_odd(odd_strip, "gx", "grp")
    lf, h, via, even_strip = call(
        pack_kernel,
        (field, grid, grid, wide),
        [pltpu.VMEM(x.shape, x.dtype) for x in sources] + [sems],
        10**5,
        *pinned,
        space=pltpu.HBM,
    )
    x_a = swap(even_strip, "gx", 1)

    fl, acc, edge, low, strip, res = call(
        functools.partial(core_kernel, scen),
        (field, f32(4 * scen, cols), f32(10 * scen, cols), f32(8, cols), f32(parts * PICKED, cols), f32(16, cols)),
        [vmem(rows, cols), vmem(4, rows, cols), vmem(size + cols * (-(-rows // cols)), cols)],
        10**7,
        lf, h, via, col_conductance, pad_mask, col_residual, pick,
    )
    x_a, x_b, acc = lax.optimization_barrier((x_a, x_b, acc))

    plain_shape, full_shape = f32(parts * USED + 0, cols), f32(parts * (USED + 8) + 0, cols)
    seam_shape = f32(parts * (USED + 8) + 8, cols)
    pair, plain, seam, fl_last = call(
        functools.partial(join_kernel, scen),
        (full_shape, plain_shape, seam_shape, f32(scen, cols)),
        [vmem(cols, cols)],
        10**6,
        lf, h, via, acc, edge, low, strip, res, x_a, x_b, pick,
    )

    ext = rows + 2 * SLOT
    reach = (rows + 2 * (STEPS - 1)) * scen
    v, t, gv, gt, br = call(
        functools.partial(row_kernel, scen),
        (field, field, field, field, grid),
        [vmem(ext, cols)] * 3 + [vmem(reach, cols)] * 2 + [vmem(rows + 16, cols)],
        10**7,
        lf, h, via, row_residual, x_a, x_b,
    )

    own_pair, own_seam, masks, received = pair, seam, [], []
    step, count = 1, lax.axis_size("gy")
    while step < count:
        radix = 4 if 4 * step <= count else 2
        got = []
        for k in range(1, radix):
            mask = k * step + step - 1
            whole = k % 2 == 1
            got.append(swap((pair if mask == 1 else seam) if whole else plain, "gy", mask))
            if whole:
                masks.append(mask)
                received.append(got[-1])
        if step * radix == count:
            *got, br = lax.optimization_barrier((*got, br))
        merge = functools.partial(merge_kernel, scen, parts, "gy", step, radix)
        if step * radix < count:
            plain, seam = call(merge, (plain_shape, seam_shape), [], 10**5, plain, *got, seam)
        else:
            sums = call(merge, f32(8, cols), [], 10**5, plain, *got)
        step *= radix

    gl, bc = call(
        functools.partial(col_kernel, scen, masks),
        (field, grid),
        [vmem(size, cols)],
        10**7,
        fl, fl_last, col_residual, own_pair, own_seam, *received, source, start,
    )

    step, others = 1, []
    while step < lax.axis_size("gx"):
        radix = 4 if 4 * step <= lax.axis_size("gx") else 2
        sums = sum(others, sums)
        others = [swap(sums, "gx", step * k) for k in range(1, radix)]
        if step == 1:
            *others, bc = lax.optimization_barrier((*others, bc))
        step *= radix

    shape = f32(scen, rows, cols)
    return call(
        functools.partial(final_kernel, scen, rows),
        (shape, shape, shape),
        [],
        10**6,
        v, t, gv, gt, gl, br, bc, sums, *others,
    )


def solution(mesh):
    field = P(None, ("grp", "gx"), "gy")
    grid = P(("grp", "gx"), "gy")
    return jax.shard_map(
        on_device,
        mesh=mesh,
        in_specs=(field,) + (grid,) * 7,
        out_specs=(field,) * 3,
        check_vma=False,
    )
```

```python
import functools

import jax
import jax.numpy as jnp
import numpy as np
from jax import lax
from jax.experimental import pallas as pl
from jax.experimental.pallas import tpu as pltpu
from jax.sharding import PartitionSpec as P

STEPS = 8
RELAX = 0.45
DRIVE = 4.0
PAD = 20.0
LEAK = 0.05

F32 = jnp.float32
HALO = STEPS + 1
SLOT = 16

SUM_LANES = [-1, 0, 13, 10, 12]
FIRST_LANES = [11, 1, 2, 3, 4, 5, 6]
LAST_LANES = [8, -7, -6, -5, -4, -3, 9, 15]
PICKED = 8 + 8 + 8
USED = 8


def dot_nt(a, b):
    return lax.dot_general(
        a, b, (((1,), (1,)), ((), ())), precision=lax.Precision.HIGHEST, preferred_element_type=F32
    )


def pick_nt(pick, b):
    out = None
    for _ in range(3):
        part = b.astype(jnp.bfloat16)
        b = b - part.astype(F32)
        term = lax.dot_general(
            pick.astype(jnp.bfloat16), part, (((1,), (1,)), ((), ())), preferred_element_type=F32
        )
        out = term if out is None else out + term
    return out


def dot_nn(a, b):
    return lax.dot_general(
        a, b, (((1,), (0,)), ((), ())), precision=lax.Precision.HIGHEST, preferred_element_type=F32
    )


def dot_tn(a, b):
    return lax.dot_general(
        a, b, (((0,), (0,)), ((), ())), precision=lax.Precision.HIGHEST, preferred_element_type=F32
    )


def picker(cols):
    e = np.zeros((PICKED + 8 + 16, cols), np.float32)
    for base, lanes in ((0, SUM_LANES), (8, FIRST_LANES), (16, LAST_LANES)):
        for i, lane in enumerate(lanes):
            e[base + i, lane % cols] = 1
    e[PICKED : PICKED + 8] = 1
    for i in range(8):
        e[PICKED + 8 + i, i] = 1
        e[PICKED + 16 + i, cols - 8 + i] = 1
    return e


def spread(cols):
    size = cols + 16
    sources, starts = [], []
    for first, last in ((0, 0), (1, 0), (0, 1), (1, 1)):
        rate = np.full(size + 1, RELAX)
        rate[0] = rate[size] = 0
        if first:
            rate[8] = 0
        if last:
            rate[8 + cols] = 0
        step = np.eye(size)
        for i in range(size):
            step[i, i] -= rate[i] + rate[i + 1]
            if i:
                step[i, i - 1] += rate[i]
            if i + 1 < size:
                step[i, i + 1] += rate[i + 1]
        power, total = np.eye(size), np.zeros((size, size))
        for _ in range(STEPS):
            total += power
            power = step @ power
        source = (RELAX * DRIVE * total)[8 : 8 + cols].T
        start = power[8 : 8 + cols].T
        extra = np.zeros((24, cols))
        extra[0:7] = source[1:8]
        extra[8:15] = source[8 + cols : 15 + cols]
        extra[16] = source[8]
        extra[17] = source[8 + cols - 2]
        extra[18] = source[8 + cols - 1]
        sources.append(np.concatenate([source[8 : 8 + cols], extra]))
        starts.append(np.concatenate([start[8 : 8 + cols], start[:8], start[8 + cols :]]))
    return np.stack(sources).astype(np.float32), np.stack(starts).astype(np.float32)


def taps():
    size = 4 * STEPS + 1
    step = np.eye(size) * (1 - 2 * RELAX) + RELAX * (np.eye(size, k=1) + np.eye(size, k=-1))
    total = sum(np.linalg.matrix_power(step, k) for k in range(STEPS))
    return [float(x) for x in RELAX * DRIVE * total[size // 2, size // 2 : size // 2 + STEPS]]


def place(axis):
    at, count = lax.axis_index(axis), lax.axis_size(axis)
    return at, at == 0, at == count - 1


def sides(axis, even_ref, odd_ref):
    at, first, last = place(axis)
    odd = lax.rem(at, 2) == 1

    def before(*where):
        return jnp.where(odd, even_ref[where], jnp.where(first, 0.0, odd_ref[where]))

    def after(*where):
        return jnp.where(odd, jnp.where(last, 0.0, odd_ref[where]), even_ref[where])

    return before, after


def fetch(args, held, sem):
    copies = [pltpu.make_async_copy(src, dst, sem.at[i]) for i, (src, dst) in enumerate(zip(args, held))]
    for copy in copies:
        copy.start()
    for copy in copies:
        copy.wait()


def edge_kernel(load_ref, rc_ref, vc_ref, vm_ref, rr_ref, out_ref, *scratch):
    *held, lf_s, sem = scratch
    scen, rows, cols = load_ref.shape
    odd = lax.rem(lax.axis_index("gx"), 2) == 1
    part = pl.ds(pl.multiple_of(jnp.where(odd, rows - SLOT, 0), SLOT), SLOT)
    fetch([load_ref.at[:, part], *(ref.at[part] for ref in (rc_ref, vc_ref, vm_ref, rr_ref))], held, sem)
    load_v, rc_v, vc_v, vm_v, rr_v = held
    for s in range(scen):
        lf_s[pl.ds(s, SLOT, stride=scen), :] = load_v[s].astype(F32)
    n = HALO * scen
    out_ref[0:n, :] = jnp.where(odd, lf_s[(SLOT - HALO) * scen :, :], lf_s[0:n, :])
    out_ref[n : n + SLOT, :] = rc_v[...]
    out_ref[n + SLOT : n + 2 * SLOT, :] = vm_v[...].astype(F32) * vc_v[...]
    out_ref[n + 2 * SLOT :, :] = jnp.where(odd, rr_v[SLOT - 8 :, :], rr_v[:8, :])


def pack_kernel(load_ref, rc_ref, vc_ref, vm_ref, rr_ref, lf_ref, h_ref, via_ref, out_ref, *scratch):
    *held, sem = scratch
    fetch([load_ref, rc_ref, vc_ref, vm_ref, rr_ref], held, sem)
    load_v, rc_v, vc_v, vm_v, rr_v = held
    scen, rows, cols = load_ref.shape
    at, first, _ = place("gx")
    even = lax.rem(at, 2) == 0
    for s in range(scen):
        lf_ref[pl.ds(s, rows, stride=scen), :] = load_v[s].astype(F32)
    row = lax.broadcasted_iota(jnp.int32, (rows, cols), 0)
    h = jnp.where(jnp.logical_and(first, row == 0), 0.0, rc_v[...])
    via = vm_v[...].astype(F32) * vc_v[...]
    h_ref[...] = h
    via_ref[...] = via
    n = HALO * scen
    out_ref[0:n, :] = jnp.where(even, lf_ref[rows * scen - n :, :], lf_ref[0:n, :])
    out_ref[n : n + SLOT, :] = jnp.where(even, h[rows - SLOT :], h[:SLOT])
    out_ref[n + SLOT : n + 2 * SLOT, :] = jnp.where(even, via[rows - SLOT :], via[:SLOT])
    out_ref[n + 2 * SLOT :, :] = jnp.where(even, rr_v[rows - 8 :, :], rr_v[:8, :])


def packer(scen, cols):
    lane = lax.broadcasted_iota(jnp.int32, (scen, cols), 1)
    is_flux = jnp.logical_or(
        jnp.logical_and(lane >= 1, lane <= 6), jnp.logical_and(lane >= cols - 7, lane <= cols - 3)
    )
    is_end = lane == cols - 1
    is_rolled = jnp.logical_and(lane >= 8, lane <= 11)

    def pack(q, jl, fl, p, grid_row):
        ends = jl if p is None else jl + p
        return jnp.where(
            is_flux,
            fl,
            jnp.where(
                is_end,
                q,
                jnp.where(lane == 0, pltpu.roll(ends, 1, 1), jnp.where(is_rolled, pltpu.roll(jl, 10, 1), grid_row)),
            ),
        )

    def add_p(w, p):
        return w + jnp.where(lane == 0, pltpu.roll(p, 1, 1), 0.0)

    return pack, add_p


def lower_row(v, via, minus_inv, vs, open_end):
    scen, cols = v.shape
    lane = lax.broadcasted_iota(jnp.int32, (scen, cols), 1)
    q = via * v
    tl = q * minus_inv
    dl = jnp.where(lane == 0, 0.0, pltpu.roll(tl, 1, 1)) - tl
    jl = vs * dl
    inner = jnp.where(jnp.logical_or(lane == 0, jnp.logical_and(open_end, lane == cols - 1)), 0.0, jl)
    return q, tl, dl, jl, inner - pltpu.roll(inner, cols - 1, 1)


def core_kernel(
    scen, lf_ref, h_ref, via_ref, cc_ref, pm_ref, cr_ref, pick_ref,
    fl_ref, acc_ref, edge_ref, low_ref, strip_ref, res_ref,
    inv_s, low_s, w_s,
):
    rows, cols = h_ref.shape
    _, first_y, last_y = place("gy")
    lane = lax.broadcasted_iota(jnp.int32, (rows, cols), 1)
    h, via = h_ref[...], via_ref[...]
    inv_s[...] = 1.0 / (h + pltpu.roll(h, rows - 1, 0) + via + LEAK)

    tie_low = via + pm_ref[...].astype(F32) * PAD + LEAK
    vs = jnp.where(jnp.logical_and(first_y, lane == 0), 0.0, cc_ref[...])
    open_end = jnp.logical_and(jnp.logical_not(last_y), lane == cols - 1)
    vs_next = jnp.where(lane == cols - 1, 0.0, pltpu.roll(vs, cols - 1, 1))
    diag_low = vs + vs_next + tie_low
    low_s[0] = jnp.where(open_end, 0.0, -1.0 / diag_low)
    low_s[1] = tie_low
    low_s[2] = vs
    low_s[3] = jnp.where(
        lane == 12,
        pltpu.roll(vs, 12, 1),
        jnp.where(
            lane == 13,
            pltpu.roll(diag_low, 14, 1),
            pltpu.roll(vs, 16, 1),
        ),
    )
    low_ref[...] = jnp.concatenate([low_s[k, rows - 1 : rows, :] for k in range(4)] * 2, 0)
    pack, _ = packer(scen, cols)

    def bc(ref, r):
        return jnp.broadcast_to(ref[pl.ds(r, 1), :], (scen, cols))

    def low(k, r):
        return jnp.broadcast_to(low_s[k, pl.ds(r, 1), :], (scen, cols))

    def keep(i, x):
        edge_ref[pl.ds(i * scen, scen), :] = x

    zero = jnp.zeros((scen, cols), F32)
    g0 = g1 = g2 = g3 = zero
    v0 = hv0 = t0 = None
    last = rows - 1
    for r in range(rows):
        v1 = hv1 = dv1 = None
        if r < last:
            load = lf_ref[pl.ds(r * scen, scen), :]
            v1 = load * bc(inv_s, r)
            g0 += load * v1
            g1 += (bc(via_ref, r) + LEAK) * v1 * v1
            if r > 0:
                dv1 = v0 - v1
                hv1 = bc(h_ref, r) * dv1
                g1 += hv1 * dv1
        if r > 0:
            m = r - 1
            via_m = bc(via_ref, m)
            tie = via_m + LEAK
            q, tl, dl, jl, fl = lower_row(v0, via_m, low(0, m), low(2, m), jnp.logical_not(last_y))
            fl_ref[pl.ds(m * scen, scen), :] = fl
            g2 -= q * tl
            g3 += low(1, m) * tl * tl + jl * dl
            p = t1 = None
            if 0 < m < last - 1:
                q_up = tie * v0 - hv0 + hv1
                t1 = q_up * bc(inv_s, m)
                p = via_m * t1
                g2 += q_up * t1
                g3 += tie * t1 * t1 - 2.0 * p * tl
                if m > 1:
                    dt = t0 - t1
                    g3 += bc(h_ref, m) * dt * dt
            w = pack(q, jl, fl, p, low(3, m))
            w_s[pl.ds(m * scen, scen), :] = w
            if m == 0:
                keep(0, v0)
                keep(1, hv1)
                keep(3, tl)
                keep(8, w)
            if m == 1:
                keep(2, t1)
            if m == last - 2:
                keep(6, t1)
            if m == last - 1:
                keep(4, v0)
                keep(5, hv0)
                keep(7, tl)
                keep(9, w)
            t0 = t1
        v0, hv0 = v1, hv1

    size = rows * scen
    fl_ref[pl.ds(last * scen, scen), :] = zero
    w_s[pl.ds(last * scen, scen), :] = zero
    w_s[pl.ds(size, rows), :] = cr_ref[...]
    w_s[size + rows :, :] = jnp.zeros((w_s.shape[0] - size - rows, cols), F32)
    for k, g in enumerate((g0, g1, g2, g3)):
        acc_ref[pl.ds(k * scen, scen), :] = g
    picked = pick_nt(pick_ref[...], w_s[...])
    for k in range(size // cols):
        strip_ref[pl.ds(k * PICKED, PICKED), :] = picked[:PICKED, k * cols : (k + 1) * cols]
    res = picked[PICKED + 8 :, size : size + cols]
    per = cols // rows
    group = lax.div(lax.broadcasted_iota(jnp.int32, (1, cols), 1), rows)
    packed = []
    for start in range(0, 16, per):
        line = res[start : start + 1]
        for k in range(1, per):
            line = jnp.where(group == k, pltpu.roll(res[start + k : start + k + 1], k * rows, 1), line)
        packed.append(line)
    res_ref[...] = jnp.concatenate(packed + [jnp.zeros((16 - len(packed), cols), F32)], 0)


def join_kernel(
    scen, lf_ref, h_ref, via_ref, acc_ref, edge_ref, low_ref, strip_ref, res_ref, a_ref, b_ref, pick_ref,
    pair_ref, plain_ref, seam_ref, fl_ref,
    w_s,
):
    rows, cols = h_ref.shape
    at_y, _, last_y = place("gy")
    even_y = lax.rem(at_y, 2) == 0
    before, after = sides("gx", a_ref, b_ref)
    n = HALO * scen
    last = rows - 1

    def grid(h, via):
        tie = via + LEAK
        inv = 1.0 / (h + pltpu.roll(h, 15, 0) + tie)

        def row(x, i):
            return jnp.broadcast_to(x[i : i + 1], (scen, cols))

        return (lambda i: row(h, i)), (lambda i: row(tie, i)), (lambda i: row(inv, i)), (lambda i: row(via, i))

    def edge(i):
        return edge_ref[pl.ds(i * scen, scen), :]

    pack, add_p = packer(scen, cols)

    h, tie, inv, via = grid(
        jnp.concatenate([before(pl.ds(n + SLOT - 8, 8)), h_ref[:8, :]], 0),
        jnp.concatenate([before(pl.ds(n + 2 * SLOT - 8, 8)), via_ref[:8, :]], 0),
    )
    v0, hv1, t1, tl0 = (edge(i) for i in range(4))
    far, near = before(pl.ds(n - 2 * scen, scen)) * inv(6), before(pl.ds(n - scen, scen)) * inv(7)
    dv0 = near - v0
    hv0 = h(8) * dv0
    t_near = (tie(7) * near - h(7) * (far - near) + hv0) * inv(7)
    q_up = tie(8) * v0 - hv0 + hv1
    t0 = q_up * inv(8)
    d0, d1 = t_near - t0, t0 - t1
    p = via(8) * t0
    g1 = hv0 * dv0
    g2 = q_up * t0
    g3 = tie(8) * t0 * t0 + h(8) * d0 * d0 + h(9) * d1 * d1 - 2.0 * p * tl0
    w_first = add_p(edge(8), p)

    h, tie, inv, via = grid(
        jnp.concatenate([h_ref[rows - 8 :, :], after(pl.ds(n, 8))], 0),
        jnp.concatenate([via_ref[rows - 8 :, :], after(pl.ds(n + SLOT, 8))], 0),
    )
    v0, hv0, t0, tl0 = (edge(i) for i in range(4, 8))
    load = lf_ref[pl.ds(last * scen, scen), :]
    v1 = load * inv(7)
    v2 = after(pl.ds(0, scen)) * inv(8)
    dv1 = v0 - v1
    hv1, hv2 = h(7) * dv1, h(8) * (v1 - v2)
    q0 = tie(6) * v0 - hv0 + hv1
    q1 = tie(7) * v1 - hv1 + hv2
    t1 = q0 * inv(6)
    t2 = q1 * inv(7)
    d1, d2 = t0 - t1, t1 - t2
    p0, p1 = via(6) * t1, via(7) * t2
    g0 = load * v1
    g1 += hv1 * dv1 + tie(7) * v1 * v1
    g2 += q0 * t1 + q1 * t2
    g3 += tie(6) * t1 * t1 + tie(7) * t2 * t2 + h(6) * d1 * d1 + h(7) * d2 * d2 - 2.0 * p0 * tl0

    def low(k):
        return jnp.broadcast_to(low_ref[pl.ds(k, 1), :], (scen, cols))

    q, tl, dl, jl, fl = lower_row(v1, via(7), low(0), low(2), jnp.logical_not(last_y))
    fl_ref[...] = fl
    g2 -= q * tl
    g3 += tl * (low(1) * tl - 2.0 * p1) + jl * dl

    w_s[...] = jnp.zeros_like(w_s)
    w_s[0:scen, :] = w_first
    for k, g in enumerate((g0, g1, g2, g3)):
        w_s[pl.ds((k + 1) * scen, scen), :] = acc_ref[pl.ds(k * scen, scen), :] + g
    w_s[cols - 2 * scen : cols - scen, :] = add_p(edge(9), p0)
    w_s[cols - scen :, :] = pack(q, jl, fl, p1, low(3))
    fresh = pick_nt(pick_ref[: PICKED + 8, :], w_s[...])

    lane = lax.broadcasted_iota(jnp.int32, (PICKED, cols), 1)
    parts = rows * scen // cols
    base = parts * USED
    half = 8 * rows // cols
    row = lax.broadcasted_iota(jnp.int32, (8, cols), 0)
    groups, pair_groups, seam_groups = [], [], []
    for k in range(parts):
        strip = strip_ref[pl.ds(k * PICKED, PICKED), :]
        if k == 0:
            strip = jnp.where(lane < scen, fresh[:PICKED], strip)
        if k == parts - 1:
            strip = jnp.where(lane >= cols - 2 * scen, fresh[:PICKED], strip)
        group = strip[:8]
        if k == 0:
            group = jnp.where(row == USED - 1, fresh[PICKED:], group)
        of_pair = of_seam = group
        if 1 <= k <= half:
            firsts, lasts = res_ref[k - 1 : k, :], res_ref[half + k - 1 : half + k, :]
            of_pair = jnp.where(row == USED - 1, jnp.where(even_y, lasts, firsts), group)
            of_seam = jnp.where(row == USED - 1, jnp.where(even_y, firsts, lasts), group)
        groups.append(group)
        pair_groups.append(of_pair)
        seam_groups.append(of_seam)
        firsts, lasts = strip[8:16], strip[16:24]
        pair_ref[pl.ds(base + k * 8, 8), :] = jnp.where(even_y, lasts, firsts)
        seam_ref[pl.ds(base + k * 8, 8), :] = jnp.where(even_y, firsts, lasts)
    pack_rows(pair_ref, pair_groups)
    pack_rows(plain_ref, groups)
    pack_rows(seam_ref, seam_groups)


def pack_rows(ref, groups):
    ref[0 : len(groups) * USED, :] = jnp.concatenate([g[:USED] for g in groups], 0)


def unpack_rows(ref, parts):
    return jnp.concatenate([ref[k * USED : (k + 1) * USED, :] for k in range(parts)], 1)


def across(ref, start, parts):
    return jnp.concatenate([ref[pl.ds(start + 8 * k, 8), :] for k in range(parts)], 1)


def merge_kernel(scen, parts, axis, step, radix, *refs):
    in_refs, held_refs, out_refs = refs[:radix], refs[radix:-2], refs[-2:]
    if not held_refs:
        in_refs, out_refs = refs[:radix], refs[radix:]
    cols = in_refs[0].shape[1]
    at = lax.rem(lax.div(lax.axis_index(axis), step), radix)
    given = [unpack_rows(ref, parts) for ref in in_refs]
    blocks = []
    for j in range(radix):
        block = given[0]
        for k in range(1, radix):
            block = jnp.where(jnp.bitwise_xor(at, k) == j, given[k], block)
        blocks.append(block)
    i2 = i3 = 0.0
    for left, right in zip(blocks, blocks[1:]):
        q, e, d = (left[i : i + 1] for i in range(3))
        jl_next, vs_next = right[3:4], right[4:5]
        r = q / (d + vs_next)
        i2 = i2 + q * r
        i3 = i3 + r * (e - jl_next)
    i3 = i2 + 2.0 * i3
    both = jnp.concatenate([i2, i3], 0)
    both = sum(both[:, k * cols : (k + 1) * cols] for k in range(parts))
    shift = scen
    while shift < cols:
        both = both + pltpu.roll(both, shift, 1)
        shift *= 2
    group = lax.div(lax.broadcasted_iota(jnp.int32, (1, cols), 1), scen)
    sums = jnp.where(group == 3, both[0:1], jnp.where(group == 4, both[1:2], 0.0))
    sums = sum((block[USED - 1 : USED, :cols] for block in given), sums)
    if not held_refs:
        out_refs[0][...] = jnp.broadcast_to(sums, (8, cols))
        return
    row = lax.broadcasted_iota(jnp.int32, (USED, cols), 0)
    held = unpack_rows(held_refs[0], parts)
    groups = []
    for k in range(parts):
        where = slice(k * cols, (k + 1) * cols)
        group = jnp.where(row < 3, blocks[-1][:, where], blocks[0][:, where])
        groups.append(jnp.where(row == USED - 1, sums if k == 0 else held[:, where], group))
    pack_rows(out_refs[0], groups)
    pack_rows(out_refs[1], groups)
    out_refs[1][parts * USED :, :] = held_refs[0][parts * USED :, :]


def row_kernel(
    scen, lf_ref, h_ref, via_ref, rr_ref, a_ref, b_ref,
    v_ref, t_ref, gv_ref, gt_ref, br_ref,
    inv_s, h_s, tie_s, fv_s, ft_s, s0_s,
):
    rows, cols = h_ref.shape
    _, first, last = place("gx")
    before, after = sides("gx", a_ref, b_ref)
    n = HALO * scen
    at = pl.ds(n, SLOT)
    h = jnp.concatenate([before(at), h_ref[...], after(at)], 0)
    at = pl.ds(n + SLOT, SLOT)
    tie = jnp.concatenate([before(at), via_ref[...], after(at)], 0) + LEAK
    h_s[...] = h
    tie_s[...] = tie
    inv_s[...] = 1.0 / (h + pltpu.roll(h, h.shape[0] - 1, 0) + tie)

    def load(r):
        if r < 0:
            return before(pl.ds((r + HALO) * scen, scen))
        if r >= rows:
            return after(pl.ds((r - rows) * scen, scen))
        return lf_ref[pl.ds(r * scen, scen), :]

    def bc(ref, r):
        return jnp.broadcast_to(ref[pl.ds(r + SLOT, 1), :], (scen, cols))

    v0 = hv0 = t0 = ht0 = None
    for r in range(-HALO, rows + HALO):
        v1 = load(r) * bc(inv_s, r)
        hv1 = None
        if r > -HALO:
            hv1 = bc(h_s, r) * (v0 - v1)
        if r > 1 - HALO:
            m = r - 1
            fv = hv0 - hv1
            t1 = (bc(tie_s, m) * v0 - fv) * bc(inv_s, m)
            ht1 = None
            if m > 1 - HALO:
                ht1 = bc(h_s, m) * (t0 - t1)
                if m > 2 - HALO:
                    ft_s[pl.ds((m - 1 + STEPS - 1) * scen, scen), :] = ht0 - ht1
                if m < rows + STEPS - 1:
                    fv_s[pl.ds((m + STEPS - 1) * scen, scen), :] = fv
            if 0 <= m < rows:
                v_ref[pl.ds(m, scen, stride=rows), :] = v0
                t_ref[pl.ds(m, scen, stride=rows), :] = t1
            t0, ht0 = t1, ht1
        v0, hv0 = v1, hv1

    n += 2 * SLOT
    size = rows + 16
    row = lax.broadcasted_iota(jnp.int32, (size, cols), 0)
    closed = jnp.logical_or(jnp.logical_and(first, row == 8), jnp.logical_and(last, row == 8 + rows))
    rates = jnp.where(closed, 0.0, RELAX)
    s0_s[...] = jnp.concatenate([before(pl.ds(n, 8)), rr_ref[...], after(pl.ds(n, 8))], 0)

    def one(_, carry):
        now = s0_s[...]
        flux = rates * (pltpu.roll(now, 1, 0) - now)
        s0_s[...] = now + flux - pltpu.roll(flux, size - 1, 0)
        return carry

    lax.fori_loop(0, STEPS, one, 0)
    br_ref[...] = s0_s[8 : 8 + rows, :]

    weights = taps()
    reach = STEPS - 1
    for f_ref, out_ref in ((fv_s, gv_ref), (ft_s, gt_ref)):

        def at(r):
            return f_ref[pl.ds((r + reach) * scen, scen), :]

        window = {}
        for r in range(-reach, rows + reach):
            if r < 0:
                x = jnp.where(first, at(-1 - r), at(r))
            elif r >= rows:
                x = jnp.where(last, at(2 * rows - 1 - r), at(r))
            else:
                x = at(r)
            window[r] = x
            m = r - reach
            if m >= 0:
                total = weights[0] * window[m]
                for d in range(1, STEPS):
                    total = total + weights[d] * (window[m - d] + window[m + d])
                out_ref[pl.ds(m, scen, stride=rows), :] = total
                del window[m - reach]


def col_kernel(scen, steps, fl_ref, fl_last_ref, cr_ref, pair_ref, seam_ref, *rest):
    *got_refs, source_ref, start_ref, gl_ref, bc_ref, out_s = rest
    rows, cols = cr_ref.shape
    parts = rows * scen // cols
    base = parts * USED
    at, first, last = place("gy")
    kind = first.astype(jnp.int32) + 2 * last.astype(jnp.int32)
    odd = lax.rem(at, 2) == 1

    def contents(ref):
        return unpack_rows(ref, parts), across(ref, base, parts)

    paired = contents(got_refs[0])
    met = tuple(jnp.zeros_like(x) for x in paired)
    for mask, ref in zip(steps[1:], got_refs[1:]):
        here = jnp.abs(jnp.bitwise_xor(at, mask) - at) == 1
        met = tuple(jnp.where(here, x, y) for x, y in zip(contents(ref), met))
    sums_before, before = (jnp.where(odd, x, y) for x, y in zip(paired, met))
    sums_after, after = (jnp.where(odd, y, x) for x, y in zip(paired, met))
    own, own_pair = contents(pair_ref)
    own_last = jnp.where(odd, across(seam_ref, base, parts), own_pair)

    def seam(left, lasts, right):
        q, d = left[0:1], left[2:3]
        u, vs = lasts[6:7], lasts[7:8]
        jl_next, vs_next = right[3:4], right[4:5]
        diag = d + vs_next
        t = -q / jnp.where(diag > 0, diag, 1.0)
        return u - vs * t, vs_next * t + jl_next

    jl_last, jl_0 = seam(sums_before, before, own)
    jr_last, jr_0 = seam(own, own_last, sums_after)
    jr_last = jnp.where(last, 0.0, jr_last)
    jr_0 = jnp.where(last, 0.0, jr_0)
    zero = jnp.zeros_like(jl_0)
    strip = jnp.concatenate(
        [
            before[1:6],
            before[0:1] - jl_last,
            jl_last - jl_0,
            zero,
            jr_0 - after[0:1],
            after[1:7],
            zero,
            jl_0,
            -jr_last,
            jr_last - jr_0,
            zero,
            zero,
            zero,
            zero,
            zero,
        ],
        0,
    )
    source = source_ref[kind]
    edge = dot_tn(strip, source[cols:])
    done = (rows - 1) * scen
    out_s[0:done, :] = dot_nn(fl_ref[0:done, :], source[:cols]) + edge[:done]
    out_s[done:, :] = dot_nn(fl_last_ref[...], source[:cols]) + edge[done:]
    for m in range(rows):
        gl_ref[pl.ds(m, scen, stride=rows), :] = out_s[pl.ds(m * scen, scen), :]
    start = start_ref[kind]
    per = cols // rows
    res = []
    for block in (sums_before, sums_after):
        for k in range(8):
            lanes = block[USED - 1 : USED, (1 + k // per) * cols : (2 + k // per) * cols]
            res.append(lanes if k % per == 0 else pltpu.roll(lanes, cols - k % per * rows, 1))
    edge = dot_tn(jnp.concatenate(res, 0), start[cols:])
    bc_ref[...] = dot_nn(cr_ref[...], start[:cols]) + edge[:rows]


def final_kernel(scen, rows, v_ref, t_ref, gv_ref, gt_ref, gl_ref, br_ref, bc_ref, *rest):
    *sum_refs, up_ref, row_ref, col_ref = rest
    cols = v_ref.shape[1]
    sums = sum(ref[...] for ref in sum_refs)
    g0, g1, g2, g3 = (pltpu.roll(sums, cols - (k + 1) * scen, 1) for k in range(4))
    alpha, ratio = g0 / g1, g2 / g1
    c1 = (g1 - alpha * g2) / (g3 - ratio * g2)
    c0 = alpha - ratio * c1
    lane = lax.broadcasted_iota(jnp.int32, (scen, cols), 1)
    sub = lax.broadcasted_iota(jnp.int32, (scen, cols), 0)

    def column(c):
        tall = jnp.concatenate([c] * (scen // 8), 0)
        return jnp.sum(jnp.where(lane == sub, tall, 0.0), 1, keepdims=True)

    c0, c1 = column(c0), column(c1)
    br, bc = br_ref[...], bc_ref[...]
    for s in range(scen):
        at = pl.ds(s * rows, rows)
        a = jnp.broadcast_to(c0[s : s + 1], (rows, cols))
        b = jnp.broadcast_to(c1[s : s + 1], (rows, cols))
        up_ref[s] = a * v_ref[at, :] + b * t_ref[at, :]
        row_ref[s] = br + a * gv_ref[at, :] + b * gt_ref[at, :]
        col_ref[s] = bc + b * gl_ref[at, :]


def swap(block, axis, mask):
    count = lax.axis_size(axis)
    return lax.ppermute(block, axis, [(i, i ^ mask) for i in range(count)])


def swap_odd(block, axis, idle):
    count, lines = lax.axis_size(axis), lax.axis_size(idle)
    pairs = []
    for line in range(lines):
        for i in range(count):
            if 0 < i < count - 1:
                partner = line * count + (i + 1 if i % 2 else i - 1)
            elif lines % 2 == 0:
                partner = (line ^ 1) * count + i
            else:
                partner = line * count + count - 1 - i
            pairs.append((line * count + i, partner))
    return lax.ppermute(block, (idle, axis), pairs)


def call(kernel, out, scratch, cost, *args, space=pltpu.VMEM):
    return pl.pallas_call(
        kernel,
        out_shape=out,
        in_specs=[pl.BlockSpec(memory_space=space)] * len(args),
        out_specs=jax.tree.map(lambda _: pl.BlockSpec(memory_space=pltpu.VMEM), out),
        scratch_shapes=scratch,
        compiler_params=pltpu.CompilerParams(vmem_limit_bytes=24 * 2**20),
        cost_estimate=pl.CostEstimate(flops=cost, bytes_accessed=0, transcendentals=0),
    )(*args)


def on_device(
    load_current, row_conductance, col_conductance, via_conductance, pad_mask, via_mask, row_residual, col_residual
):
    scen, rows, cols = load_current.shape
    size = rows * scen
    parts = size // cols

    def f32(*shape):
        return jax.ShapeDtypeStruct(shape, F32)

    def vmem(*shape):
        return pltpu.VMEM(shape, F32)

    pick = jnp.asarray(picker(cols))
    source, start = (jnp.asarray(m) for m in spread(cols))
    grid, field = f32(rows, cols), f32(size, cols)

    wide = f32(HALO * scen + 2 * SLOT + 8, cols)
    sources = (load_current, row_conductance, via_conductance, via_mask, row_residual)
    pinned = [pltpu.with_memory_space_constraint(x, pltpu.HBM) for x in sources]
    sems = pltpu.SemaphoreType.DMA((len(sources),))
    shapes = [(scen, SLOT, cols)] + [(SLOT, cols)] * 4
    odd_strip = call(
        edge_kernel,
        wide,
        [pltpu.VMEM(shape, x.dtype) for shape, x in zip(shapes, sources)] + [vmem(SLOT * scen, cols), sems],
        10**5,
        *pinned,
        space=pltpu.HBM,
    )
    x_b = swap_odd(odd_strip, "gx", "grp")
    lf, h, via, even_strip = call(
        pack_kernel,
        (field, grid, grid, wide),
        [pltpu.VMEM(x.shape, x.dtype) for x in sources] + [sems],
        10**5,
        *pinned,
        space=pltpu.HBM,
    )
    x_a = swap(even_strip, "gx", 1)

    fl, acc, edge, low, strip, res = call(
        functools.partial(core_kernel, scen),
        (field, f32(4 * scen, cols), f32(10 * scen, cols), f32(8, cols), f32(parts * PICKED, cols), f32(16, cols)),
        [vmem(rows, cols), vmem(4, rows, cols), vmem(size + cols * (-(-rows // cols)), cols)],
        10**7,
        lf, h, via, col_conductance, pad_mask, col_residual, pick,
    )
    x_a, x_b, acc = lax.optimization_barrier((x_a, x_b, acc))

    plain_shape, full_shape = f32(parts * USED + 0, cols), f32(parts * (USED + 8) + 0, cols)
    seam_shape = f32(parts * (USED + 8) + 8, cols)
    pair, plain, seam, fl_last = call(
        functools.partial(join_kernel, scen),
        (full_shape, plain_shape, seam_shape, f32(scen, cols)),
        [vmem(cols, cols)],
        10**6,
        lf, h, via, acc, edge, low, strip, res, x_a, x_b, pick,
    )

    ext = rows + 2 * SLOT
    reach = (rows + 2 * (STEPS - 1)) * scen
    v, t, gv, gt, br = call(
        functools.partial(row_kernel, scen),
        (field, field, field, field, grid),
        [vmem(ext, cols)] * 3 + [vmem(reach, cols)] * 2 + [vmem(rows + 16, cols)],
        10**7,
        lf, h, via, row_residual, x_a, x_b,
    )

    own_pair, own_seam, masks, received = pair, seam, [], []
    step, count = 1, lax.axis_size("gy")
    while step < count:
        radix = 4 if 4 * step <= count else 2
        got = []
        for k in range(1, radix):
            mask = k * step + step - 1
            whole = k % 2 == 1
            got.append(swap((pair if mask == 1 else seam) if whole else plain, "gy", mask))
            if whole:
                masks.append(mask)
                received.append(got[-1])
        if step * radix == count:
            *got, br = lax.optimization_barrier((*got, br))
        merge = functools.partial(merge_kernel, scen, parts, "gy", step, radix)
        if step * radix < count:
            plain, seam = call(merge, (plain_shape, seam_shape), [], 10**5, plain, *got, seam)
        else:
            sums = call(merge, f32(8, cols), [], 10**5, plain, *got)
        step *= radix

    gl, bc = call(
        functools.partial(col_kernel, scen, masks),
        (field, grid),
        [vmem(size, cols)],
        10**7,
        fl, fl_last, col_residual, own_pair, own_seam, *received, source, start,
    )

    step, others = 1, []
    while step < lax.axis_size("gx"):
        radix = 4 if 4 * step <= lax.axis_size("gx") else 2
        sums = sum(others, sums)
        others = [swap(sums, "gx", step * k) for k in range(1, radix)]
        if step == 1:
            *others, bc = lax.optimization_barrier((*others, bc))
        step *= radix

    shape = f32(scen, rows, cols)
    return call(
        functools.partial(final_kernel, scen, rows),
        (shape, shape, shape),
        [],
        10**6,
        v, t, gv, gt, gl, br, bc, sums, *others,
    )


def solution(mesh):
    field = P(None, ("grp", "gx"), "gy")
    grid = P(("grp", "gx"), "gy")
    return jax.shard_map(
        on_device,
        mesh=mesh,
        in_specs=(field,) + (grid,) * 7,
        out_specs=(field,) * 3,
        check_vma=False,
    )
```

```python
import functools

import jax
import jax.numpy as jnp
import numpy as np
from jax import lax
from jax.experimental import pallas as pl
from jax.experimental.pallas import tpu as pltpu
from jax.sharding import PartitionSpec as P

STEPS = 8
RELAX = 0.45
DRIVE = 4.0
PAD = 20.0
LEAK = 0.05

F32 = jnp.float32
HALO = STEPS + 1
SLOT = 16

SUM_LANES = [-1, 0, 13, 10, 12]
FIRST_LANES = [11, 1, 2, 3, 4, 5, 6]
LAST_LANES = [8, -7, -6, -5, -4, -3, 9, 15]
PICKED = 8 + 8 + 8
USED = 8


def dot_nt(a, b):
    return lax.dot_general(
        a, b, (((1,), (1,)), ((), ())), precision=lax.Precision.HIGHEST, preferred_element_type=F32
    )


def pick_nt(pick, b):
    out = None
    for _ in range(3):
        part = b.astype(jnp.bfloat16)
        b = b - part.astype(F32)
        term = lax.dot_general(
            pick.astype(jnp.bfloat16), part, (((1,), (1,)), ((), ())), preferred_element_type=F32
        )
        out = term if out is None else out + term
    return out


def dot_nn(a, b):
    return lax.dot_general(
        a, b, (((1,), (0,)), ((), ())), precision=lax.Precision.HIGHEST, preferred_element_type=F32
    )


def dot_tn(a, b):
    return lax.dot_general(
        a, b, (((0,), (0,)), ((), ())), precision=lax.Precision.HIGHEST, preferred_element_type=F32
    )


def picker(cols):
    e = np.zeros((PICKED + 8 + 16, cols), np.float32)
    for base, lanes in ((0, SUM_LANES), (8, FIRST_LANES), (16, LAST_LANES)):
        for i, lane in enumerate(lanes):
            e[base + i, lane % cols] = 1
    e[PICKED : PICKED + 8] = 1
    for i in range(8):
        e[PICKED + 8 + i, i] = 1
        e[PICKED + 16 + i, cols - 8 + i] = 1
    return e


def spread(cols):
    size = cols + 16
    sources, starts = [], []
    for first, last in ((0, 0), (1, 0), (0, 1), (1, 1)):
        rate = np.full(size + 1, RELAX)
        rate[0] = rate[size] = 0
        if first:
            rate[8] = 0
        if last:
            rate[8 + cols] = 0
        step = np.eye(size)
        for i in range(size):
            step[i, i] -= rate[i] + rate[i + 1]
            if i:
                step[i, i - 1] += rate[i]
            if i + 1 < size:
                step[i, i + 1] += rate[i + 1]
        power, total = np.eye(size), np.zeros((size, size))
        for _ in range(STEPS):
            total += power
            power = step @ power
        source = (RELAX * DRIVE * total)[8 : 8 + cols].T
        start = power[8 : 8 + cols].T
        extra = np.zeros((24, cols))
        extra[0:7] = source[1:8]
        extra[8:15] = source[8 + cols : 15 + cols]
        extra[16] = source[8]
        extra[17] = source[8 + cols - 2]
        extra[18] = source[8 + cols - 1]
        sources.append(np.concatenate([source[8 : 8 + cols], extra]))
        starts.append(np.concatenate([start[8 : 8 + cols], start[:8], start[8 + cols :]]))
    return np.stack(sources).astype(np.float32), np.stack(starts).astype(np.float32)


def taps():
    size = 4 * STEPS + 1
    step = np.eye(size) * (1 - 2 * RELAX) + RELAX * (np.eye(size, k=1) + np.eye(size, k=-1))
    total = sum(np.linalg.matrix_power(step, k) for k in range(STEPS))
    return [float(x) for x in RELAX * DRIVE * total[size // 2, size // 2 : size // 2 + STEPS]]


def place(axis):
    at, count = lax.axis_index(axis), lax.axis_size(axis)
    return at, at == 0, at == count - 1


def sides(axis, even_ref, odd_ref):
    at, first, last = place(axis)
    odd = lax.rem(at, 2) == 1

    def before(*where):
        return jnp.where(odd, even_ref[where], jnp.where(first, 0.0, odd_ref[where]))

    def after(*where):
        return jnp.where(odd, jnp.where(last, 0.0, odd_ref[where]), even_ref[where])

    return before, after


def fetch(args, held, sem):
    copies = [pltpu.make_async_copy(src, dst, sem.at[i]) for i, (src, dst) in enumerate(zip(args, held))]
    for copy in copies:
        copy.start()
    for copy in copies:
        copy.wait()


def edge_kernel(load_ref, rc_ref, vc_ref, vm_ref, rr_ref, out_ref, *scratch):
    *held, lf_s, sem = scratch
    scen, rows, cols = load_ref.shape
    odd = lax.rem(lax.axis_index("gx"), 2) == 1
    part = pl.ds(pl.multiple_of(jnp.where(odd, rows - SLOT, 0), SLOT), SLOT)
    fetch([load_ref.at[:, part], *(ref.at[part] for ref in (rc_ref, vc_ref, vm_ref, rr_ref))], held, sem)
    load_v, rc_v, vc_v, vm_v, rr_v = held
    for s in range(scen):
        lf_s[pl.ds(s, SLOT, stride=scen), :] = load_v[s].astype(F32)
    n = HALO * scen
    out_ref[0:n, :] = jnp.where(odd, lf_s[(SLOT - HALO) * scen :, :], lf_s[0:n, :])
    out_ref[n : n + SLOT, :] = rc_v[...]
    out_ref[n + SLOT : n + 2 * SLOT, :] = vm_v[...].astype(F32) * vc_v[...]
    out_ref[n + 2 * SLOT :, :] = jnp.where(odd, rr_v[SLOT - 8 :, :], rr_v[:8, :])


def pack_kernel(load_ref, rc_ref, vc_ref, vm_ref, rr_ref, lf_ref, h_ref, via_ref, out_ref, *scratch):
    *held, sem = scratch
    fetch([load_ref, rc_ref, vc_ref, vm_ref, rr_ref], held, sem)
    load_v, rc_v, vc_v, vm_v, rr_v = held
    scen, rows, cols = load_ref.shape
    at, first, _ = place("gx")
    even = lax.rem(at, 2) == 0
    for s in range(scen):
        lf_ref[pl.ds(s, rows, stride=scen), :] = load_v[s].astype(F32)
    row = lax.broadcasted_iota(jnp.int32, (rows, cols), 0)
    h = jnp.where(jnp.logical_and(first, row == 0), 0.0, rc_v[...])
    via = vm_v[...].astype(F32) * vc_v[...]
    h_ref[...] = h
    via_ref[...] = via
    n = HALO * scen
    out_ref[0:n, :] = jnp.where(even, lf_ref[rows * scen - n :, :], lf_ref[0:n, :])
    out_ref[n : n + SLOT, :] = jnp.where(even, h[rows - SLOT :], h[:SLOT])
    out_ref[n + SLOT : n + 2 * SLOT, :] = jnp.where(even, via[rows - SLOT :], via[:SLOT])
    out_ref[n + 2 * SLOT :, :] = jnp.where(even, rr_v[rows - 8 :, :], rr_v[:8, :])


def packer(scen, cols):
    lane = lax.broadcasted_iota(jnp.int32, (scen, cols), 1)
    is_flux = jnp.logical_or(
        jnp.logical_and(lane >= 1, lane <= 6), jnp.logical_and(lane >= cols - 7, lane <= cols - 3)
    )
    is_end = lane == cols - 1
    is_rolled = jnp.logical_and(lane >= 8, lane <= 11)

    def pack(q, jl, fl, p, grid_row):
        ends = jl if p is None else jl + p
        return jnp.where(
            is_flux,
            fl,
            jnp.where(
                is_end,
                q,
                jnp.where(lane == 0, pltpu.roll(ends, 1, 1), jnp.where(is_rolled, pltpu.roll(jl, 10, 1), grid_row)),
            ),
        )

    def add_p(w, p):
        return w + jnp.where(lane == 0, pltpu.roll(p, 1, 1), 0.0)

    return pack, add_p


def lower_row(v, via, minus_inv, vs, open_end):
    scen, cols = v.shape
    lane = lax.broadcasted_iota(jnp.int32, (scen, cols), 1)
    q = via * v
    tl = q * minus_inv
    dl = jnp.where(lane == 0, 0.0, pltpu.roll(tl, 1, 1)) - tl
    jl = vs * dl
    inner = jnp.where(jnp.logical_or(lane == 0, jnp.logical_and(open_end, lane == cols - 1)), 0.0, jl)
    return q, tl, dl, jl, inner - pltpu.roll(inner, cols - 1, 1)


def core_kernel(
    scen, lf_ref, h_ref, via_ref, cc_ref, pm_ref, cr_ref, pick_ref,
    fl_ref, acc_ref, edge_ref, low_ref, strip_ref, res_ref,
    inv_s, low_s, w_s,
):
    rows, cols = h_ref.shape
    _, first_y, last_y = place("gy")
    lane = lax.broadcasted_iota(jnp.int32, (rows, cols), 1)
    h, via = h_ref[...], via_ref[...]
    inv_s[...] = 1.0 / (h + pltpu.roll(h, rows - 1, 0) + via + LEAK)

    tie_low = via + pm_ref[...].astype(F32) * PAD + LEAK
    vs = jnp.where(jnp.logical_and(first_y, lane == 0), 0.0, cc_ref[...])
    open_end = jnp.logical_and(jnp.logical_not(last_y), lane == cols - 1)
    vs_next = jnp.where(lane == cols - 1, 0.0, pltpu.roll(vs, cols - 1, 1))
    diag_low = vs + vs_next + tie_low
    low_s[0] = jnp.where(open_end, 0.0, -1.0 / diag_low)
    low_s[1] = tie_low
    low_s[2] = vs
    low_s[3] = jnp.where(
        lane == 12,
        pltpu.roll(vs, 12, 1),
        jnp.where(
            lane == 13,
            pltpu.roll(diag_low, 14, 1),
            pltpu.roll(vs, 16, 1),
        ),
    )
    low_ref[...] = jnp.concatenate([low_s[k, rows - 1 : rows, :] for k in range(4)] * 2, 0)
    pack, _ = packer(scen, cols)

    def bc(ref, r):
        return jnp.broadcast_to(ref[pl.ds(r, 1), :], (scen, cols))

    def low(k, r):
        return jnp.broadcast_to(low_s[k, pl.ds(r, 1), :], (scen, cols))

    def keep(i, x):
        edge_ref[pl.ds(i * scen, scen), :] = x

    zero = jnp.zeros((scen, cols), F32)
    g0 = g1 = g2 = g3 = zero
    v0 = hv0 = t0 = None
    last = rows - 1
    for r in range(rows):
        v1 = hv1 = dv1 = None
        if r < last:
            load = lf_ref[pl.ds(r * scen, scen), :]
            v1 = load * bc(inv_s, r)
            g0 += load * v1
            g1 += (bc(via_ref, r) + LEAK) * v1 * v1
            if r > 0:
                dv1 = v0 - v1
                hv1 = bc(h_ref, r) * dv1
                g1 += hv1 * dv1
        if r > 0:
            m = r - 1
            via_m = bc(via_ref, m)
            tie = via_m + LEAK
            q, tl, dl, jl, fl = lower_row(v0, via_m, low(0, m), low(2, m), jnp.logical_not(last_y))
            fl_ref[pl.ds(m * scen, scen), :] = fl
            g2 -= q * tl
            g3 += low(1, m) * tl * tl + jl * dl
            p = t1 = None
            if 0 < m < last - 1:
                q_up = tie * v0 - hv0 + hv1
                t1 = q_up * bc(inv_s, m)
                p = via_m * t1
                g2 += q_up * t1
                g3 += tie * t1 * t1 - 2.0 * p * tl
                if m > 1:
                    dt = t0 - t1
                    g3 += bc(h_ref, m) * dt * dt
            w = pack(q, jl, fl, p, low(3, m))
            w_s[pl.ds(m * scen, scen), :] = w
            if m == 0:
                keep(0, v0)
                keep(1, hv1)
                keep(3, tl)
                keep(8, w)
            if m == 1:
                keep(2, t1)
            if m == last - 2:
                keep(6, t1)
            if m == last - 1:
                keep(4, v0)
                keep(5, hv0)
                keep(7, tl)
                keep(9, w)
            t0 = t1
        v0, hv0 = v1, hv1

    size = rows * scen
    fl_ref[pl.ds(last * scen, scen), :] = zero
    w_s[pl.ds(last * scen, scen), :] = zero
    w_s[pl.ds(size, rows), :] = cr_ref[...]
    w_s[size + rows :, :] = jnp.zeros((w_s.shape[0] - size - rows, cols), F32)
    for k, g in enumerate((g0, g1, g2, g3)):
        acc_ref[pl.ds(k * scen, scen), :] = g
    picked = pick_nt(pick_ref[...], w_s[...])
    for k in range(size // cols):
        strip_ref[pl.ds(k * PICKED, PICKED), :] = picked[:PICKED, k * cols : (k + 1) * cols]
    res = picked[PICKED + 8 :, size : size + cols]
    per = cols // rows
    group = lax.div(lax.broadcasted_iota(jnp.int32, (1, cols), 1), rows)
    packed = []
    for start in range(0, 16, per):
        line = res[start : start + 1]
        for k in range(1, per):
            line = jnp.where(group == k, pltpu.roll(res[start + k : start + k + 1], k * rows, 1), line)
        packed.append(line)
    res_ref[...] = jnp.concatenate(packed + [jnp.zeros((16 - len(packed), cols), F32)], 0)


def join_kernel(
    scen, lf_ref, h_ref, via_ref, acc_ref, edge_ref, low_ref, strip_ref, res_ref, a_ref, b_ref, pick_ref,
    pair_ref, plain_ref, seam_ref, fl_ref,
    w_s,
):
    rows, cols = h_ref.shape
    at_y, _, last_y = place("gy")
    even_y = lax.rem(at_y, 2) == 0
    before, after = sides("gx", a_ref, b_ref)
    n = HALO * scen
    last = rows - 1

    def grid(h, via):
        tie = via + LEAK
        inv = 1.0 / (h + pltpu.roll(h, 15, 0) + tie)

        def row(x, i):
            return jnp.broadcast_to(x[i : i + 1], (scen, cols))

        return (lambda i: row(h, i)), (lambda i: row(tie, i)), (lambda i: row(inv, i)), (lambda i: row(via, i))

    def edge(i):
        return edge_ref[pl.ds(i * scen, scen), :]

    pack, add_p = packer(scen, cols)

    h, tie, inv, via = grid(
        jnp.concatenate([before(pl.ds(n + SLOT - 8, 8)), h_ref[:8, :]], 0),
        jnp.concatenate([before(pl.ds(n + 2 * SLOT - 8, 8)), via_ref[:8, :]], 0),
    )
    v0, hv1, t1, tl0 = (edge(i) for i in range(4))
    far, near = before(pl.ds(n - 2 * scen, scen)) * inv(6), before(pl.ds(n - scen, scen)) * inv(7)
    dv0 = near - v0
    hv0 = h(8) * dv0
    t_near = (tie(7) * near - h(7) * (far - near) + hv0) * inv(7)
    q_up = tie(8) * v0 - hv0 + hv1
    t0 = q_up * inv(8)
    d0, d1 = t_near - t0, t0 - t1
    p = via(8) * t0
    g1 = hv0 * dv0
    g2 = q_up * t0
    g3 = tie(8) * t0 * t0 + h(8) * d0 * d0 + h(9) * d1 * d1 - 2.0 * p * tl0
    w_first = add_p(edge(8), p)

    h, tie, inv, via = grid(
        jnp.concatenate([h_ref[rows - 8 :, :], after(pl.ds(n, 8))], 0),
        jnp.concatenate([via_ref[rows - 8 :, :], after(pl.ds(n + SLOT, 8))], 0),
    )
    v0, hv0, t0, tl0 = (edge(i) for i in range(4, 8))
    load = lf_ref[pl.ds(last * scen, scen), :]
    v1 = load * inv(7)
    v2 = after(pl.ds(0, scen)) * inv(8)
    dv1 = v0 - v1
    hv1, hv2 = h(7) * dv1, h(8) * (v1 - v2)
    q0 = tie(6) * v0 - hv0 + hv1
    q1 = tie(7) * v1 - hv1 + hv2
    t1 = q0 * inv(6)
    t2 = q1 * inv(7)
    d1, d2 = t0 - t1, t1 - t2
    p0, p1 = via(6) * t1, via(7) * t2
    g0 = load * v1
    g1 += hv1 * dv1 + tie(7) * v1 * v1
    g2 += q0 * t1 + q1 * t2
    g3 += tie(6) * t1 * t1 + tie(7) * t2 * t2 + h(6) * d1 * d1 + h(7) * d2 * d2 - 2.0 * p0 * tl0

    def low(k):
        return jnp.broadcast_to(low_ref[pl.ds(k, 1), :], (scen, cols))

    q, tl, dl, jl, fl = lower_row(v1, via(7), low(0), low(2), jnp.logical_not(last_y))
    fl_ref[...] = fl
    g2 -= q * tl
    g3 += tl * (low(1) * tl - 2.0 * p1) + jl * dl

    w_s[...] = jnp.zeros_like(w_s)
    w_s[0:scen, :] = w_first
    for k, g in enumerate((g0, g1, g2, g3)):
        w_s[pl.ds((k + 1) * scen, scen), :] = acc_ref[pl.ds(k * scen, scen), :] + g
    w_s[cols - 2 * scen : cols - scen, :] = add_p(edge(9), p0)
    w_s[cols - scen :, :] = pack(q, jl, fl, p1, low(3))
    fresh = pick_nt(pick_ref[: PICKED + 8, :], w_s[...])

    lane = lax.broadcasted_iota(jnp.int32, (PICKED, cols), 1)
    parts = rows * scen // cols
    base = parts * USED
    half = 8 * rows // cols
    row = lax.broadcasted_iota(jnp.int32, (8, cols), 0)
    groups, pair_groups, seam_groups = [], [], []
    for k in range(parts):
        strip = strip_ref[pl.ds(k * PICKED, PICKED), :]
        if k == 0:
            strip = jnp.where(lane < scen, fresh[:PICKED], strip)
        if k == parts - 1:
            strip = jnp.where(lane >= cols - 2 * scen, fresh[:PICKED], strip)
        group = strip[:8]
        if k == 0:
            group = jnp.where(row == USED - 1, fresh[PICKED:], group)
        of_pair = of_seam = group
        if 1 <= k <= half:
            firsts, lasts = res_ref[k - 1 : k, :], res_ref[half + k - 1 : half + k, :]
            of_pair = jnp.where(row == USED - 1, jnp.where(even_y, lasts, firsts), group)
            of_seam = jnp.where(row == USED - 1, jnp.where(even_y, firsts, lasts), group)
        groups.append(group)
        pair_groups.append(of_pair)
        seam_groups.append(of_seam)
        firsts, lasts = strip[8:16], strip[16:24]
        pair_ref[pl.ds(base + k * 8, 8), :] = jnp.where(even_y, lasts, firsts)
        seam_ref[pl.ds(base + k * 8, 8), :] = jnp.where(even_y, firsts, lasts)
    pack_rows(pair_ref, pair_groups)
    pack_rows(plain_ref, groups)
    pack_rows(seam_ref, seam_groups)


def pack_rows(ref, groups):
    ref[0 : len(groups) * USED, :] = jnp.concatenate([g[:USED] for g in groups], 0)


def unpack_rows(ref, parts):
    return jnp.concatenate([ref[k * USED : (k + 1) * USED, :] for k in range(parts)], 1)


def across(ref, start, parts):
    return jnp.concatenate([ref[pl.ds(start + 8 * k, 8), :] for k in range(parts)], 1)


def merge_kernel(scen, parts, axis, step, radix, *refs):
    in_refs, held_refs, out_refs = refs[:radix], refs[radix:-2], refs[-2:]
    if not held_refs:
        in_refs, out_refs = refs[:radix], refs[radix:]
    cols = in_refs[0].shape[1]
    at = lax.rem(lax.div(lax.axis_index(axis), step), radix)
    given = [unpack_rows(ref, parts) for ref in in_refs]
    blocks = []
    for j in range(radix):
        block = given[0]
        for k in range(1, radix):
            block = jnp.where(jnp.bitwise_xor(at, k) == j, given[k], block)
        blocks.append(block)
    i2 = i3 = 0.0
    for left, right in zip(blocks, blocks[1:]):
        q, e, d = (left[i : i + 1] for i in range(3))
        jl_next, vs_next = right[3:4], right[4:5]
        r = q / (d + vs_next)
        i2 = i2 + q * r
        i3 = i3 + r * (e - jl_next)
    i3 = i2 + 2.0 * i3
    both = jnp.concatenate([i2, i3], 0)
    both = sum(both[:, k * cols : (k + 1) * cols] for k in range(parts))
    shift = scen
    while shift < cols:
        both = both + pltpu.roll(both, shift, 1)
        shift *= 2
    group = lax.div(lax.broadcasted_iota(jnp.int32, (1, cols), 1), scen)
    sums = jnp.where(group == 3, both[0:1], jnp.where(group == 4, both[1:2], 0.0))
    sums = sum((block[USED - 1 : USED, :cols] for block in given), sums)
    if not held_refs:
        out_refs[0][...] = sums
        return
    row = lax.broadcasted_iota(jnp.int32, (USED, cols), 0)
    held = unpack_rows(held_refs[0], parts)
    groups = []
    for k in range(parts):
        where = slice(k * cols, (k + 1) * cols)
        group = jnp.where(row < 3, blocks[-1][:, where], blocks[0][:, where])
        groups.append(jnp.where(row == USED - 1, sums if k == 0 else held[:, where], group))
    pack_rows(out_refs[0], groups)
    pack_rows(out_refs[1], groups)
    out_refs[1][parts * USED :, :] = held_refs[0][parts * USED :, :]


def row_kernel(
    scen, lf_ref, h_ref, via_ref, rr_ref, a_ref, b_ref,
    v_ref, t_ref, gv_ref, gt_ref, br_ref,
    inv_s, h_s, tie_s, fv_s, ft_s, s0_s,
):
    rows, cols = h_ref.shape
    _, first, last = place("gx")
    before, after = sides("gx", a_ref, b_ref)
    n = HALO * scen
    at = pl.ds(n, SLOT)
    h = jnp.concatenate([before(at), h_ref[...], after(at)], 0)
    at = pl.ds(n + SLOT, SLOT)
    tie = jnp.concatenate([before(at), via_ref[...], after(at)], 0) + LEAK
    h_s[...] = h
    tie_s[...] = tie
    inv_s[...] = 1.0 / (h + pltpu.roll(h, h.shape[0] - 1, 0) + tie)

    def load(r):
        if r < 0:
            return before(pl.ds((r + HALO) * scen, scen))
        if r >= rows:
            return after(pl.ds((r - rows) * scen, scen))
        return lf_ref[pl.ds(r * scen, scen), :]

    def bc(ref, r):
        return jnp.broadcast_to(ref[pl.ds(r + SLOT, 1), :], (scen, cols))

    v0 = hv0 = t0 = ht0 = None
    for r in range(-HALO, rows + HALO):
        v1 = load(r) * bc(inv_s, r)
        hv1 = None
        if r > -HALO:
            hv1 = bc(h_s, r) * (v0 - v1)
        if r > 1 - HALO:
            m = r - 1
            fv = hv0 - hv1
            t1 = (bc(tie_s, m) * v0 - fv) * bc(inv_s, m)
            ht1 = None
            if m > 1 - HALO:
                ht1 = bc(h_s, m) * (t0 - t1)
                if m > 2 - HALO:
                    ft_s[pl.ds((m - 1 + STEPS - 1) * scen, scen), :] = ht0 - ht1
                if m < rows + STEPS - 1:
                    fv_s[pl.ds((m + STEPS - 1) * scen, scen), :] = fv
            if 0 <= m < rows:
                v_ref[pl.ds(m, scen, stride=rows), :] = v0
                t_ref[pl.ds(m, scen, stride=rows), :] = t1
            t0, ht0 = t1, ht1
        v0, hv0 = v1, hv1

    n += 2 * SLOT
    size = rows + 16
    row = lax.broadcasted_iota(jnp.int32, (size, cols), 0)
    closed = jnp.logical_or(jnp.logical_and(first, row == 8), jnp.logical_and(last, row == 8 + rows))
    rates = jnp.where(closed, 0.0, RELAX)
    s0_s[...] = jnp.concatenate([before(pl.ds(n, 8)), rr_ref[...], after(pl.ds(n, 8))], 0)

    def one(_, carry):
        now = s0_s[...]
        flux = rates * (pltpu.roll(now, 1, 0) - now)
        s0_s[...] = now + flux - pltpu.roll(flux, size - 1, 0)
        return carry

    lax.fori_loop(0, STEPS, one, 0)
    br_ref[...] = s0_s[8 : 8 + rows, :]

    weights = taps()
    reach = STEPS - 1
    for f_ref, out_ref in ((fv_s, gv_ref), (ft_s, gt_ref)):

        def at(r):
            return f_ref[pl.ds((r + reach) * scen, scen), :]

        window = {}
        for r in range(-reach, rows + reach):
            if r < 0:
                x = jnp.where(first, at(-1 - r), at(r))
            elif r >= rows:
                x = jnp.where(last, at(2 * rows - 1 - r), at(r))
            else:
                x = at(r)
            window[r] = x
            m = r - reach
            if m >= 0:
                total = weights[0] * window[m]
                for d in range(1, STEPS):
                    total = total + weights[d] * (window[m - d] + window[m + d])
                out_ref[pl.ds(m, scen, stride=rows), :] = total
                del window[m - reach]


def col_kernel(scen, steps, fl_ref, fl_last_ref, cr_ref, pair_ref, seam_ref, *rest):
    *got_refs, source_ref, start_ref, gl_ref, bc_ref, out_s = rest
    rows, cols = cr_ref.shape
    parts = rows * scen // cols
    base = parts * USED
    at, first, last = place("gy")
    kind = first.astype(jnp.int32) + 2 * last.astype(jnp.int32)
    odd = lax.rem(at, 2) == 1

    def contents(ref):
        return unpack_rows(ref, parts), across(ref, base, parts)

    paired = contents(got_refs[0])
    met = tuple(jnp.zeros_like(x) for x in paired)
    for mask, ref in zip(steps[1:], got_refs[1:]):
        here = jnp.abs(jnp.bitwise_xor(at, mask) - at) == 1
        met = tuple(jnp.where(here, x, y) for x, y in zip(contents(ref), met))
    sums_before, before = (jnp.where(odd, x, y) for x, y in zip(paired, met))
    sums_after, after = (jnp.where(odd, y, x) for x, y in zip(paired, met))
    own, own_pair = contents(pair_ref)
    own_last = jnp.where(odd, across(seam_ref, base, parts), own_pair)

    def seam(left, lasts, right):
        q, d = left[0:1], left[2:3]
        u, vs = lasts[6:7], lasts[7:8]
        jl_next, vs_next = right[3:4], right[4:5]
        diag = d + vs_next
        t = -q / jnp.where(diag > 0, diag, 1.0)
        return u - vs * t, vs_next * t + jl_next

    jl_last, jl_0 = seam(sums_before, before, own)
    jr_last, jr_0 = seam(own, own_last, sums_after)
    jr_last = jnp.where(last, 0.0, jr_last)
    jr_0 = jnp.where(last, 0.0, jr_0)
    zero = jnp.zeros_like(jl_0)
    strip = jnp.concatenate(
        [
            before[1:6],
            before[0:1] - jl_last,
            jl_last - jl_0,
            zero,
            jr_0 - after[0:1],
            after[1:7],
            zero,
            jl_0,
            -jr_last,
            jr_last - jr_0,
            zero,
            zero,
            zero,
            zero,
            zero,
        ],
        0,
    )
    source = source_ref[kind]
    edge = dot_tn(strip, source[cols:])
    done = (rows - 1) * scen
    out_s[0:done, :] = dot_nn(fl_ref[0:done, :], source[:cols]) + edge[:done]
    out_s[done:, :] = dot_nn(fl_last_ref[...], source[:cols]) + edge[done:]
    for m in range(rows):
        gl_ref[pl.ds(m, scen, stride=rows), :] = out_s[pl.ds(m * scen, scen), :]
    start = start_ref[kind]
    per = cols // rows
    res = []
    for block in (sums_before, sums_after):
        for k in range(8):
            lanes = block[USED - 1 : USED, (1 + k // per) * cols : (2 + k // per) * cols]
            res.append(lanes if k % per == 0 else pltpu.roll(lanes, cols - k % per * rows, 1))
    edge = dot_tn(jnp.concatenate(res, 0), start[cols:])
    bc_ref[...] = dot_nn(cr_ref[...], start[:cols]) + edge[:rows]


def final_kernel(scen, rows, v_ref, t_ref, gv_ref, gt_ref, gl_ref, br_ref, bc_ref, *rest):
    *sum_refs, up_ref, row_ref, col_ref = rest
    cols = v_ref.shape[1]
    sums = sum(ref[...] for ref in sum_refs)
    g0, g1, g2, g3 = (pltpu.roll(sums, cols - (k + 1) * scen, 1) for k in range(4))
    alpha, ratio = g0 / g1, g2 / g1
    c1 = (g1 - alpha * g2) / (g3 - ratio * g2)
    c0 = alpha - ratio * c1
    lane = lax.broadcasted_iota(jnp.int32, (scen, cols), 1)
    sub = lax.broadcasted_iota(jnp.int32, (scen, cols), 0)

    def column(c):
        return jnp.sum(jnp.where(lane == sub, jnp.broadcast_to(c, lane.shape), 0.0), 1, keepdims=True)

    c0, c1 = column(c0), column(c1)
    br, bc = br_ref[...], bc_ref[...]
    for s in range(scen):
        at = pl.ds(s * rows, rows)
        a = jnp.broadcast_to(c0[s : s + 1], (rows, cols))
        b = jnp.broadcast_to(c1[s : s + 1], (rows, cols))
        up_ref[s] = a * v_ref[at, :] + b * t_ref[at, :]
        row_ref[s] = br + a * gv_ref[at, :] + b * gt_ref[at, :]
        col_ref[s] = bc + b * gl_ref[at, :]


def swap(block, axis, mask):
    count = lax.axis_size(axis)
    return lax.ppermute(block, axis, [(i, i ^ mask) for i in range(count)])


def swap_odd(block, axis, idle):
    count, lines = lax.axis_size(axis), lax.axis_size(idle)
    pairs = []
    for line in range(lines):
        for i in range(count):
            if 0 < i < count - 1:
                partner = line * count + (i + 1 if i % 2 else i - 1)
            elif lines % 2 == 0:
                partner = (line ^ 1) * count + i
            else:
                partner = line * count + count - 1 - i
            pairs.append((line * count + i, partner))
    return lax.ppermute(block, (idle, axis), pairs)


def call(kernel, out, scratch, cost, *args, space=pltpu.VMEM):
    return pl.pallas_call(
        kernel,
        out_shape=out,
        in_specs=[pl.BlockSpec(memory_space=space)] * len(args),
        out_specs=jax.tree.map(lambda _: pl.BlockSpec(memory_space=pltpu.VMEM), out),
        scratch_shapes=scratch,
        compiler_params=pltpu.CompilerParams(vmem_limit_bytes=24 * 2**20),
        cost_estimate=pl.CostEstimate(flops=cost, bytes_accessed=0, transcendentals=0),
    )(*args)


def on_device(
    load_current, row_conductance, col_conductance, via_conductance, pad_mask, via_mask, row_residual, col_residual
):
    scen, rows, cols = load_current.shape
    size = rows * scen
    parts = size // cols

    def f32(*shape):
        return jax.ShapeDtypeStruct(shape, F32)

    def vmem(*shape):
        return pltpu.VMEM(shape, F32)

    pick = jnp.asarray(picker(cols))
    source, start = (jnp.asarray(m) for m in spread(cols))
    grid, field = f32(rows, cols), f32(size, cols)

    wide = f32(HALO * scen + 2 * SLOT + 8, cols)
    sources = (load_current, row_conductance, via_conductance, via_mask, row_residual)
    pinned = [pltpu.with_memory_space_constraint(x, pltpu.HBM) for x in sources]
    sems = pltpu.SemaphoreType.DMA((len(sources),))
    shapes = [(scen, SLOT, cols)] + [(SLOT, cols)] * 4
    odd_strip = call(
        edge_kernel,
        wide,
        [pltpu.VMEM(shape, x.dtype) for shape, x in zip(shapes, sources)] + [vmem(SLOT * scen, cols), sems],
        10**5,
        *pinned,
        space=pltpu.HBM,
    )
    x_b = swap_odd(odd_strip, "gx", "grp")
    lf, h, via, even_strip = call(
        pack_kernel,
        (field, grid, grid, wide),
        [pltpu.VMEM(x.shape, x.dtype) for x in sources] + [sems],
        10**5,
        *pinned,
        space=pltpu.HBM,
    )
    x_a = swap(even_strip, "gx", 1)

    fl, acc, edge, low, strip, res = call(
        functools.partial(core_kernel, scen),
        (field, f32(4 * scen, cols), f32(10 * scen, cols), f32(8, cols), f32(parts * PICKED, cols), f32(16, cols)),
        [vmem(rows, cols), vmem(4, rows, cols), vmem(size + cols * (-(-rows // cols)), cols)],
        10**7,
        lf, h, via, col_conductance, pad_mask, col_residual, pick,
    )
    x_a, x_b, acc = lax.optimization_barrier((x_a, x_b, acc))

    plain_shape, full_shape = f32(parts * USED + 0, cols), f32(parts * (USED + 8) + 0, cols)
    seam_shape = f32(parts * (USED + 8) + 8, cols)
    pair, plain, seam, fl_last = call(
        functools.partial(join_kernel, scen),
        (full_shape, plain_shape, seam_shape, f32(scen, cols)),
        [vmem(cols, cols)],
        10**6,
        lf, h, via, acc, edge, low, strip, res, x_a, x_b, pick,
    )

    ext = rows + 2 * SLOT
    reach = (rows + 2 * (STEPS - 1)) * scen
    v, t, gv, gt, br = call(
        functools.partial(row_kernel, scen),
        (field, field, field, field, grid),
        [vmem(ext, cols)] * 3 + [vmem(reach, cols)] * 2 + [vmem(rows + 16, cols)],
        10**7,
        lf, h, via, row_residual, x_a, x_b,
    )

    own_pair, own_seam, masks, received = pair, seam, [], []
    step, count = 1, lax.axis_size("gy")
    while step < count:
        radix = 4 if 4 * step <= count else 2
        got = []
        for k in range(1, radix):
            mask = k * step + step - 1
            whole = k % 2 == 1
            got.append(swap((pair if mask == 1 else seam) if whole else plain, "gy", mask))
            if whole:
                masks.append(mask)
                received.append(got[-1])
        if step * radix == count:
            *got, br = lax.optimization_barrier((*got, br))
        merge = functools.partial(merge_kernel, scen, parts, "gy", step, radix)
        if step * radix < count:
            plain, seam = call(merge, (plain_shape, seam_shape), [], 10**5, plain, *got, seam)
        else:
            sums = call(merge, f32(1, cols), [], 10**5, plain, *got)
        step *= radix

    gl, bc = call(
        functools.partial(col_kernel, scen, masks),
        (field, grid),
        [vmem(size, cols)],
        10**7,
        fl, fl_last, col_residual, own_pair, own_seam, *received, source, start,
    )

    step, others = 1, []
    while step < lax.axis_size("gx"):
        radix = 4 if 4 * step <= lax.axis_size("gx") else 2
        sums = sum(others, sums)
        others = [swap(sums, "gx", step * k) for k in range(1, radix)]
        if step == 1:
            *others, bc = lax.optimization_barrier((*others, bc))
        step *= radix

    shape = f32(scen, rows, cols)
    return call(
        functools.partial(final_kernel, scen, rows),
        (shape, shape, shape),
        [],
        10**6,
        v, t, gv, gt, gl, br, bc, sums, *others,
    )


def solution(mesh):
    field = P(None, ("grp", "gx"), "gy")
    grid = P(("grp", "gx"), "gy")
    return jax.shard_map(
        on_device,
        mesh=mesh,
        in_specs=(field,) + (grid,) * 7,
        out_specs=(field,) * 3,
        check_vma=False,
    )
```

```python
import functools

import jax
import jax.numpy as jnp
import numpy as np
from jax import lax
from jax.experimental import pallas as pl
from jax.experimental.pallas import tpu as pltpu
from jax.sharding import PartitionSpec as P

STEPS = 8
RELAX = 0.45
DRIVE = 4.0
PAD = 20.0
LEAK = 0.05

F32 = jnp.float32
HALO = STEPS + 1
SLOT = 16

SUM_LANES = [-1, 0, 13, 10, 12]
FIRST_LANES = [11, 1, 2, 3, 4, 5, 6]
LAST_LANES = [8, -7, -6, -5, -4, -3, 9, 15]
PICKED = 8 + 8 + 8
USED = 8


def dot_nt(a, b):
    return lax.dot_general(
        a, b, (((1,), (1,)), ((), ())), precision=lax.Precision.HIGHEST, preferred_element_type=F32
    )


def pick_nt(pick, b):
    out = None
    for _ in range(3):
        part = b.astype(jnp.bfloat16)
        b = b - part.astype(F32)
        term = lax.dot_general(
            pick.astype(jnp.bfloat16), part, (((1,), (1,)), ((), ())), preferred_element_type=F32
        )
        out = term if out is None else out + term
    return out


def dot_nn(a, b):
    return lax.dot_general(
        a, b, (((1,), (0,)), ((), ())), precision=lax.Precision.HIGHEST, preferred_element_type=F32
    )


def dot_tn(a, b):
    return lax.dot_general(
        a, b, (((0,), (0,)), ((), ())), precision=lax.Precision.HIGHEST, preferred_element_type=F32
    )


def picker(cols):
    e = np.zeros((PICKED + 8 + 16, cols), np.float32)
    for base, lanes in ((0, SUM_LANES), (8, FIRST_LANES), (16, LAST_LANES)):
        for i, lane in enumerate(lanes):
            e[base + i, lane % cols] = 1
    e[PICKED : PICKED + 8] = 1
    for i in range(8):
        e[PICKED + 8 + i, i] = 1
        e[PICKED + 16 + i, cols - 8 + i] = 1
    return e


def spread(cols):
    size = cols + 16
    sources, starts = [], []
    for first, last in ((0, 0), (1, 0), (0, 1), (1, 1)):
        rate = np.full(size + 1, RELAX)
        rate[0] = rate[size] = 0
        if first:
            rate[8] = 0
        if last:
            rate[8 + cols] = 0
        step = np.eye(size)
        for i in range(size):
            step[i, i] -= rate[i] + rate[i + 1]
            if i:
                step[i, i - 1] += rate[i]
            if i + 1 < size:
                step[i, i + 1] += rate[i + 1]
        power, total = np.eye(size), np.zeros((size, size))
        for _ in range(STEPS):
            total += power
            power = step @ power
        source = (RELAX * DRIVE * total)[8 : 8 + cols].T
        start = power[8 : 8 + cols].T
        extra = np.zeros((24, cols))
        extra[0:7] = source[1:8]
        extra[8:15] = source[8 + cols : 15 + cols]
        extra[16] = source[8]
        extra[17] = source[8 + cols - 2]
        extra[18] = source[8 + cols - 1]
        sources.append(np.concatenate([source[8 : 8 + cols], extra]))
        starts.append(np.concatenate([start[8 : 8 + cols], start[:8], start[8 + cols :]]))
    return np.stack(sources).astype(np.float32), np.stack(starts).astype(np.float32)


def taps():
    size = 4 * STEPS + 1
    step = np.eye(size) * (1 - 2 * RELAX) + RELAX * (np.eye(size, k=1) + np.eye(size, k=-1))
    total = sum(np.linalg.matrix_power(step, k) for k in range(STEPS))
    return [float(x) for x in RELAX * DRIVE * total[size // 2, size // 2 : size // 2 + STEPS]]


def place(axis):
    at, count = lax.axis_index(axis), lax.axis_size(axis)
    return at, at == 0, at == count - 1


def sides(axis, even_ref, odd_ref):
    at, first, last = place(axis)
    odd = lax.rem(at, 2) == 1

    def before(*where):
        return jnp.where(odd, even_ref[where], jnp.where(first, 0.0, odd_ref[where]))

    def after(*where):
        return jnp.where(odd, jnp.where(last, 0.0, odd_ref[where]), even_ref[where])

    return before, after


def fetch(args, held, sem):
    copies = [pltpu.make_async_copy(src, dst, sem.at[i]) for i, (src, dst) in enumerate(zip(args, held))]
    for copy in copies:
        copy.start()
    for copy in copies:
        copy.wait()


def edge_kernel(load_ref, rc_ref, vc_ref, vm_ref, rr_ref, out_ref, *scratch):
    *held, lf_s, sem = scratch
    scen, rows, cols = load_ref.shape
    odd = lax.rem(lax.axis_index("gx"), 2) == 1
    part = pl.ds(pl.multiple_of(jnp.where(odd, rows - SLOT, 0), SLOT), SLOT)
    fetch([load_ref.at[:, part], *(ref.at[part] for ref in (rc_ref, vc_ref, vm_ref, rr_ref))], held, sem)
    load_v, rc_v, vc_v, vm_v, rr_v = held
    for s in range(scen):
        lf_s[pl.ds(s, SLOT, stride=scen), :] = load_v[s].astype(F32)
    n = HALO * scen
    out_ref[0:n, :] = jnp.where(odd, lf_s[(SLOT - HALO) * scen :, :], lf_s[0:n, :])
    out_ref[n : n + SLOT, :] = rc_v[...]
    out_ref[n + SLOT : n + 2 * SLOT, :] = vm_v[...].astype(F32) * vc_v[...]
    out_ref[n + 2 * SLOT :, :] = jnp.where(odd, rr_v[SLOT - 8 :, :], rr_v[:8, :])


def pack_kernel(load_ref, rc_ref, vc_ref, vm_ref, rr_ref, lf_ref, h_ref, via_ref, out_ref, *scratch):
    *held, sem = scratch
    fetch([load_ref, rc_ref, vc_ref, vm_ref, rr_ref], held, sem)
    load_v, rc_v, vc_v, vm_v, rr_v = held
    scen, rows, cols = load_ref.shape
    at, first, _ = place("gx")
    even = lax.rem(at, 2) == 0
    for s in range(scen):
        lf_ref[pl.ds(s, rows, stride=scen), :] = load_v[s].astype(F32)
    row = lax.broadcasted_iota(jnp.int32, (rows, cols), 0)
    h = jnp.where(jnp.logical_and(first, row == 0), 0.0, rc_v[...])
    via = vm_v[...].astype(F32) * vc_v[...]
    h_ref[...] = h
    via_ref[...] = via
    n = HALO * scen
    out_ref[0:n, :] = jnp.where(even, lf_ref[rows * scen - n :, :], lf_ref[0:n, :])
    out_ref[n : n + SLOT, :] = jnp.where(even, h[rows - SLOT :], h[:SLOT])
    out_ref[n + SLOT : n + 2 * SLOT, :] = jnp.where(even, via[rows - SLOT :], via[:SLOT])
    out_ref[n + 2 * SLOT :, :] = jnp.where(even, rr_v[rows - 8 :, :], rr_v[:8, :])


def packer(scen, cols):
    lane = lax.broadcasted_iota(jnp.int32, (scen, cols), 1)
    is_flux = jnp.logical_or(
        jnp.logical_and(lane >= 1, lane <= 6), jnp.logical_and(lane >= cols - 7, lane <= cols - 3)
    )
    is_end = lane == cols - 1
    is_rolled = jnp.logical_and(lane >= 8, lane <= 11)

    def pack(q, jl, fl, p, grid_row):
        ends = jl if p is None else jl + p
        return jnp.where(
            is_flux,
            fl,
            jnp.where(
                is_end,
                q,
                jnp.where(lane == 0, pltpu.roll(ends, 1, 1), jnp.where(is_rolled, pltpu.roll(jl, 10, 1), grid_row)),
            ),
        )

    def add_p(w, p):
        return w + jnp.where(lane == 0, pltpu.roll(p, 1, 1), 0.0)

    return pack, add_p


def lower_row(v, via, minus_inv, vs, open_end):
    scen, cols = v.shape
    lane = lax.broadcasted_iota(jnp.int32, (scen, cols), 1)
    q = via * v
    tl = q * minus_inv
    dl = jnp.where(lane == 0, 0.0, pltpu.roll(tl, 1, 1)) - tl
    jl = vs * dl
    inner = jnp.where(jnp.logical_or(lane == 0, jnp.logical_and(open_end, lane == cols - 1)), 0.0, jl)
    return q, tl, dl, jl, inner - pltpu.roll(inner, cols - 1, 1)


def core_kernel(
    scen, lf_ref, h_ref, via_ref, cc_ref, pm_ref, cr_ref, pick_ref,
    fl_ref, acc_ref, edge_ref, low_ref, strip_ref, res_ref,
    inv_s, low_s, w_s,
):
    rows, cols = h_ref.shape
    _, first_y, last_y = place("gy")
    lane = lax.broadcasted_iota(jnp.int32, (rows, cols), 1)
    h, via = h_ref[...], via_ref[...]
    inv_s[...] = 1.0 / (h + pltpu.roll(h, rows - 1, 0) + via + LEAK)

    tie_low = via + pm_ref[...].astype(F32) * PAD + LEAK
    vs = jnp.where(jnp.logical_and(first_y, lane == 0), 0.0, cc_ref[...])
    open_end = jnp.logical_and(jnp.logical_not(last_y), lane == cols - 1)
    vs_next = jnp.where(lane == cols - 1, 0.0, pltpu.roll(vs, cols - 1, 1))
    diag_low = vs + vs_next + tie_low
    low_s[0] = jnp.where(open_end, 0.0, -1.0 / diag_low)
    low_s[1] = tie_low
    low_s[2] = vs
    low_s[3] = jnp.where(
        lane == 12,
        pltpu.roll(vs, 12, 1),
        jnp.where(
            lane == 13,
            pltpu.roll(diag_low, 14, 1),
            pltpu.roll(vs, 16, 1),
        ),
    )
    low_ref[...] = jnp.concatenate([low_s[k, rows - 1 : rows, :] for k in range(4)] * 2, 0)
    pack, _ = packer(scen, cols)

    def bc(ref, r):
        return jnp.broadcast_to(ref[pl.ds(r, 1), :], (scen, cols))

    def low(k, r):
        return jnp.broadcast_to(low_s[k, pl.ds(r, 1), :], (scen, cols))

    def keep(i, x):
        edge_ref[pl.ds(i * scen, scen), :] = x

    zero = jnp.zeros((scen, cols), F32)
    g0 = g1 = g2 = g3 = zero
    v0 = hv0 = t0 = None
    last = rows - 1
    for r in range(rows):
        v1 = hv1 = dv1 = None
        if r < last:
            load = lf_ref[pl.ds(r * scen, scen), :]
            v1 = load * bc(inv_s, r)
            g0 += load * v1
            g1 += (bc(via_ref, r) + LEAK) * v1 * v1
            if r > 0:
                dv1 = v0 - v1
                hv1 = bc(h_ref, r) * dv1
                g1 += hv1 * dv1
        if r > 0:
            m = r - 1
            via_m = bc(via_ref, m)
            tie = via_m + LEAK
            q, tl, dl, jl, fl = lower_row(v0, via_m, low(0, m), low(2, m), jnp.logical_not(last_y))
            fl_ref[pl.ds(m * scen, scen), :] = fl
            g2 -= q * tl
            g3 += low(1, m) * tl * tl + jl * dl
            p = t1 = None
            if 0 < m < last - 1:
                q_up = tie * v0 - hv0 + hv1
                t1 = q_up * bc(inv_s, m)
                p = via_m * t1
                g2 += q_up * t1
                g3 += tie * t1 * t1 - 2.0 * p * tl
                if m > 1:
                    dt = t0 - t1
                    g3 += bc(h_ref, m) * dt * dt
            w = pack(q, jl, fl, p, low(3, m))
            w_s[pl.ds(m * scen, scen), :] = w
            if m == 0:
                keep(0, v0)
                keep(1, hv1)
                keep(3, tl)
                keep(8, w)
            if m == 1:
                keep(2, t1)
            if m == last - 2:
                keep(6, t1)
            if m == last - 1:
                keep(4, v0)
                keep(5, hv0)
                keep(7, tl)
                keep(9, w)
            t0 = t1
        v0, hv0 = v1, hv1

    size = rows * scen
    fl_ref[pl.ds(last * scen, scen), :] = zero
    w_s[pl.ds(last * scen, scen), :] = zero
    w_s[pl.ds(size, rows), :] = cr_ref[...]
    w_s[size + rows :, :] = jnp.zeros((w_s.shape[0] - size - rows, cols), F32)
    for k, g in enumerate((g0, g1, g2, g3)):
        acc_ref[pl.ds(k * scen, scen), :] = g
    picked = pick_nt(pick_ref[...], w_s[...])
    for k in range(size // cols):
        strip_ref[pl.ds(k * PICKED, PICKED), :] = picked[:PICKED, k * cols : (k + 1) * cols]
    res = picked[PICKED + 8 :, size : size + cols]
    per = cols // rows
    group = lax.div(lax.broadcasted_iota(jnp.int32, (1, cols), 1), rows)
    packed = []
    for start in range(0, 16, per):
        line = res[start : start + 1]
        for k in range(1, per):
            line = jnp.where(group == k, pltpu.roll(res[start + k : start + k + 1], k * rows, 1), line)
        packed.append(line)
    res_ref[...] = jnp.concatenate(packed + [jnp.zeros((16 - len(packed), cols), F32)], 0)


def join_kernel(
    scen, lf_ref, h_ref, via_ref, acc_ref, edge_ref, low_ref, strip_ref, res_ref, a_ref, b_ref, pick_ref,
    pair_ref, plain_ref, seam_ref, fl_ref,
    w_s,
):
    rows, cols = h_ref.shape
    at_y, _, last_y = place("gy")
    even_y = lax.rem(at_y, 2) == 0
    before, after = sides("gx", a_ref, b_ref)
    n = HALO * scen
    last = rows - 1

    def grid(h, via):
        tie = via + LEAK
        inv = 1.0 / (h + pltpu.roll(h, 15, 0) + tie)

        def row(x, i):
            return jnp.broadcast_to(x[i : i + 1], (scen, cols))

        return (lambda i: row(h, i)), (lambda i: row(tie, i)), (lambda i: row(inv, i)), (lambda i: row(via, i))

    def edge(i):
        return edge_ref[pl.ds(i * scen, scen), :]

    pack, add_p = packer(scen, cols)

    h, tie, inv, via = grid(
        jnp.concatenate([before(pl.ds(n + SLOT - 8, 8)), h_ref[:8, :]], 0),
        jnp.concatenate([before(pl.ds(n + 2 * SLOT - 8, 8)), via_ref[:8, :]], 0),
    )
    v0, hv1, t1, tl0 = (edge(i) for i in range(4))
    far, near = before(pl.ds(n - 2 * scen, scen)) * inv(6), before(pl.ds(n - scen, scen)) * inv(7)
    dv0 = near - v0
    hv0 = h(8) * dv0
    t_near = (tie(7) * near - h(7) * (far - near) + hv0) * inv(7)
    q_up = tie(8) * v0 - hv0 + hv1
    t0 = q_up * inv(8)
    d0, d1 = t_near - t0, t0 - t1
    p = via(8) * t0
    g1 = hv0 * dv0
    g2 = q_up * t0
    g3 = tie(8) * t0 * t0 + h(8) * d0 * d0 + h(9) * d1 * d1 - 2.0 * p * tl0
    w_first = add_p(edge(8), p)

    h, tie, inv, via = grid(
        jnp.concatenate([h_ref[rows - 8 :, :], after(pl.ds(n, 8))], 0),
        jnp.concatenate([via_ref[rows - 8 :, :], after(pl.ds(n + SLOT, 8))], 0),
    )
    v0, hv0, t0, tl0 = (edge(i) for i in range(4, 8))
    load = lf_ref[pl.ds(last * scen, scen), :]
    v1 = load * inv(7)
    v2 = after(pl.ds(0, scen)) * inv(8)
    dv1 = v0 - v1
    hv1, hv2 = h(7) * dv1, h(8) * (v1 - v2)
    q0 = tie(6) * v0 - hv0 + hv1
    q1 = tie(7) * v1 - hv1 + hv2
    t1 = q0 * inv(6)
    t2 = q1 * inv(7)
    d1, d2 = t0 - t1, t1 - t2
    p0, p1 = via(6) * t1, via(7) * t2
    g0 = load * v1
    g1 += hv1 * dv1 + tie(7) * v1 * v1
    g2 += q0 * t1 + q1 * t2
    g3 += tie(6) * t1 * t1 + tie(7) * t2 * t2 + h(6) * d1 * d1 + h(7) * d2 * d2 - 2.0 * p0 * tl0

    def low(k):
        return jnp.broadcast_to(low_ref[pl.ds(k, 1), :], (scen, cols))

    q, tl, dl, jl, fl = lower_row(v1, via(7), low(0), low(2), jnp.logical_not(last_y))
    fl_ref[...] = fl
    g2 -= q * tl
    g3 += tl * (low(1) * tl - 2.0 * p1) + jl * dl

    w_s[...] = jnp.zeros_like(w_s)
    w_s[0:scen, :] = w_first
    for k, g in enumerate((g0, g1, g2, g3)):
        w_s[pl.ds((k + 1) * scen, scen), :] = acc_ref[pl.ds(k * scen, scen), :] + g
    w_s[cols - 2 * scen : cols - scen, :] = add_p(edge(9), p0)
    w_s[cols - scen :, :] = pack(q, jl, fl, p1, low(3))
    fresh = pick_nt(pick_ref[: PICKED + 8, :], w_s[...])

    lane = lax.broadcasted_iota(jnp.int32, (PICKED, cols), 1)
    parts = rows * scen // cols
    base = parts * USED
    half = 8 * rows // cols
    row = lax.broadcasted_iota(jnp.int32, (8, cols), 0)
    groups, pair_groups, seam_groups = [], [], []
    for k in range(parts):
        strip = strip_ref[pl.ds(k * PICKED, PICKED), :]
        if k == 0:
            strip = jnp.where(lane < scen, fresh[:PICKED], strip)
        if k == parts - 1:
            strip = jnp.where(lane >= cols - 2 * scen, fresh[:PICKED], strip)
        group = strip[:8]
        if k == 0:
            group = jnp.where(row == USED - 1, fresh[PICKED:], group)
        of_pair = of_seam = group
        if 1 <= k <= half:
            firsts, lasts = res_ref[k - 1 : k, :], res_ref[half + k - 1 : half + k, :]
            of_pair = jnp.where(row == USED - 1, jnp.where(even_y, lasts, firsts), group)
            of_seam = jnp.where(row == USED - 1, jnp.where(even_y, firsts, lasts), group)
        groups.append(group)
        pair_groups.append(of_pair)
        seam_groups.append(of_seam)
        firsts, lasts = strip[8:16], strip[16:24]
        pair_ref[pl.ds(base + k * 8, 8), :] = jnp.where(even_y, lasts, firsts)
        seam_ref[pl.ds(base + k * 8, 8), :] = jnp.where(even_y, firsts, lasts)
    pack_rows(pair_ref, pair_groups)
    pack_rows(plain_ref, groups)
    pack_rows(seam_ref, seam_groups)


def pack_rows(ref, groups):
    ref[0 : len(groups) * USED, :] = jnp.concatenate([g[:USED] for g in groups], 0)


def unpack_rows(ref, parts):
    return jnp.concatenate([ref[k * USED : (k + 1) * USED, :] for k in range(parts)], 1)


def across(ref, start, parts):
    return jnp.concatenate([ref[pl.ds(start + 8 * k, 8), :] for k in range(parts)], 1)


def merge_kernel(scen, parts, axis, step, radix, *refs):
    in_refs, held_refs, out_refs = refs[:radix], refs[radix:-2], refs[-2:]
    if not held_refs:
        in_refs, out_refs = refs[:radix], refs[radix:]
    cols = in_refs[0].shape[1]
    at = lax.rem(lax.div(lax.axis_index(axis), step), radix)
    given = [unpack_rows(ref, parts) for ref in in_refs]
    blocks = []
    for j in range(radix):
        block = given[0]
        for k in range(1, radix):
            block = jnp.where(jnp.bitwise_xor(at, k) == j, given[k], block)
        blocks.append(block)
    i2 = i3 = 0.0
    for left, right in zip(blocks, blocks[1:]):
        q, e, d = (left[i : i + 1] for i in range(3))
        jl_next, vs_next = right[3:4], right[4:5]
        r = q / (d + vs_next)
        i2 = i2 + q * r
        i3 = i3 + r * (e - jl_next)
    i3 = i2 + 2.0 * i3
    both = jnp.concatenate([i2, i3], 0)
    both = sum(both[:, k * cols : (k + 1) * cols] for k in range(parts))
    shift = scen
    while shift < cols:
        both = both + pltpu.roll(both, shift, 1)
        shift *= 2
    group = lax.div(lax.broadcasted_iota(jnp.int32, (1, cols), 1), scen)
    sums = jnp.where(group == 3, both[0:1], jnp.where(group == 4, both[1:2], 0.0))
    sums = sum((block[USED - 1 : USED, :cols] for block in given), sums)
    if not held_refs:
        out_refs[0][...] = sums
        return
    row = lax.broadcasted_iota(jnp.int32, (USED, cols), 0)
    held = unpack_rows(held_refs[0], parts)
    groups = []
    for k in range(parts):
        where = slice(k * cols, (k + 1) * cols)
        group = jnp.where(row < 3, blocks[-1][:, where], blocks[0][:, where])
        groups.append(jnp.where(row == USED - 1, sums if k == 0 else held[:, where], group))
    pack_rows(out_refs[0], groups)
    pack_rows(out_refs[1], groups)
    out_refs[1][parts * USED :, :] = held_refs[0][parts * USED :, :]


def row_kernel(
    scen, lf_ref, h_ref, via_ref, rr_ref, a_ref, b_ref,
    v_ref, t_ref, gv_ref, gt_ref, br_ref,
    inv_s, h_s, tie_s, fv_s, ft_s, s0_s,
):
    rows, cols = h_ref.shape
    _, first, last = place("gx")
    before, after = sides("gx", a_ref, b_ref)
    n = HALO * scen
    at = pl.ds(n, SLOT)
    h = jnp.concatenate([before(at), h_ref[...], after(at)], 0)
    at = pl.ds(n + SLOT, SLOT)
    tie = jnp.concatenate([before(at), via_ref[...], after(at)], 0) + LEAK
    h_s[...] = h
    tie_s[...] = tie
    inv_s[...] = 1.0 / (h + pltpu.roll(h, h.shape[0] - 1, 0) + tie)

    def load(r):
        if r < 0:
            return before(pl.ds((r + HALO) * scen, scen))
        if r >= rows:
            return after(pl.ds((r - rows) * scen, scen))
        return lf_ref[pl.ds(r * scen, scen), :]

    def bc(ref, r):
        return jnp.broadcast_to(ref[pl.ds(r + SLOT, 1), :], (scen, cols))

    v0 = hv0 = t0 = ht0 = None
    for r in range(-HALO, rows + HALO):
        v1 = load(r) * bc(inv_s, r)
        hv1 = None
        if r > -HALO:
            hv1 = bc(h_s, r) * (v0 - v1)
        if r > 1 - HALO:
            m = r - 1
            fv = hv0 - hv1
            t1 = (bc(tie_s, m) * v0 - fv) * bc(inv_s, m)
            ht1 = None
            if m > 1 - HALO:
                ht1 = bc(h_s, m) * (t0 - t1)
                if m > 2 - HALO:
                    ft_s[pl.ds((m - 1 + STEPS - 1) * scen, scen), :] = ht0 - ht1
                if m < rows + STEPS - 1:
                    fv_s[pl.ds((m + STEPS - 1) * scen, scen), :] = fv
            if 0 <= m < rows:
                v_ref[pl.ds(m, scen, stride=rows), :] = v0
                t_ref[pl.ds(m, scen, stride=rows), :] = t1
            t0, ht0 = t1, ht1
        v0, hv0 = v1, hv1

    n += 2 * SLOT
    size = rows + 16
    row = lax.broadcasted_iota(jnp.int32, (size, cols), 0)
    closed = jnp.logical_or(jnp.logical_and(first, row == 8), jnp.logical_and(last, row == 8 + rows))
    rates = jnp.where(closed, 0.0, RELAX)
    s0_s[...] = jnp.concatenate([before(pl.ds(n, 8)), rr_ref[...], after(pl.ds(n, 8))], 0)

    def one(_, carry):
        now = s0_s[...]
        flux = rates * (pltpu.roll(now, 1, 0) - now)
        s0_s[...] = now + flux - pltpu.roll(flux, size - 1, 0)
        return carry

    lax.fori_loop(0, STEPS, one, 0)
    br_ref[...] = s0_s[8 : 8 + rows, :]

    weights = taps()
    reach = STEPS - 1
    for f_ref, out_ref in ((fv_s, gv_ref), (ft_s, gt_ref)):

        def at(r):
            return f_ref[pl.ds((r + reach) * scen, scen), :]

        window = {}
        for r in range(-reach, rows + reach):
            if r < 0:
                x = jnp.where(first, at(-1 - r), at(r))
            elif r >= rows:
                x = jnp.where(last, at(2 * rows - 1 - r), at(r))
            else:
                x = at(r)
            window[r] = x
            m = r - reach
            if m >= 0:
                total = weights[0] * window[m]
                for d in range(1, STEPS):
                    total = total + weights[d] * (window[m - d] + window[m + d])
                out_ref[pl.ds(m, scen, stride=rows), :] = total
                del window[m - reach]


def col_kernel(scen, steps, fl_ref, fl_last_ref, cr_ref, pair_ref, seam_ref, *rest):
    *got_refs, source_ref, start_ref, gl_ref, bc_ref, out_s = rest
    rows, cols = cr_ref.shape
    parts = rows * scen // cols
    base = parts * USED
    at, first, last = place("gy")
    kind = first.astype(jnp.int32) + 2 * last.astype(jnp.int32)
    odd = lax.rem(at, 2) == 1

    def contents(ref):
        return unpack_rows(ref, parts), across(ref, base, parts)

    paired = contents(got_refs[0])
    met = tuple(jnp.zeros_like(x) for x in paired)
    for mask, ref in zip(steps[1:], got_refs[1:]):
        here = jnp.abs(jnp.bitwise_xor(at, mask) - at) == 1
        met = tuple(jnp.where(here, x, y) for x, y in zip(contents(ref), met))
    sums_before, before = (jnp.where(odd, x, y) for x, y in zip(paired, met))
    sums_after, after = (jnp.where(odd, y, x) for x, y in zip(paired, met))
    own, own_pair = contents(pair_ref)
    own_last = jnp.where(odd, across(seam_ref, base, parts), own_pair)

    def seam(left, lasts, right):
        q, d = left[0:1], left[2:3]
        u, vs = lasts[6:7], lasts[7:8]
        jl_next, vs_next = right[3:4], right[4:5]
        diag = d + vs_next
        t = -q / jnp.where(diag > 0, diag, 1.0)
        return u - vs * t, vs_next * t + jl_next

    jl_last, jl_0 = seam(sums_before, before, own)
    jr_last, jr_0 = seam(own, own_last, sums_after)
    jr_last = jnp.where(last, 0.0, jr_last)
    jr_0 = jnp.where(last, 0.0, jr_0)
    zero = jnp.zeros_like(jl_0)
    strip = jnp.concatenate(
        [
            before[1:6],
            before[0:1] - jl_last,
            jl_last - jl_0,
            zero,
            jr_0 - after[0:1],
            after[1:7],
            zero,
            jl_0,
            -jr_last,
            jr_last - jr_0,
            zero,
            zero,
            zero,
            zero,
            zero,
        ],
        0,
    )
    source = source_ref[kind]
    edge = dot_tn(strip, source[cols:])
    done = (rows - 1) * scen
    out_s[0:done, :] = dot_nn(fl_ref[0:done, :], source[:cols]) + edge[:done]
    out_s[done:, :] = dot_nn(fl_last_ref[...], source[:cols]) + edge[done:]
    for m in range(rows):
        gl_ref[pl.ds(m, scen, stride=rows), :] = out_s[pl.ds(m * scen, scen), :]
    start = start_ref[kind]
    per = cols // rows
    res = []
    for block in (sums_before, sums_after):
        for k in range(8):
            lanes = block[USED - 1 : USED, (1 + k // per) * cols : (2 + k // per) * cols]
            res.append(lanes if k % per == 0 else pltpu.roll(lanes, cols - k % per * rows, 1))
    edge = dot_tn(jnp.concatenate(res, 0), start[cols:])
    bc_ref[...] = dot_nn(cr_ref[...], start[:cols]) + edge[:rows]


def final_kernel(scen, rows, v_ref, t_ref, gv_ref, gt_ref, gl_ref, br_ref, bc_ref, *rest):
    *sum_refs, up_ref, row_ref, col_ref = rest
    cols = v_ref.shape[1]
    sums = sum(ref[...] for ref in sum_refs)
    g0, g1, g2, g3 = (pltpu.roll(sums, cols - (k + 1) * scen, 1) for k in range(4))
    alpha, ratio = g0 / g1, g2 / g1
    c1 = (g1 - alpha * g2) / (g3 - ratio * g2)
    c0 = alpha - ratio * c1
    lane = lax.broadcasted_iota(jnp.int32, (scen, cols), 1)
    sub = lax.broadcasted_iota(jnp.int32, (scen, cols), 0)

    def column(c):
        picked = jnp.where(lane == sub, jnp.broadcast_to(c, lane.shape), 0.0)
        return jnp.broadcast_to(jnp.sum(picked, 1, keepdims=True), lane.shape)

    c0, c1 = column(c0), column(c1)
    br, bc = br_ref[...], bc_ref[...]
    for s in range(scen):
        at = pl.ds(s * rows, rows)
        a = jnp.broadcast_to(c0[s : s + 1], (rows, cols))
        b = jnp.broadcast_to(c1[s : s + 1], (rows, cols))
        up_ref[s] = a * v_ref[at, :] + b * t_ref[at, :]
        row_ref[s] = br + a * gv_ref[at, :] + b * gt_ref[at, :]
        col_ref[s] = bc + b * gl_ref[at, :]


def swap(block, axis, mask):
    count = lax.axis_size(axis)
    return lax.ppermute(block, axis, [(i, i ^ mask) for i in range(count)])


def swap_odd(block, axis, idle):
    count, lines = lax.axis_size(axis), lax.axis_size(idle)
    pairs = []
    for line in range(lines):
        for i in range(count):
            if 0 < i < count - 1:
                partner = line * count + (i + 1 if i % 2 else i - 1)
            elif lines % 2 == 0:
                partner = (line ^ 1) * count + i
            else:
                partner = line * count + count - 1 - i
            pairs.append((line * count + i, partner))
    return lax.ppermute(block, (idle, axis), pairs)


def call(kernel, out, scratch, cost, *args, space=pltpu.VMEM):
    return pl.pallas_call(
        kernel,
        out_shape=out,
        in_specs=[pl.BlockSpec(memory_space=space)] * len(args),
        out_specs=jax.tree.map(lambda _: pl.BlockSpec(memory_space=pltpu.VMEM), out),
        scratch_shapes=scratch,
        compiler_params=pltpu.CompilerParams(vmem_limit_bytes=24 * 2**20),
        cost_estimate=pl.CostEstimate(flops=cost, bytes_accessed=0, transcendentals=0),
    )(*args)


def on_device(
    load_current, row_conductance, col_conductance, via_conductance, pad_mask, via_mask, row_residual, col_residual
):
    scen, rows, cols = load_current.shape
    size = rows * scen
    parts = size // cols

    def f32(*shape):
        return jax.ShapeDtypeStruct(shape, F32)

    def vmem(*shape):
        return pltpu.VMEM(shape, F32)

    pick = jnp.asarray(picker(cols))
    source, start = (jnp.asarray(m) for m in spread(cols))
    grid, field = f32(rows, cols), f32(size, cols)

    wide = f32(HALO * scen + 2 * SLOT + 8, cols)
    sources = (load_current, row_conductance, via_conductance, via_mask, row_residual)
    pinned = [pltpu.with_memory_space_constraint(x, pltpu.HBM) for x in sources]
    sems = pltpu.SemaphoreType.DMA((len(sources),))
    shapes = [(scen, SLOT, cols)] + [(SLOT, cols)] * 4
    odd_strip = call(
        edge_kernel,
        wide,
        [pltpu.VMEM(shape, x.dtype) for shape, x in zip(shapes, sources)] + [vmem(SLOT * scen, cols), sems],
        10**5,
        *pinned,
        space=pltpu.HBM,
    )
    x_b = swap_odd(odd_strip, "gx", "grp")
    lf, h, via, even_strip = call(
        pack_kernel,
        (field, grid, grid, wide),
        [pltpu.VMEM(x.shape, x.dtype) for x in sources] + [sems],
        10**5,
        *pinned,
        space=pltpu.HBM,
    )
    x_a = swap(even_strip, "gx", 1)

    fl, acc, edge, low, strip, res = call(
        functools.partial(core_kernel, scen),
        (field, f32(4 * scen, cols), f32(10 * scen, cols), f32(8, cols), f32(parts * PICKED, cols), f32(16, cols)),
        [vmem(rows, cols), vmem(4, rows, cols), vmem(size + cols * (-(-rows // cols)), cols)],
        10**7,
        lf, h, via, col_conductance, pad_mask, col_residual, pick,
    )
    x_a, x_b, acc = lax.optimization_barrier((x_a, x_b, acc))

    plain_shape, full_shape = f32(parts * USED + 0, cols), f32(parts * (USED + 8) + 0, cols)
    seam_shape = f32(parts * (USED + 8) + 8, cols)
    pair, plain, seam, fl_last = call(
        functools.partial(join_kernel, scen),
        (full_shape, plain_shape, seam_shape, f32(scen, cols)),
        [vmem(cols, cols)],
        10**6,
        lf, h, via, acc, edge, low, strip, res, x_a, x_b, pick,
    )

    ext = rows + 2 * SLOT
    reach = (rows + 2 * (STEPS - 1)) * scen
    v, t, gv, gt, br = call(
        functools.partial(row_kernel, scen),
        (field, field, field, field, grid),
        [vmem(ext, cols)] * 3 + [vmem(reach, cols)] * 2 + [vmem(rows + 16, cols)],
        10**7,
        lf, h, via, row_residual, x_a, x_b,
    )

    own_pair, own_seam, masks, received = pair, seam, [], []
    step, count = 1, lax.axis_size("gy")
    while step < count:
        radix = 4 if 4 * step <= count else 2
        got = []
        for k in range(1, radix):
            mask = k * step + step - 1
            whole = k % 2 == 1
            got.append(swap((pair if mask == 1 else seam) if whole else plain, "gy", mask))
            if whole:
                masks.append(mask)
                received.append(got[-1])
        if step * radix == count:
            *got, br = lax.optimization_barrier((*got, br))
        merge = functools.partial(merge_kernel, scen, parts, "gy", step, radix)
        if step * radix < count:
            plain, seam = call(merge, (plain_shape, seam_shape), [], 10**5, plain, *got, seam)
        else:
            sums = call(merge, f32(1, cols), [], 10**5, plain, *got)
        step *= radix

    gl, bc = call(
        functools.partial(col_kernel, scen, masks),
        (field, grid),
        [vmem(size, cols)],
        10**7,
        fl, fl_last, col_residual, own_pair, own_seam, *received, source, start,
    )

    step, others = 1, []
    while step < lax.axis_size("gx"):
        radix = 4 if 4 * step <= lax.axis_size("gx") else 2
        sums = sum(others, sums)
        others = [swap(sums, "gx", step * k) for k in range(1, radix)]
        if step == 1:
            *others, bc = lax.optimization_barrier((*others, bc))
        step *= radix

    shape = f32(scen, rows, cols)
    return call(
        functools.partial(final_kernel, scen, rows),
        (shape, shape, shape),
        [],
        10**6,
        v, t, gv, gt, gl, br, bc, sums, *others,
    )


def solution(mesh):
    field = P(None, ("grp", "gx"), "gy")
    grid = P(("grp", "gx"), "gy")
    return jax.shard_map(
        on_device,
        mesh=mesh,
        in_specs=(field,) + (grid,) * 7,
        out_specs=(field,) * 3,
        check_vma=False,
    )
```

```python
import functools

import jax
import jax.numpy as jnp
import numpy as np
from jax import lax
from jax.experimental import pallas as pl
from jax.experimental.pallas import tpu as pltpu
from jax.sharding import PartitionSpec as P

STEPS = 8
RELAX = 0.45
DRIVE = 4.0
PAD = 20.0
LEAK = 0.05

F32 = jnp.float32
HALO = STEPS + 1
SLOT = 16

SUM_LANES = [-1, 0, 13, 10, 12]
FIRST_LANES = [11, 1, 2, 3, 4, 5, 6]
LAST_LANES = [8, -7, -6, -5, -4, -3, 9, 15]
PICKED = 8 + 8 + 8
USED = 8


def dot_nt(a, b):
    return lax.dot_general(
        a, b, (((1,), (1,)), ((), ())), precision=lax.Precision.HIGHEST, preferred_element_type=F32
    )


def pick_nt(pick, b):
    out = None
    for _ in range(3):
        part = b.astype(jnp.bfloat16)
        b = b - part.astype(F32)
        term = lax.dot_general(
            pick.astype(jnp.bfloat16), part, (((1,), (1,)), ((), ())), preferred_element_type=F32
        )
        out = term if out is None else out + term
    return out


def dot_nn(a, b):
    return lax.dot_general(
        a, b, (((1,), (0,)), ((), ())), precision=lax.Precision.HIGHEST, preferred_element_type=F32
    )


def dot_tn(a, b):
    return lax.dot_general(
        a, b, (((0,), (0,)), ((), ())), precision=lax.Precision.HIGHEST, preferred_element_type=F32
    )


def picker(cols):
    e = np.zeros((PICKED + 8 + 16, cols), np.float32)
    for base, lanes in ((0, SUM_LANES), (8, FIRST_LANES), (16, LAST_LANES)):
        for i, lane in enumerate(lanes):
            e[base + i, lane % cols] = 1
    e[PICKED : PICKED + 8] = 1
    for i in range(8):
        e[PICKED + 8 + i, i] = 1
        e[PICKED + 16 + i, cols - 8 + i] = 1
    return e


def spread(cols):
    size = cols + 16
    sources, starts = [], []
    for first, last in ((0, 0), (1, 0), (0, 1), (1, 1)):
        rate = np.full(size + 1, RELAX)
        rate[0] = rate[size] = 0
        if first:
            rate[8] = 0
        if last:
            rate[8 + cols] = 0
        step = np.eye(size)
        for i in range(size):
            step[i, i] -= rate[i] + rate[i + 1]
            if i:
                step[i, i - 1] += rate[i]
            if i + 1 < size:
                step[i, i + 1] += rate[i + 1]
        power, total = np.eye(size), np.zeros((size, size))
        for _ in range(STEPS):
            total += power
            power = step @ power
        source = (RELAX * DRIVE * total)[8 : 8 + cols].T
        start = power[8 : 8 + cols].T
        extra = np.zeros((24, cols))
        extra[0:7] = source[1:8]
        extra[8:15] = source[8 + cols : 15 + cols]
        extra[16] = source[8]
        extra[17] = source[8 + cols - 2]
        extra[18] = source[8 + cols - 1]
        sources.append(np.concatenate([source[8 : 8 + cols], extra]))
        starts.append(np.concatenate([start[8 : 8 + cols], start[:8], start[8 + cols :]]))
    return np.stack(sources).astype(np.float32), np.stack(starts).astype(np.float32)


def taps():
    size = 4 * STEPS + 1
    step = np.eye(size) * (1 - 2 * RELAX) + RELAX * (np.eye(size, k=1) + np.eye(size, k=-1))
    total = sum(np.linalg.matrix_power(step, k) for k in range(STEPS))
    return [float(x) for x in RELAX * DRIVE * total[size // 2, size // 2 : size // 2 + STEPS]]


def place(axis):
    at, count = lax.axis_index(axis), lax.axis_size(axis)
    return at, at == 0, at == count - 1


def sides(axis, even_ref, odd_ref):
    at, first, last = place(axis)
    odd = lax.rem(at, 2) == 1

    def before(*where):
        return jnp.where(odd, even_ref[where], jnp.where(first, 0.0, odd_ref[where]))

    def after(*where):
        return jnp.where(odd, jnp.where(last, 0.0, odd_ref[where]), even_ref[where])

    return before, after


def fetch(args, held, sem):
    copies = [pltpu.make_async_copy(src, dst, sem.at[i]) for i, (src, dst) in enumerate(zip(args, held))]
    for copy in copies:
        copy.start()
    for copy in copies:
        copy.wait()


def edge_kernel(load_ref, rc_ref, vc_ref, vm_ref, rr_ref, out_ref, *scratch):
    *held, lf_s, sem = scratch
    scen, rows, cols = load_ref.shape
    odd = lax.rem(lax.axis_index("gx"), 2) == 1
    part = pl.ds(pl.multiple_of(jnp.where(odd, rows - SLOT, 0), SLOT), SLOT)
    fetch([load_ref.at[:, part], *(ref.at[part] for ref in (rc_ref, vc_ref, vm_ref, rr_ref))], held, sem)
    load_v, rc_v, vc_v, vm_v, rr_v = held
    for s in range(scen):
        lf_s[pl.ds(s, SLOT, stride=scen), :] = load_v[s].astype(F32)
    n = HALO * scen
    out_ref[0:n, :] = jnp.where(odd, lf_s[(SLOT - HALO) * scen :, :], lf_s[0:n, :])
    out_ref[n : n + SLOT, :] = rc_v[...]
    out_ref[n + SLOT : n + 2 * SLOT, :] = vm_v[...].astype(F32) * vc_v[...]
    out_ref[n + 2 * SLOT :, :] = jnp.where(odd, rr_v[SLOT - 8 :, :], rr_v[:8, :])


def pack_kernel(load_ref, rc_ref, vc_ref, vm_ref, rr_ref, lf_ref, h_ref, via_ref, out_ref, *scratch):
    *held, sem = scratch
    fetch([load_ref, rc_ref, vc_ref, vm_ref, rr_ref], held, sem)
    load_v, rc_v, vc_v, vm_v, rr_v = held
    scen, rows, cols = load_ref.shape
    at, first, _ = place("gx")
    even = lax.rem(at, 2) == 0
    for s in range(scen):
        lf_ref[pl.ds(s, rows, stride=scen), :] = load_v[s].astype(F32)
    row = lax.broadcasted_iota(jnp.int32, (rows, cols), 0)
    h = jnp.where(jnp.logical_and(first, row == 0), 0.0, rc_v[...])
    via = vm_v[...].astype(F32) * vc_v[...]
    h_ref[...] = h
    via_ref[...] = via
    n = HALO * scen
    out_ref[0:n, :] = jnp.where(even, lf_ref[rows * scen - n :, :], lf_ref[0:n, :])
    out_ref[n : n + SLOT, :] = jnp.where(even, h[rows - SLOT :], h[:SLOT])
    out_ref[n + SLOT : n + 2 * SLOT, :] = jnp.where(even, via[rows - SLOT :], via[:SLOT])
    out_ref[n + 2 * SLOT :, :] = jnp.where(even, rr_v[rows - 8 :, :], rr_v[:8, :])


def packer(scen, cols):
    lane = lax.broadcasted_iota(jnp.int32, (scen, cols), 1)
    is_flux = jnp.logical_or(
        jnp.logical_and(lane >= 1, lane <= 6), jnp.logical_and(lane >= cols - 7, lane <= cols - 3)
    )
    is_end = lane == cols - 1
    is_rolled = jnp.logical_and(lane >= 8, lane <= 11)

    def pack(q, jl, fl, p, grid_row):
        ends = jl if p is None else jl + p
        return jnp.where(
            is_flux,
            fl,
            jnp.where(
                is_end,
                q,
                jnp.where(lane == 0, pltpu.roll(ends, 1, 1), jnp.where(is_rolled, pltpu.roll(jl, 10, 1), grid_row)),
            ),
        )

    def add_p(w, p):
        return w + jnp.where(lane == 0, pltpu.roll(p, 1, 1), 0.0)

    return pack, add_p


def lower_row(v, via, minus_inv, vs, open_end):
    scen, cols = v.shape
    lane = lax.broadcasted_iota(jnp.int32, (scen, cols), 1)
    q = via * v
    tl = q * minus_inv
    dl = jnp.where(lane == 0, 0.0, pltpu.roll(tl, 1, 1)) - tl
    jl = vs * dl
    inner = jnp.where(jnp.logical_or(lane == 0, jnp.logical_and(open_end, lane == cols - 1)), 0.0, jl)
    return q, tl, dl, jl, inner - pltpu.roll(inner, cols - 1, 1)


def core_kernel(
    scen, lf_ref, h_ref, via_ref, cc_ref, pm_ref, cr_ref, pick_ref,
    fl_ref, acc_ref, edge_ref, low_ref, strip_ref, res_ref,
    inv_s, low_s, w_s,
):
    rows, cols = h_ref.shape
    _, first_y, last_y = place("gy")
    lane = lax.broadcasted_iota(jnp.int32, (rows, cols), 1)
    h, via = h_ref[...], via_ref[...]
    inv_s[...] = 1.0 / (h + pltpu.roll(h, rows - 1, 0) + via + LEAK)

    tie_low = via + pm_ref[...].astype(F32) * PAD + LEAK
    vs = jnp.where(jnp.logical_and(first_y, lane == 0), 0.0, cc_ref[...])
    open_end = jnp.logical_and(jnp.logical_not(last_y), lane == cols - 1)
    vs_next = jnp.where(lane == cols - 1, 0.0, pltpu.roll(vs, cols - 1, 1))
    diag_low = vs + vs_next + tie_low
    low_s[0] = jnp.where(open_end, 0.0, -1.0 / diag_low)
    low_s[1] = tie_low
    low_s[2] = vs
    low_s[3] = jnp.where(
        lane == 12,
        pltpu.roll(vs, 12, 1),
        jnp.where(
            lane == 13,
            pltpu.roll(diag_low, 14, 1),
            pltpu.roll(vs, 16, 1),
        ),
    )
    low_ref[...] = jnp.concatenate([low_s[k, rows - 1 : rows, :] for k in range(4)] * 2, 0)
    pack, _ = packer(scen, cols)

    def bc(ref, r):
        return jnp.broadcast_to(ref[pl.ds(r, 1), :], (scen, cols))

    def low(k, r):
        return jnp.broadcast_to(low_s[k, pl.ds(r, 1), :], (scen, cols))

    def keep(i, x):
        edge_ref[pl.ds(i * scen, scen), :] = x

    zero = jnp.zeros((scen, cols), F32)
    g0 = g1 = g2 = g3 = zero
    v0 = hv0 = t0 = None
    last = rows - 1
    for r in range(rows):
        v1 = hv1 = dv1 = None
        if r < last:
            load = lf_ref[pl.ds(r * scen, scen), :]
            v1 = load * bc(inv_s, r)
            g0 += load * v1
            g1 += (bc(via_ref, r) + LEAK) * v1 * v1
            if r > 0:
                dv1 = v0 - v1
                hv1 = bc(h_ref, r) * dv1
                g1 += hv1 * dv1
        if r > 0:
            m = r - 1
            via_m = bc(via_ref, m)
            tie = via_m + LEAK
            q, tl, dl, jl, fl = lower_row(v0, via_m, low(0, m), low(2, m), jnp.logical_not(last_y))
            fl_ref[pl.ds(m * scen, scen), :] = fl
            g2 -= q * tl
            g3 += low(1, m) * tl * tl + jl * dl
            p = t1 = None
            if 0 < m < last - 1:
                q_up = tie * v0 - hv0 + hv1
                t1 = q_up * bc(inv_s, m)
                p = via_m * t1
                g2 += q_up * t1
                g3 += tie * t1 * t1 - 2.0 * p * tl
                if m > 1:
                    dt = t0 - t1
                    g3 += bc(h_ref, m) * dt * dt
            w = pack(q, jl, fl, p, low(3, m))
            w_s[pl.ds(m * scen, scen), :] = w
            if m == 0:
                keep(0, v0)
                keep(1, hv1)
                keep(3, tl)
                keep(8, w)
            if m == 1:
                keep(2, t1)
            if m == last - 2:
                keep(6, t1)
            if m == last - 1:
                keep(4, v0)
                keep(5, hv0)
                keep(7, tl)
                keep(9, w)
            t0 = t1
        v0, hv0 = v1, hv1

    size = rows * scen
    fl_ref[pl.ds(last * scen, scen), :] = zero
    w_s[pl.ds(last * scen, scen), :] = zero
    w_s[pl.ds(size, rows), :] = cr_ref[...]
    w_s[size + rows :, :] = jnp.zeros((w_s.shape[0] - size - rows, cols), F32)
    for k, g in enumerate((g0, g1, g2, g3)):
        acc_ref[pl.ds(k * scen, scen), :] = g
    picked = pick_nt(pick_ref[...], w_s[...])
    for k in range(size // cols):
        strip_ref[pl.ds(k * PICKED, PICKED), :] = picked[:PICKED, k * cols : (k + 1) * cols]
    res = picked[PICKED + 8 :, size : size + cols]
    per = cols // rows
    group = lax.div(lax.broadcasted_iota(jnp.int32, (1, cols), 1), rows)
    packed = []
    for start in range(0, 16, per):
        line = res[start : start + 1]
        for k in range(1, per):
            line = jnp.where(group == k, pltpu.roll(res[start + k : start + k + 1], k * rows, 1), line)
        packed.append(line)
    res_ref[...] = jnp.concatenate(packed + [jnp.zeros((16 - len(packed), cols), F32)], 0)


def join_kernel(
    scen, lf_ref, h_ref, via_ref, acc_ref, edge_ref, low_ref, strip_ref, res_ref, a_ref, b_ref, pick_ref,
    pair_ref, plain_ref, seam_ref, fl_ref,
    w_s,
):
    rows, cols = h_ref.shape
    at_y, _, last_y = place("gy")
    even_y = lax.rem(at_y, 2) == 0
    before, after = sides("gx", a_ref, b_ref)
    n = HALO * scen
    last = rows - 1

    def grid(h, via):
        tie = via + LEAK
        inv = 1.0 / (h + pltpu.roll(h, 15, 0) + tie)

        def row(x, i):
            return jnp.broadcast_to(x[i : i + 1], (scen, cols))

        return (lambda i: row(h, i)), (lambda i: row(tie, i)), (lambda i: row(inv, i)), (lambda i: row(via, i))

    def edge(i):
        return edge_ref[pl.ds(i * scen, scen), :]

    pack, add_p = packer(scen, cols)

    h, tie, inv, via = grid(
        jnp.concatenate([before(pl.ds(n + SLOT - 8, 8)), h_ref[:8, :]], 0),
        jnp.concatenate([before(pl.ds(n + 2 * SLOT - 8, 8)), via_ref[:8, :]], 0),
    )
    v0, hv1, t1, tl0 = (edge(i) for i in range(4))
    far, near = before(pl.ds(n - 2 * scen, scen)) * inv(6), before(pl.ds(n - scen, scen)) * inv(7)
    dv0 = near - v0
    hv0 = h(8) * dv0
    t_near = (tie(7) * near - h(7) * (far - near) + hv0) * inv(7)
    q_up = tie(8) * v0 - hv0 + hv1
    t0 = q_up * inv(8)
    d0, d1 = t_near - t0, t0 - t1
    p = via(8) * t0
    g1 = hv0 * dv0
    g2 = q_up * t0
    g3 = tie(8) * t0 * t0 + h(8) * d0 * d0 + h(9) * d1 * d1 - 2.0 * p * tl0
    w_first = add_p(edge(8), p)

    h, tie, inv, via = grid(
        jnp.concatenate([h_ref[rows - 8 :, :], after(pl.ds(n, 8))], 0),
        jnp.concatenate([via_ref[rows - 8 :, :], after(pl.ds(n + SLOT, 8))], 0),
    )
    v0, hv0, t0, tl0 = (edge(i) for i in range(4, 8))
    load = lf_ref[pl.ds(last * scen, scen), :]
    v1 = load * inv(7)
    v2 = after(pl.ds(0, scen)) * inv(8)
    dv1 = v0 - v1
    hv1, hv2 = h(7) * dv1, h(8) * (v1 - v2)
    q0 = tie(6) * v0 - hv0 + hv1
    q1 = tie(7) * v1 - hv1 + hv2
    t1 = q0 * inv(6)
    t2 = q1 * inv(7)
    d1, d2 = t0 - t1, t1 - t2
    p0, p1 = via(6) * t1, via(7) * t2
    g0 = load * v1
    g1 += hv1 * dv1 + tie(7) * v1 * v1
    g2 += q0 * t1 + q1 * t2
    g3 += tie(6) * t1 * t1 + tie(7) * t2 * t2 + h(6) * d1 * d1 + h(7) * d2 * d2 - 2.0 * p0 * tl0

    def low(k):
        return jnp.broadcast_to(low_ref[pl.ds(k, 1), :], (scen, cols))

    q, tl, dl, jl, fl = lower_row(v1, via(7), low(0), low(2), jnp.logical_not(last_y))
    fl_ref[...] = fl
    g2 -= q * tl
    g3 += tl * (low(1) * tl - 2.0 * p1) + jl * dl

    w_s[5 * scen : cols - 2 * scen, :] = jnp.zeros((cols - 7 * scen, cols), F32)
    w_s[0:scen, :] = w_first
    for k, g in enumerate((g0, g1, g2, g3)):
        w_s[pl.ds((k + 1) * scen, scen), :] = acc_ref[pl.ds(k * scen, scen), :] + g
    w_s[cols - 2 * scen : cols - scen, :] = add_p(edge(9), p0)
    w_s[cols - scen :, :] = pack(q, jl, fl, p1, low(3))
    fresh = pick_nt(pick_ref[: PICKED + 8, :], w_s[...])

    lane = lax.broadcasted_iota(jnp.int32, (PICKED, cols), 1)
    parts = rows * scen // cols
    base = parts * USED
    half = 8 * rows // cols
    row = lax.broadcasted_iota(jnp.int32, (8, cols), 0)
    groups, pair_groups, seam_groups = [], [], []
    for k in range(parts):
        strip = strip_ref[pl.ds(k * PICKED, PICKED), :]
        if k == 0:
            strip = jnp.where(lane < scen, fresh[:PICKED], strip)
        if k == parts - 1:
            strip = jnp.where(lane >= cols - 2 * scen, fresh[:PICKED], strip)
        group = strip[:8]
        if k == 0:
            group = jnp.where(row == USED - 1, fresh[PICKED:], group)
        of_pair = of_seam = group
        if 1 <= k <= half:
            firsts, lasts = res_ref[k - 1 : k, :], res_ref[half + k - 1 : half + k, :]
            of_pair = jnp.where(row == USED - 1, jnp.where(even_y, lasts, firsts), group)
            of_seam = jnp.where(row == USED - 1, jnp.where(even_y, firsts, lasts), group)
        groups.append(group)
        pair_groups.append(of_pair)
        seam_groups.append(of_seam)
        firsts, lasts = strip[8:16], strip[16:24]
        pair_ref[pl.ds(base + k * 8, 8), :] = jnp.where(even_y, lasts, firsts)
        seam_ref[pl.ds(base + k * 8, 8), :] = jnp.where(even_y, firsts, lasts)
    pack_rows(pair_ref, pair_groups)
    pack_rows(plain_ref, groups)
    pack_rows(seam_ref, seam_groups)


def pack_rows(ref, groups):
    ref[0 : len(groups) * USED, :] = jnp.concatenate([g[:USED] for g in groups], 0)


def unpack_rows(ref, parts):
    return jnp.concatenate([ref[k * USED : (k + 1) * USED, :] for k in range(parts)], 1)


def across(ref, start, parts):
    return jnp.concatenate([ref[pl.ds(start + 8 * k, 8), :] for k in range(parts)], 1)


def merge_kernel(scen, parts, axis, step, radix, *refs):
    in_refs, held_refs, out_refs = refs[:radix], refs[radix:-2], refs[-2:]
    if not held_refs:
        in_refs, out_refs = refs[:radix], refs[radix:]
    cols = in_refs[0].shape[1]
    at = lax.rem(lax.div(lax.axis_index(axis), step), radix)
    given = [unpack_rows(ref, parts) for ref in in_refs]
    blocks = []
    for j in range(radix):
        block = given[0]
        for k in range(1, radix):
            block = jnp.where(jnp.bitwise_xor(at, k) == j, given[k], block)
        blocks.append(block)
    i2 = i3 = 0.0
    for left, right in zip(blocks, blocks[1:]):
        q, e, d = (left[i : i + 1] for i in range(3))
        jl_next, vs_next = right[3:4], right[4:5]
        r = q / (d + vs_next)
        i2 = i2 + q * r
        i3 = i3 + r * (e - jl_next)
    i3 = i2 + 2.0 * i3
    both = jnp.concatenate([i2, i3], 0)
    both = sum(both[:, k * cols : (k + 1) * cols] for k in range(parts))
    shift = scen
    while shift < cols:
        both = both + pltpu.roll(both, shift, 1)
        shift *= 2
    group = lax.div(lax.broadcasted_iota(jnp.int32, (1, cols), 1), scen)
    sums = jnp.where(group == 3, both[0:1], jnp.where(group == 4, both[1:2], 0.0))
    sums = sum((block[USED - 1 : USED, :cols] for block in given), sums)
    if not held_refs:
        out_refs[0][...] = sums
        return
    row = lax.broadcasted_iota(jnp.int32, (USED, cols), 0)
    held = unpack_rows(held_refs[0], parts)
    groups = []
    for k in range(parts):
        where = slice(k * cols, (k + 1) * cols)
        group = jnp.where(row < 3, blocks[-1][:, where], blocks[0][:, where])
        groups.append(jnp.where(row == USED - 1, sums if k == 0 else held[:, where], group))
    pack_rows(out_refs[0], groups)
    pack_rows(out_refs[1], groups)
    out_refs[1][parts * USED :, :] = held_refs[0][parts * USED :, :]


def row_kernel(
    scen, lf_ref, h_ref, via_ref, rr_ref, a_ref, b_ref,
    v_ref, t_ref, gv_ref, gt_ref, br_ref,
    inv_s, h_s, tie_s, fv_s, ft_s, s0_s,
):
    rows, cols = h_ref.shape
    _, first, last = place("gx")
    before, after = sides("gx", a_ref, b_ref)
    n = HALO * scen
    at = pl.ds(n, SLOT)
    h = jnp.concatenate([before(at), h_ref[...], after(at)], 0)
    at = pl.ds(n + SLOT, SLOT)
    tie = jnp.concatenate([before(at), via_ref[...], after(at)], 0) + LEAK
    h_s[...] = h
    tie_s[...] = tie
    inv_s[...] = 1.0 / (h + pltpu.roll(h, h.shape[0] - 1, 0) + tie)

    def load(r):
        if r < 0:
            return before(pl.ds((r + HALO) * scen, scen))
        if r >= rows:
            return after(pl.ds((r - rows) * scen, scen))
        return lf_ref[pl.ds(r * scen, scen), :]

    def bc(ref, r):
        return jnp.broadcast_to(ref[pl.ds(r + SLOT, 1), :], (scen, cols))

    v0 = hv0 = t0 = ht0 = None
    for r in range(-HALO, rows + HALO):
        v1 = load(r) * bc(inv_s, r)
        hv1 = None
        if r > -HALO:
            hv1 = bc(h_s, r) * (v0 - v1)
        if r > 1 - HALO:
            m = r - 1
            fv = hv0 - hv1
            t1 = (bc(tie_s, m) * v0 - fv) * bc(inv_s, m)
            ht1 = None
            if m > 1 - HALO:
                ht1 = bc(h_s, m) * (t0 - t1)
                if m > 2 - HALO:
                    ft_s[pl.ds((m - 1 + STEPS - 1) * scen, scen), :] = ht0 - ht1
                if m < rows + STEPS - 1:
                    fv_s[pl.ds((m + STEPS - 1) * scen, scen), :] = fv
            if 0 <= m < rows:
                v_ref[pl.ds(m, scen, stride=rows), :] = v0
                t_ref[pl.ds(m, scen, stride=rows), :] = t1
            t0, ht0 = t1, ht1
        v0, hv0 = v1, hv1

    n += 2 * SLOT
    size = rows + 16
    row = lax.broadcasted_iota(jnp.int32, (size, cols), 0)
    closed = jnp.logical_or(jnp.logical_and(first, row == 8), jnp.logical_and(last, row == 8 + rows))
    rates = jnp.where(closed, 0.0, RELAX)
    s0_s[...] = jnp.concatenate([before(pl.ds(n, 8)), rr_ref[...], after(pl.ds(n, 8))], 0)

    def one(_, carry):
        now = s0_s[...]
        flux = rates * (pltpu.roll(now, 1, 0) - now)
        s0_s[...] = now + flux - pltpu.roll(flux, size - 1, 0)
        return carry

    lax.fori_loop(0, STEPS, one, 0)
    br_ref[...] = s0_s[8 : 8 + rows, :]

    weights = taps()
    reach = STEPS - 1
    for f_ref, out_ref in ((fv_s, gv_ref), (ft_s, gt_ref)):

        def at(r):
            return f_ref[pl.ds((r + reach) * scen, scen), :]

        window = {}
        for r in range(-reach, rows + reach):
            if r < 0:
                x = jnp.where(first, at(-1 - r), at(r))
            elif r >= rows:
                x = jnp.where(last, at(2 * rows - 1 - r), at(r))
            else:
                x = at(r)
            window[r] = x
            m = r - reach
            if m >= 0:
                total = weights[0] * window[m]
                for d in range(1, STEPS):
                    total = total + weights[d] * (window[m - d] + window[m + d])
                out_ref[pl.ds(m, scen, stride=rows), :] = total
                del window[m - reach]


def col_kernel(scen, steps, fl_ref, fl_last_ref, cr_ref, pair_ref, seam_ref, *rest):
    *got_refs, source_ref, start_ref, gl_ref, bc_ref, out_s = rest
    rows, cols = cr_ref.shape
    parts = rows * scen // cols
    base = parts * USED
    at, first, last = place("gy")
    kind = first.astype(jnp.int32) + 2 * last.astype(jnp.int32)
    odd = lax.rem(at, 2) == 1

    def contents(ref):
        return unpack_rows(ref, parts), across(ref, base, parts)

    paired = contents(got_refs[0])
    met = tuple(jnp.zeros_like(x) for x in paired)
    for mask, ref in zip(steps[1:], got_refs[1:]):
        here = jnp.abs(jnp.bitwise_xor(at, mask) - at) == 1
        met = tuple(jnp.where(here, x, y) for x, y in zip(contents(ref), met))
    sums_before, before = (jnp.where(odd, x, y) for x, y in zip(paired, met))
    sums_after, after = (jnp.where(odd, y, x) for x, y in zip(paired, met))
    own, own_pair = contents(pair_ref)
    own_last = jnp.where(odd, across(seam_ref, base, parts), own_pair)

    def seam(left, lasts, right):
        q, d = left[0:1], left[2:3]
        u, vs = lasts[6:7], lasts[7:8]
        jl_next, vs_next = right[3:4], right[4:5]
        diag = d + vs_next
        t = -q / jnp.where(diag > 0, diag, 1.0)
        return u - vs * t, vs_next * t + jl_next

    jl_last, jl_0 = seam(sums_before, before, own)
    jr_last, jr_0 = seam(own, own_last, sums_after)
    jr_last = jnp.where(last, 0.0, jr_last)
    jr_0 = jnp.where(last, 0.0, jr_0)
    zero = jnp.zeros_like(jl_0)
    strip = jnp.concatenate(
        [
            before[1:6],
            before[0:1] - jl_last,
            jl_last - jl_0,
            zero,
            jr_0 - after[0:1],
            after[1:7],
            zero,
            jl_0,
            -jr_last,
            jr_last - jr_0,
            zero,
            zero,
            zero,
            zero,
            zero,
        ],
        0,
    )
    source = source_ref[kind]
    edge = dot_tn(strip, source[cols:])
    done = (rows - 1) * scen
    out_s[0:done, :] = dot_nn(fl_ref[0:done, :], source[:cols]) + edge[:done]
    out_s[done:, :] = dot_nn(fl_last_ref[...], source[:cols]) + edge[done:]
    for m in range(rows):
        gl_ref[pl.ds(m, scen, stride=rows), :] = out_s[pl.ds(m * scen, scen), :]
    start = start_ref[kind]
    per = cols // rows
    res = []
    for block in (sums_before, sums_after):
        for k in range(8):
            lanes = block[USED - 1 : USED, (1 + k // per) * cols : (2 + k // per) * cols]
            res.append(lanes if k % per == 0 else pltpu.roll(lanes, cols - k % per * rows, 1))
    edge = dot_tn(jnp.concatenate(res, 0), start[cols:])
    bc_ref[...] = dot_nn(cr_ref[...], start[:cols]) + edge[:rows]


def final_kernel(scen, rows, v_ref, t_ref, gv_ref, gt_ref, gl_ref, br_ref, bc_ref, *rest):
    *sum_refs, up_ref, row_ref, col_ref = rest
    cols = v_ref.shape[1]
    sums = sum(ref[...] for ref in sum_refs)
    g0, g1, g2, g3 = (pltpu.roll(sums, cols - (k + 1) * scen, 1) for k in range(4))
    alpha, ratio = g0 / g1, g2 / g1
    c1 = (g1 - alpha * g2) / (g3 - ratio * g2)
    c0 = alpha - ratio * c1
    lane = lax.broadcasted_iota(jnp.int32, (scen, cols), 1)
    sub = lax.broadcasted_iota(jnp.int32, (scen, cols), 0)

    def column(c):
        picked = jnp.where(lane == sub, jnp.broadcast_to(c, lane.shape), 0.0)
        return jnp.broadcast_to(jnp.sum(picked, 1, keepdims=True), lane.shape)

    c0, c1 = column(c0), column(c1)
    br, bc = br_ref[...], bc_ref[...]
    for s in range(scen):
        at = pl.ds(s * rows, rows)
        a = jnp.broadcast_to(c0[s : s + 1], (rows, cols))
        b = jnp.broadcast_to(c1[s : s + 1], (rows, cols))
        up_ref[s] = a * v_ref[at, :] + b * t_ref[at, :]
        row_ref[s] = br + a * gv_ref[at, :] + b * gt_ref[at, :]
        col_ref[s] = bc + b * gl_ref[at, :]


def swap(block, axis, mask):
    count = lax.axis_size(axis)
    return lax.ppermute(block, axis, [(i, i ^ mask) for i in range(count)])


def swap_odd(block, axis, idle):
    count, lines = lax.axis_size(axis), lax.axis_size(idle)
    pairs = []
    for line in range(lines):
        for i in range(count):
            if 0 < i < count - 1:
                partner = line * count + (i + 1 if i % 2 else i - 1)
            elif lines % 2 == 0:
                partner = (line ^ 1) * count + i
            else:
                partner = line * count + count - 1 - i
            pairs.append((line * count + i, partner))
    return lax.ppermute(block, (idle, axis), pairs)


def call(kernel, out, scratch, cost, *args, space=pltpu.VMEM):
    return pl.pallas_call(
        kernel,
        out_shape=out,
        in_specs=[pl.BlockSpec(memory_space=space)] * len(args),
        out_specs=jax.tree.map(lambda _: pl.BlockSpec(memory_space=pltpu.VMEM), out),
        scratch_shapes=scratch,
        compiler_params=pltpu.CompilerParams(vmem_limit_bytes=24 * 2**20),
        cost_estimate=pl.CostEstimate(flops=cost, bytes_accessed=0, transcendentals=0),
    )(*args)


def on_device(
    load_current, row_conductance, col_conductance, via_conductance, pad_mask, via_mask, row_residual, col_residual
):
    scen, rows, cols = load_current.shape
    size = rows * scen
    parts = size // cols

    def f32(*shape):
        return jax.ShapeDtypeStruct(shape, F32)

    def vmem(*shape):
        return pltpu.VMEM(shape, F32)

    pick = jnp.asarray(picker(cols))
    source, start = (jnp.asarray(m) for m in spread(cols))
    grid, field = f32(rows, cols), f32(size, cols)

    wide = f32(HALO * scen + 2 * SLOT + 8, cols)
    sources = (load_current, row_conductance, via_conductance, via_mask, row_residual)
    pinned = [pltpu.with_memory_space_constraint(x, pltpu.HBM) for x in sources]
    sems = pltpu.SemaphoreType.DMA((len(sources),))
    shapes = [(scen, SLOT, cols)] + [(SLOT, cols)] * 4
    odd_strip = call(
        edge_kernel,
        wide,
        [pltpu.VMEM(shape, x.dtype) for shape, x in zip(shapes, sources)] + [vmem(SLOT * scen, cols), sems],
        10**5,
        *pinned,
        space=pltpu.HBM,
    )
    x_b = swap_odd(odd_strip, "gx", "grp")
    lf, h, via, even_strip = call(
        pack_kernel,
        (field, grid, grid, wide),
        [pltpu.VMEM(x.shape, x.dtype) for x in sources] + [sems],
        10**5,
        *pinned,
        space=pltpu.HBM,
    )
    x_a = swap(even_strip, "gx", 1)

    fl, acc, edge, low, strip, res = call(
        functools.partial(core_kernel, scen),
        (field, f32(4 * scen, cols), f32(10 * scen, cols), f32(8, cols), f32(parts * PICKED, cols), f32(16, cols)),
        [vmem(rows, cols), vmem(4, rows, cols), vmem(size + cols * (-(-rows // cols)), cols)],
        10**7,
        lf, h, via, col_conductance, pad_mask, col_residual, pick,
    )
    x_a, x_b, acc = lax.optimization_barrier((x_a, x_b, acc))

    plain_shape, full_shape = f32(parts * USED + 0, cols), f32(parts * (USED + 8) + 0, cols)
    seam_shape = f32(parts * (USED + 8) + 8, cols)
    pair, plain, seam, fl_last = call(
        functools.partial(join_kernel, scen),
        (full_shape, plain_shape, seam_shape, f32(scen, cols)),
        [vmem(cols, cols)],
        10**6,
        lf, h, via, acc, edge, low, strip, res, x_a, x_b, pick,
    )

    ext = rows + 2 * SLOT
    reach = (rows + 2 * (STEPS - 1)) * scen
    v, t, gv, gt, br = call(
        functools.partial(row_kernel, scen),
        (field, field, field, field, grid),
        [vmem(ext, cols)] * 3 + [vmem(reach, cols)] * 2 + [vmem(rows + 16, cols)],
        10**7,
        lf, h, via, row_residual, x_a, x_b,
    )

    own_pair, own_seam, masks, received = pair, seam, [], []
    step, count = 1, lax.axis_size("gy")
    while step < count:
        radix = 4 if 4 * step <= count else 2
        got = []
        for k in range(1, radix):
            mask = k * step + step - 1
            whole = k % 2 == 1
            got.append(swap((pair if mask == 1 else seam) if whole else plain, "gy", mask))
            if whole:
                masks.append(mask)
                received.append(got[-1])
        if step * radix == count:
            *got, br = lax.optimization_barrier((*got, br))
        merge = functools.partial(merge_kernel, scen, parts, "gy", step, radix)
        if step * radix < count:
            plain, seam = call(merge, (plain_shape, seam_shape), [], 10**5, plain, *got, seam)
        else:
            sums = call(merge, f32(1, cols), [], 10**5, plain, *got)
        step *= radix

    gl, bc = call(
        functools.partial(col_kernel, scen, masks),
        (field, grid),
        [vmem(size, cols)],
        10**7,
        fl, fl_last, col_residual, own_pair, own_seam, *received, source, start,
    )

    step, others = 1, []
    while step < lax.axis_size("gx"):
        radix = 4 if 4 * step <= lax.axis_size("gx") else 2
        sums = sum(others, sums)
        others = [swap(sums, "gx", step * k) for k in range(1, radix)]
        if step == 1:
            *others, bc = lax.optimization_barrier((*others, bc))
        step *= radix

    shape = f32(scen, rows, cols)
    return call(
        functools.partial(final_kernel, scen, rows),
        (shape, shape, shape),
        [],
        10**6,
        v, t, gv, gt, gl, br, bc, sums, *others,
    )


def solution(mesh):
    field = P(None, ("grp", "gx"), "gy")
    grid = P(("grp", "gx"), "gy")
    return jax.shard_map(
        on_device,
        mesh=mesh,
        in_specs=(field,) + (grid,) * 7,
        out_specs=(field,) * 3,
        check_vma=False,
    )
```
